32 devices in a mesh: gx: 4 (over z), gy: 8 (over y, x, core).
Axes of the slice: x: 2, y: 2, z: 4, core: 2. Of those that a mesh axis runs over, the one named last changes fastest.
Arguments:
- board_activations_input: bfloat16 [128, 19, 19, 256], P(('gx', 'gy')), may hold values from -14 to 14
- conv1_weight: bfloat16 [9, 256, 256], P(None, ('gx', 'gy')), may hold values from -0.125 to 0.125
- conv2_weight: bfloat16 [9, 256, 256], P(None, ('gx', 'gy')), may hold values from -0.125 to 0.125
- norm_gains: bfloat16 [2, 256], P(None, ('gx', 'gy')), may hold values from 0.5 to 1.5
- norm_shifts: bfloat16 [2, 256], P(None, ('gx', 'gy')), may hold values from -1.5 to 1.5
- head_conv: bfloat16 [2, 256], P(None, ('gx', 'gy')), may hold values from -0.375 to 0.375
- head_norm_gain: float32 [2], replicated, may hold values from 0.5 to 1.5
- head_norm_shift: float32 [2], replicated, may hold values from -2 to 2
- dense_weight: bfloat16 [736, 362], P(('gx', 'gy')), may hold values from -0.4375 to 0.4375
- legal_moves: int32 [128, 362], P(('gx', 'gy')), may hold values from 0 to 1, as said below
- target_moves: int32 [128], P(('gx', 'gy')), may hold values from 0 to 361, as said below
- out_cotangent: bfloat16 [128, 19, 19, 256], P(('gx', 'gy')), may hold values from -0.35 to 0.35
Outputs:
- block_output: bfloat16 [128, 19, 19, 256], P(('gx', 'gy'))
- policy_loss: float32 [], replicated
- input_grad: bfloat16 [128, 19, 19, 256], P(('gx', 'gy'))
- conv1_grad: float32 [9, 256, 256], P(None, ('gx', 'gy'))
- conv2_grad: float32 [9, 256, 256], P(None, ('gx', 'gy'))
- gains_grad: float32 [2, 256], P(None, ('gx', 'gy'))
- shifts_grad: float32 [2, 256], P(None, ('gx', 'gy'))
- head_conv_grad: float32 [2, 256], P(None, ('gx', 'gy'))
- head_norm_grad: float32 [2, 2], replicated
- dense_grad: float32 [736, 362], P(('gx', 'gy'))
The draws below stay inside these ranges and needn't reach their ends.
Inputs may be any that keep to these rules, and one draw needn't show every extreme that they name: `legal_moves`: the pass, move 362 - 1, is legal in every position; the number of legal moves differs from position to position. `target_moves`: A legal move of its position.
All inputs are finite; a program needn't handle non-finite values.
Results may differ from the reference program's by a relative error of at most 0.011.
Values may be sent and summed in bfloat16 or wider, within the bound.
A program may use at most 64 MiB of HBM per device.

```python
import jax
import jax.numpy as jnp
from jax import lax

C = 256
SIDE = 19
HEAD_CH = 2
MOVES = 362
HEAD_IN = 722
HEAD_ROWS = 736
POSITIONS = 128


def draw_board_activations_input(key, part):
    key = jax.random.fold_in(key, 7)
    subkeys = jax.random.split(key, 4)
    dimensions = (POSITIONS, SIDE, SIDE, C)
    rising = jnp.arange(POSITIONS, dtype=jnp.float32) / max(POSITIONS - 1, 1)
    jitter = jax.random.uniform(subkeys[0], (POSITIONS,))
    scales = 0.25 * jnp.power(10.0, 0.5 * rising + 0.5 * jitter)
    spread = jnp.power(10.0, jax.random.uniform(subkeys[1], (C,), minval=-0.3, maxval=0.2))
    offsets = jax.random.uniform(subkeys[2], (C,), minval=-0.5, maxval=0.5)
    samples = jax.random.truncated_normal(subkeys[3], -2.5, 2.5, dimensions)
    values = scales[:, None, None, None] * spread * (samples + offsets)
    return values.astype(jnp.bfloat16)


def draw_out_cotangent(key, part):
    key = jax.random.fold_in(key, 13)
    subkeys = jax.random.split(key, 3)
    dimensions = (POSITIONS, SIDE, SIDE, C)
    rising = jnp.arange(POSITIONS, dtype=jnp.float32) / max(POSITIONS - 1, 1)
    jitter = jax.random.uniform(subkeys[0], (POSITIONS,))
    scales = 0.015 * jnp.power(3.0, rising) * (1.0 + jitter)
    samples = jax.random.truncated_normal(subkeys[1], -3.0, 3.0, dimensions)
    common = jax.random.uniform(subkeys[2], (C,), minval=-0.3, maxval=0.3)
    values = scales[:, None, None, None] * (samples + common)
    return values.astype(jnp.bfloat16)


def legal_and_target(key):
    subkeys = jax.random.split(key, 3)
    keep_share = jax.random.randint(subkeys[0], (POSITIONS, 1), 15, 100)
    rolled = jax.random.randint(subkeys[1], (POSITIONS, MOVES), 0, 100)
    column = jnp.arange(MOVES, dtype=jnp.int32)[None, :]
    legal = jnp.where(column == MOVES - 1, 1, (rolled < keep_share).astype(jnp.int32)).astype(jnp.int32)
    ranking = jax.random.randint(subkeys[2], (POSITIONS, MOVES), 0, 1 << 20) * MOVES + column
    ranking = jnp.where(legal == 1, ranking, -1)
    target = jnp.argmax(ranking, axis=1).astype(jnp.int32)
    return (legal, target)


def draw_legal_moves(key, part):
    return legal_and_target(key)[0]


def draw_target_moves(key, part):
    return legal_and_target(key)[1]


def shard_levels(stream_key, shape, cuts, low, high):
    level, own = 1.0, jax.random.fold_in(stream_key, 6)
    for position, shards_of in cuts:
        steps = jnp.exp(jax.random.uniform(jax.random.fold_in(own, position), (shards_of,), jnp.float32, low / len(cuts), high / len(cuts)))
        level = level * jnp.repeat(steps, shape[position] // shards_of).reshape([-1 if axis == position else 1 for axis in range(len(shape))])
    return level


def bell_draw(rng, extent, deviation, limit, pieces=(), kind=jnp.bfloat16):
    drawn = deviation * jax.random.normal(rng, extent, jnp.float32)
    if pieces:
        drawn = drawn * shard_levels(rng, extent, pieces, -0.22, 0.18)
    return jnp.clip(drawn, -limit, limit).astype(kind)


def setup_inputs(seed: int = 0) -> dict:
    streams_of = jax.random.split(jax.random.key(seed), 13)
    board_activations_input = draw_board_activations_input(jax.random.fold_in(streams_of[12], 71), 0)
    conv1_weight = bell_draw(streams_of[1], (9, C, C), (9 * C) ** -0.5, 0.125, ((1, 32),))
    conv2_weight = bell_draw(streams_of[2], (9, C, C), (9 * C) ** -0.5, 0.125, ((1, 32),))
    norm_gains = jnp.clip(1.0 + 0.1 * jax.random.normal(streams_of[3], (2, C), jnp.float32), 0.5, 1.5).astype(jnp.bfloat16)
    norm_shifts = bell_draw(streams_of[4], (2, C), 0.3, 1.5, ((1, 32),))
    head_conv = bell_draw(streams_of[5], (HEAD_CH, C), C ** -0.5, 0.375, ((1, 32),))
    head_norm_gain = jnp.clip(1.0 + 0.1 * jax.random.normal(streams_of[6], (HEAD_CH,), jnp.float32), 0.5, 1.5)
    head_norm_shift = bell_draw(streams_of[7], (HEAD_CH,), 0.5, 2.0, (), jnp.float32)
    dense_weight = bell_draw(streams_of[8], (HEAD_ROWS, MOVES), (HEAD_IN // 4) ** -0.5, 0.4375, ((0, 32),))
    legal_moves = draw_legal_moves(jax.random.fold_in(streams_of[12], 71), 0)
    target_moves = draw_target_moves(jax.random.fold_in(streams_of[12], 71), 0)
    out_cotangent = draw_out_cotangent(jax.random.fold_in(streams_of[12], 71), 0)
    return dict(board_activations_input=board_activations_input, conv1_weight=conv1_weight, conv2_weight=conv2_weight, norm_gains=norm_gains, norm_shifts=norm_shifts, head_conv=head_conv, head_norm_gain=head_norm_gain, head_norm_shift=head_norm_shift, dense_weight=dense_weight, legal_moves=legal_moves, target_moves=target_moves, out_cotangent=out_cotangent)


epsilon = 1e-05
negative_fill = -1e+30

@jax.custom_vjp
def low(v):
    return lax.optimization_barrier(v.astype(jnp.bfloat16)).astype(jnp.float32)

@jax.custom_vjp
def low_back(v):
    return v

def low_keep(v):
    return (low(v), None)

def low_pass(kept, grad):
    return (grad,)

def back_keep(v):
    return (v, None)

def back_low(kept, grad):
    return (low(grad),)
low.defvjp(low_keep, low_pass)
low_back.defvjp(back_keep, back_low)

def convolve(planes, kernel):
    filters = kernel.reshape(3, 3, kernel.shape[1], kernel.shape[2])
    return lax.conv_general_dilated(planes, filters, (1, 1), 'SAME', dimension_numbers=('NHWC', 'HWIO', 'NHWC'), precision=lax.Precision.HIGHEST)

def batch_norm(values, over_axes, gain, shift):
    center = lax.optimization_barrier(jnp.mean(values, axis=over_axes, keepdims=True))
    spread = lax.optimization_barrier(jnp.mean(jnp.square(values - center), axis=over_axes, keepdims=True))
    return (values - center) * lax.rsqrt(spread + epsilon) * gain + shift

def forward(planes, first_kernel, second_kernel, gain_rows, shift_rows, head_kernel, head_scale, head_offset, dense_rows, legal_mask, target_ids):
    first_preactivation = low_back(convolve(planes, first_kernel))
    first_normalized_output = batch_norm(first_preactivation, (0, 1, 2), gain_rows[0], shift_rows[0])
    first_act = low(jax.nn.gelu(first_normalized_output))
    second_preactivation = low_back(convolve(first_act, second_kernel))
    residual_sum = planes + batch_norm(second_preactivation, (0, 1, 2), gain_rows[1], shift_rows[1])
    output = jax.nn.gelu(residual_sum)
    rounded = low(output)
    head_preactivation = low_back(jnp.einsum('bijc,kc->bkij', rounded, head_kernel, precision=lax.Precision.HIGHEST))
    head_normalized_output = batch_norm(head_preactivation, (0, 2, 3), head_scale[None, :, None, None], head_offset[None, :, None, None])
    head_flat = low(jax.nn.gelu(head_normalized_output)).reshape(planes.shape[0], -1)
    logits = low_back(jnp.dot(head_flat, dense_rows[:HEAD_IN], precision=lax.Precision.HIGHEST) + dense_rows[HEAD_IN])
    masked = jnp.where(legal_mask == 1, logits, negative_fill)
    row_top = lax.optimization_barrier(jnp.max(masked, axis=1, keepdims=True))
    log_total = row_top[:, 0] + jnp.log(lax.optimization_barrier(jnp.sum(jnp.exp(masked - row_top), axis=1)))
    move_index = jnp.arange(MOVES, dtype=jnp.int32)[None, :]
    picked = lax.optimization_barrier(jnp.sum(jnp.where(move_index == target_ids[:, None], logits, 0.0), axis=1))
    return (output, jnp.sum(log_total - picked))

def reference(board_activations_input, conv1_weight, conv2_weight, norm_gains, norm_shifts, head_conv, head_norm_gain, head_norm_shift, dense_weight, legal_moves, target_moves, out_cotangent):
    floats = (board_activations_input.astype(jnp.float32), conv1_weight.astype(jnp.float32), conv2_weight.astype(jnp.float32), norm_gains.astype(jnp.float32), norm_shifts.astype(jnp.float32), head_conv.astype(jnp.float32), head_norm_gain.astype(jnp.float32), head_norm_shift.astype(jnp.float32), dense_weight.astype(jnp.float32))

    def objective(planes, first_kernel, second_kernel, gain_rows, shift_rows, head_kernel, head_scale, head_offset, dense_rows):
        return forward(planes, first_kernel, second_kernel, gain_rows, shift_rows, head_kernel, head_scale, head_offset, dense_rows, legal_moves, target_moves)
    (output, ce_total), pullback = jax.vjp(objective, *floats)
    grads = pullback((out_cotangent.astype(jnp.float32), jnp.ones_like(ce_total)))
    head_norm_grad = jnp.stack([grads[6], grads[7]])
    return (output.astype(jnp.bfloat16), ce_total / POSITIONS, grads[0].astype(jnp.bfloat16), grads[1], grads[2], grads[3], grads[4], grads[5], head_norm_grad, grads[8])
```

```python
import functools
import types

import jax
import jax.numpy as jnp
from jax import lax
from jax.experimental import pallas as pl
from jax.experimental.pallas import tpu as pltpu
from jax.sharding import PartitionSpec as P

MESH = pl.DeviceIdType.MESH
f32 = jnp.float32
bf16 = jnp.bfloat16
epsilon = 1e-05
negative_fill = -1e30
root = 0.7978845608028654
cube = 0.044715
lanes = 128


def up_to(value, unit):
    return -(-value // unit) * unit


def divided(values, divisor, limit):
    factor = -(-65536 // divisor)
    for n in range(limit):
        assert (n * factor) >> 16 == n // divisor and n * factor < 2**31
    return lax.shift_right_logical(values * factor, jnp.int32(16))


def iota(shape, axis):
    return lax.broadcasted_iota(jnp.int32, shape, axis)


def gelu_both(v):
    square = v * v
    slope = jnp.tanh(v * (root + (root * cube) * square))
    half = 0.5 + 0.5 * slope
    back = half + (0.5 * v) * (1.0 - slope * slope) * (root + (3.0 * root * cube) * square)
    return v * half, back


def dot(left, right):
    return jnp.dot(left, right, preferred_element_type=f32)


def dot_nt(left, right):
    return lax.dot_general(left, right, (((1,), (1,)), ((), ())), preferred_element_type=f32)


def sizes_of(gx_n, gy_n, x, w1, dense, moves):
    s = types.SimpleNamespace()
    s.gx_n, s.gy_n, s.q_n, s.n_dev = gx_n, gy_n, gy_n // 2, gx_n * gy_n
    s.nb, s.side, s.ch = x.shape[0], x.shape[1], x.shape[3]
    s.w = w1.shape[1]
    s.wide = s.side + 1
    s.br = s.wide * s.nb
    s.rows = s.side * s.br
    s.padded = s.rows + 2 * s.br
    s.gap = up_to(s.side, 8)
    s.line = up_to(s.side * s.gap, lanes)
    s.cells = s.side * s.side
    s.moves = moves
    s.mp = up_to(moves, lanes)
    s.rsh = dense.shape[0]
    s.rp = up_to(s.rsh, 16)
    s.head_in = 2 * s.cells
    s.blk = up_to(18 * s.w, 16)
    s.blk1 = up_to(19 * s.w, 16)
    s.fast = s.w == 8
    s.nch = 3 if s.fast else 1
    s.crows = s.blk // s.nch
    s.count = float(s.nb * s.cells * s.n_dev)
    assert s.nb == 4 and s.br % 16 == 0 and gy_n % 2 == 0 and 8 % s.w == 0
    return s


def kernel(s, in_names, out_names, scratch_names, *refs):
    r = types.SimpleNamespace(**dict(zip(in_names + out_names + scratch_names, refs)))
    gx, gy = lax.axis_index("gx"), lax.axis_index("gy")
    q, c = lax.div(gy, 2), lax.rem(gy, 2)
    me = gx * s.gy_n + gy
    other = (gx, gy + 1 - 2 * c)
    gxn, qn, nb, br, gap, ch = s.gx_n, s.q_n, s.nb, s.br, s.gap, s.ch

    def z_peer(k):
        return lax.rem(gx + k, gxn)

    def q_peer(j):
        return lax.rem(q + j, qn)

    def send(src, dst, out_sem, in_sem, device):
        pltpu.make_async_remote_copy(
            src_ref=src, dst_ref=dst, send_sem=out_sem, recv_sem=in_sem, device_id=device, device_id_type=MESH
        ).start()

    def take(sem, ref):
        pltpu.make_async_copy(ref, ref, sem).wait()

    barrier = pltpu.get_barrier_semaphore()
    partners = [(z_peer(k), gy) for k in range(1, gxn)]
    partners += [(gx, 2 * q_peer(j) + c) for j in range(1, qn)]
    partners += [other]
    for p in partners:
        pl.semaphore_signal(barrier, inc=1, device_id=p, device_id_type=MESH)
    fetch_x = pltpu.make_async_copy(r.x, r.x_v, r.local_sem.at[0])
    fetch_x.start()
    fetch_cot = pltpu.make_async_copy(r.cot, r.cot_v, r.local_sem.at[1])
    fetch_cot.start()

    w = s.w

    def stage(weight, rows):
        r.stage[...] = jnp.zeros_like(r.stage)
        for t in range(9):
            v = weight[t].astype(f32)
            r.stage[2 * w * t : 2 * w * t + w, :] = v[:, :lanes]
            r.stage[2 * w * t + w : 2 * w * t + 2 * w, :] = v[:, lanes:]

    r.small[...] = jnp.zeros_like(r.small)
    r.small[0:2, 0:w] = r.gains[...].astype(f32)
    r.small[2:4, 0:w] = r.shifts[...].astype(f32)
    r.small[4:6, 0:w] = r.hc[...].astype(f32)
    stage(r.w1, s.blk1)
    r.stage[18 * w : 19 * w, 0:8] = jnp.transpose(r.small[...])[0:w, :]
    r.s1[gx, q, c] = r.stage[...].astype(bf16)
    stage(r.w2, s.blk)
    r.s2[gx, q, c] = r.stage[0 : s.blk, :].astype(bf16)
    r.dense_v[...] = jnp.zeros_like(r.dense_v)
    r.dense_v[0 : s.rsh, 0 : s.moves] = r.dense[...].astype(f32)
    r.sd[gx, q, c] = r.dense_v[...].astype(bf16)

    for planes in (r.x3, r.a3, r.d3):
        planes[0:br, :] = jnp.zeros((br, 3 * ch), bf16)
        planes[s.padded - br :, :] = jnp.zeros((br, 3 * ch), bf16)
    r.slab[...] = jnp.zeros_like(r.slab)
    r.outp[:, s.side * gap :, :] = jnp.zeros((nb, s.line - s.side * gap, ch), f32)
    row, col = iota((br, nb * gap), 0), iota((br, nb * gap), 1)
    j_of, b_of = lax.shift_right_logical(row, 2), row & 3
    spread = ((col == b_of * gap + j_of) & (j_of < s.side)).astype(f32).astype(bf16)
    row, col = iota((nb * gap, br), 0), iota((nb * gap, br), 1)
    j_of, b_of = lax.shift_right_logical(col, 2), col & 3
    gather_up = ((row == b_of * gap + j_of) & (j_of < s.side)).astype(f32).astype(bf16)
    inside = iota((br, ch), 0) < nb * s.side

    def store3(planes, i, block):
        at = pl.ds(pl.multiple_of((i + 1) * br, 16), br)
        planes[at, 0:ch] = pltpu.roll(block, nb, 0).astype(bf16)
        planes[at, ch : 2 * ch] = block.astype(bf16)
        planes[at, 2 * ch :] = pltpu.roll(block, br - nb, 0).astype(bf16)

    def rows_of(i):
        return pl.ds(pl.multiple_of(i * br, 16), br)

    def to_rows(source, i):
        for b in range(nb):
            r.slab[gap * b : gap * b + s.side, :] = source[b, i].astype(f32)
        return dot(spread, r.slab[...].astype(bf16))

    def x_rows(i, _):
        store3(r.x3, i, to_rows(r.x_v, i))
        return 0

    def cot_rows(i, _):
        r.cot_r[rows_of(i), :] = to_rows(r.cot_v, i).astype(bf16)
        return 0

    fetch_x.wait()
    lax.fori_loop(0, s.side, x_rows, 0)

    pl.semaphore_wait(barrier, len(partners))

    def span(unit):
        store, part = unit
        if store is r.sd:
            return pl.ds(0, s.rp)
        whole = s.blk1 if store is r.s1 else s.blk
        if s.nch == 1:
            return pl.ds(0, whole)
        start = part * s.crows
        return pl.ds(start, whole - start if part == s.nch - 1 else s.crows)

    units = [(r.s1, p) for p in range(s.nch)] + [(r.s2, p) for p in range(s.nch)] + [(r.sd, 0)]

    def g_start(u):
        store, at = units[u][0], span(units[u])
        own = store.at[gx, q, c, at]
        for k in range(gxn - 1, 0, -1):
            send(own, own, r.g_sem.at[u, 0], r.g_sem.at[u, 1], (z_peer(k), gy))
        for j in range(1, qn):
            send(own, own, r.g_sem.at[u, 2], r.g_sem.at[u, 3], (gx, 2 * q_peer(j) + c))

    def g_forward(u):
        store, at = units[u][0], span(units[u])
        take(r.g_sem.at[u, 1], store.at[pl.ds(0, gxn - 1), 0, 0, at])
        for k in range(1, gxn):
            block = store.at[z_peer(k), q, c, at]
            for j in range(1, qn):
                send(block, block, r.g_sem.at[u, 4], r.g_sem.at[u, 3], (gx, 2 * q_peer(j) + c))

    def g_cross(u):
        store, at = units[u][0], span(units[u])
        take(r.g_sem.at[u, 3], store.at[:, pl.ds(0, qn - 1), 0, at])
        block = store.at[:, :, c, at]
        send(block, block, r.g_sem.at[u, 5], r.g_sem.at[u, 6], other)

    def g_done(u):
        store, at = units[u][0], span(units[u])
        take(r.g_sem.at[u, 6], store.at[:, :, 0, at])

    def g_drain(u):
        store, at = units[u][0], span(units[u])
        take(r.g_sem.at[u, 0], store.at[pl.ds(0, gxn - 1), 0, 0, at])
        take(r.g_sem.at[u, 2], store.at[0, pl.ds(0, qn - 1), 0, at])
        take(r.g_sem.at[u, 4], store.at[pl.ds(0, gxn - 1), pl.ds(0, qn - 1), 0, at])
        take(r.g_sem.at[u, 5], store.at[:, :, 0, at])

    def shard_of(store, d):
        return store[lax.div(d, s.gy_n), lax.div(lax.rem(d, s.gy_n), 2), lax.rem(d, 2)]

    def unpack(store, part, weight):
        if s.fast:
            for dj in range(3):
                at = 16 * (3 * part + dj)
                v = store[:, :, :, at : at + 16, :].astype(f32).reshape(s.n_dev, 16, lanes)
                low = v[:, 0:8, :].reshape(ch, lanes)
                high = v[:, 8:16, :].reshape(ch, lanes)
                weight[part, dj * ch : (dj + 1) * ch, :] = jnp.concatenate([low, high], axis=1).astype(bf16)
            return

        def one(g, _):
            for e in range(8 // w):
                r.stage[0 : s.blk, :] = shard_of(store, g * (8 // w) + e)[0 : s.blk].astype(f32)
                for t in range(9):
                    r.eight[t, w * e : w * e + w, 0:lanes] = r.stage[2 * w * t : 2 * w * t + w, :]
                    r.eight[t, w * e : w * e + w, lanes:] = r.stage[2 * w * t + w : 2 * w * t + 2 * w, :]
            for t in range(9):
                r.flat[t, pl.ds(pl.multiple_of(8 * g, 8), 8), :] = r.eight[t]
            return 0

        lax.fori_loop(0, ch // 8, one, 0)
        for t in range(9):
            weight[t // 3, (t % 3) * ch : (t % 3 + 1) * ch, :] = r.flat[t].astype(bf16)

    def unpack_small():
        if s.fast:
            v = r.s1[:, :, :, 18 * w : 18 * w + 16, :].astype(f32).reshape(s.n_dev, 16, lanes)
            rows = v[:, 0:8, :].reshape(ch, lanes)
        else:

            def one(g, _):
                for e in range(8 // w):
                    r.stage[...] = shard_of(r.s1, g * (8 // w) + e).astype(f32)
                    r.eight[0, w * e : w * e + w, 0:lanes] = r.stage[18 * w : 19 * w, :]
                r.flat[0, pl.ds(pl.multiple_of(8 * g, 8), 8), :] = r.eight[0]
                return 0

            lax.fori_loop(0, ch // 8, one, 0)
            rows = r.flat[0, :, 0:lanes]
        r.pars[...] = jnp.transpose(rows)[0:8, :]

    def x_send(number, src, slots):
        def one(n, _):
            k = s.n_dev - 1 - n
            device = (lax.rem(gx + lax.div(k, s.gy_n), gxn), lax.rem(gy + lax.rem(k, s.gy_n), s.gy_n))
            send(src, slots.at[me], r.x_sem.at[number, 0], r.x_sem.at[number, 1], device)
            return 0

        lax.fori_loop(0, s.n_dev - 1, one, 0)
        slots[me] = src[...]

    def x_wait(number, slots):
        take(r.x_sem.at[number, 1], slots.at[pl.ds(0, s.n_dev - 1)])

    def x_drain(number, slots):
        take(r.x_sem.at[number, 0], slots.at[pl.ds(0, s.n_dev - 1)])

    def rs_fill(part, grad, b):
        if s.fast:
            for dj in range(3):
                g = grad[:, (2 - dj) * ch : (3 - dj) * ch]
                low = g[:, :lanes].reshape(s.n_dev, 8, lanes)
                high = g[:, lanes:].reshape(s.n_dev, 8, lanes)
                v = jnp.concatenate([low, high], axis=1).astype(bf16).reshape(gxn, qn, 2, 16, lanes)
                for core in range(2):
                    b.rsb[part, core, :, :, 16 * dj : 16 * dj + 16, :] = v[:, :, core]
        else:
            for dj in range(3):
                r.flat[3 * part + dj] = grad[:, (2 - dj) * ch : (3 - dj) * ch]

    def rs_fill_rest(b):
        if s.fast:
            return
        r.stage[...] = jnp.zeros_like(r.stage)

        def one(g, _):
            for t in range(9):
                r.eight[t] = r.flat[t, pl.ds(pl.multiple_of(8 * g, 8), 8), :]
            for e in range(8 // w):
                d = g * (8 // w) + e
                for t in range(9):
                    v = r.eight[t, w * e : w * e + w, :]
                    r.stage[2 * w * t : 2 * w * t + w, :] = v[:, :lanes]
                    r.stage[2 * w * t + w : 2 * w * t + 2 * w, :] = v[:, lanes:]
                at = (0, lax.rem(d, 2), lax.div(d, s.gy_n), lax.div(lax.rem(d, s.gy_n), 2))
                b.rsb[at] = r.stage[0 : s.blk, :].astype(bf16)
            return 0

        lax.fori_loop(0, ch // 8, one, 0)

    def rs_cross(b, part):
        send(b.rsb.at[part, 1 - c], b.rc.at[part], b.sem.at[part, 0], b.sem.at[part, 1], other)

    def rs_plane(b, part):
        take(b.sem.at[part, 1], b.rc.at[part])
        for p in range(qn):
            total = b.rsb[part, c, :, p].astype(f32) + b.rc[part, :, p].astype(f32)
            b.pb[part, p] = total.astype(bf16)
        for j in range(1, qn):
            to = q_peer(j)
            send(b.pb.at[part, to], b.rp.at[part, j - 1], b.sem.at[part, 2], b.sem.at[part, 3], (gx, 2 * to + c))

    def rs_line(b, part):
        take(b.sem.at[part, 3], b.rp.at[part])
        total = b.pb[part, q].astype(f32)
        for j in range(qn - 1):
            total = total + b.rp[part, j].astype(f32)
        b.zb[part] = total.astype(bf16)
        for k in range(1, gxn):
            to = z_peer(k)
            send(b.zb.at[part, to], b.rz.at[part, k - 1], b.sem.at[part, 4], b.sem.at[part, 5], (to, gy))

    def rs_finish(b, part, out):
        take(b.sem.at[part, 5], b.rz.at[part])
        total = b.zb[part, gx].astype(f32)
        for k in range(gxn - 1):
            total = total + b.rz[part, k].astype(f32)
        taps = 9 // s.nch
        for t in range(taps):
            at = 2 * w * t
            out[part * taps + t] = jnp.concatenate([total[at : at + w], total[at + w : at + 2 * w]], axis=1)

    def rs_drain(b):
        for part in range(s.nch):
            take(b.sem.at[part, 0], b.rc.at[part])
            take(b.sem.at[part, 2], b.rp.at[part])
            take(b.sem.at[part, 4], b.rz.at[part])

    def rs_buffers(number):
        names = ("rsb", "rc", "pb", "rp", "zb", "rz")
        b = types.SimpleNamespace(**{n: getattr(r, n + number) for n in names})
        b.sem = getattr(r, "rs_sem" + number)
        return b

    rs1, rs2 = rs_buffers("1"), rs_buffers("2")

    def local_stats(field, out):
        pivot = field[0:1, :]

        def one(i, carry):
            d = jnp.where(inside, field[rows_of(i), :] - pivot, 0.0).reshape(br // 8, 8, ch)
            return carry[0] + jnp.sum(d, axis=0), carry[1] + jnp.sum(d * d, axis=0)

        zero = jnp.zeros((8, ch), f32)
        first, second = lax.fori_loop(0, s.side, one, (zero, zero))
        n = float(nb * s.cells)
        first = jnp.sum(first, axis=0, keepdims=True) / n
        second = jnp.sum(second, axis=0, keepdims=True) - n * first * first
        out[0:1, :] = pivot + first
        out[1:2, :] = second

    def global_stats(slots):
        v = slots[...]
        n = float(nb * s.cells)
        mean = jnp.sum(v[:, 0:1, :], axis=0) / s.n_dev
        d = v[:, 0:1, :] - mean
        spread_sum = jnp.sum(v[:, 1:2, :] + n * d * d, axis=0)
        return mean, lax.rsqrt(spread_sum / s.count + epsilon)

    n1 = s.nch
    for u in range(n1):
        g_start(u)
    for u in range(n1):
        g_forward(u)
    for u in range(n1, len(units)):
        g_start(u)
    fetch_cot.wait()
    lax.fori_loop(0, s.side, cot_rows, 0)
    r.xt[...] = jnp.transpose(r.x3[br : br + s.rows, ch : 2 * ch])
    for u in range(n1):
        g_cross(u)
    for u in range(n1, 2 * n1):
        g_forward(u)

    def conv_part(planes, weight, di, out):
        v = dot(planes[br * di : br * di + s.rows, :], weight[di])
        out[...] = v if di == 0 else out[...] + v

    def conv(planes, weight, out):
        v = dot(planes[0 : s.rows, :], weight[0])
        v = v + dot(planes[br : br + s.rows, :], weight[1])
        out[...] = v + dot(planes[2 * br : 2 * br + s.rows, :], weight[2])

    for part in range(n1):
        g_done(part)
        unpack(r.s1, part, r.wt1)
        if s.fast:
            conv_part(r.x3, r.wt1, part, r.h1)
    if not s.fast:
        conv(r.x3, r.wt1, r.h1)
    local_stats(r.h1, r.st1)
    x_send(0, r.st1, r.t1)

    unpack_small()
    for u in range(n1, 2 * n1):
        g_cross(u)
    g_forward(2 * n1)

    def flip(weight, back):
        for di in range(3):
            for dj in range(3):
                tap = weight[2 - di, (2 - dj) * ch : (3 - dj) * ch, :]
                back[di, dj * ch : (dj + 1) * ch, :] = jnp.transpose(tap)

    flip(r.wt1, r.wb1)
    for u in range(n1, 2 * n1):
        g_done(u)
        unpack(r.s2, u - n1, r.wt2)

    gain1, gain2 = r.pars[0:1, :], r.pars[1:2, :]
    shift1, shift2 = r.pars[2:3, :], r.pars[3:4, :]
    hc0, hc1 = r.pars[4:5, :], r.pars[5:6, :]

    x_wait(0, r.t1)
    mean1, inv1 = global_stats(r.t1)

    def act1(i, _):
        n = (r.h1[rows_of(i), :] - mean1) * (inv1 * gain1) + shift1
        a, back = gelu_both(n)
        r.back1[rows_of(i), :] = back
        store3(r.a3, i, jnp.where(inside, a, 0.0))
        return 0

    lax.fori_loop(0, s.side, act1, 0)
    conv(r.a3, r.wt2, r.h2)
    local_stats(r.h2, r.st2)
    x_send(1, r.st2, r.t2)

    r.at[...] = jnp.transpose(r.a3[br : br + s.rows, ch : 2 * ch])
    flip(r.wt2, r.wb2)
    g_cross(2 * n1)
    g_done(2 * n1)
    at = iota((s.line, 1), 0)
    i_of = divided(at, gap, s.line)
    j_of = at - i_of * gap
    used = (i_of < s.side) & (j_of < s.side)
    wide_slots = s.n_dev * s.rp
    shard_rows = iota((s.line, wide_slots), 1)
    dense_all = r.sd[...].reshape(wide_slots, s.mp)
    for k in range(2):
        source = k * s.cells + i_of * s.side + j_of
        if k == 0:
            source = jnp.where(at == s.side, s.head_in, source)
            wanted = used | (at == s.side)
        else:
            wanted = used
        source = jnp.where(wanted, source, 0)
        shard = divided(source, s.rsh, 1024)
        place = jnp.where(wanted, shard * s.rp + (source - shard * s.rsh), -1)
        pick = (shard_rows == place).astype(f32).astype(bf16)
        r.dk[k] = dot(pick, dense_all).astype(bf16)
    row, col = iota((s.rows, s.line), 0), iota((s.rows, s.line), 1)
    row_line = lax.shift_right_logical(iota((s.rows, 1), 0), 2)
    row_i = divided(row_line, s.wide, s.rows // nb)
    row_at = row_i * gap + (row_line - row_i * s.wide)
    r.expand[...] = (col == row_at).astype(f32).astype(bf16)
    r.dp_full[...] = jnp.zeros_like(r.dp_full)
    r.hc_full[...] = jnp.zeros_like(r.hc_full)
    row = iota((16, ch), 0)
    both = jnp.where(row < nb, hc0, jnp.where(row < 2 * nb, hc1, 0.0))
    r.hc_full[0:16, :] = both.astype(bf16)

    x_wait(1, r.t2)
    mean2, inv2 = global_stats(r.t2)

    def act2(i, _):
        at = rows_of(i)
        xin = r.x3[pl.ds(pl.multiple_of((i + 1) * br, 16), br), ch : 2 * ch].astype(f32)
        z = xin + ((r.h2[at, :] - mean2) * (inv2 * gain2) + shift2)
        a, back = gelu_both(z)
        r.dz[at, :] = back
        up = dot(gather_up, jnp.where(inside, a, 0.0).astype(bf16))
        for b in range(nb):
            r.outp[b, pl.ds(pl.multiple_of(i * gap, 8), gap), :] = up[gap * b : gap * b + gap]
            r.out[b, i] = up[gap * b : gap * b + s.side].astype(bf16)
        return 0

    lax.fori_loop(0, s.side, act2, 0)
    row = iota((8, s.line), 0)
    lane = iota((8, s.line), 1)
    lane_i = divided(lane, gap, s.line)
    valid = (lane_i < s.side) & (lane - lane_i * gap < s.side)
    first_head = row < nb
    row256 = iota((16, ch), 0)
    p8 = jnp.zeros((8, s.line), f32)
    for b in range(nb):
        head = jnp.where(row256 == b, hc0, jnp.where(row256 == nb + b, hc1, 0.0)).astype(bf16)
        p8 = p8 + dot_nt(head, r.outp[b].astype(bf16))[0:8]

    row1, lane1 = iota((8, lanes), 0), iota((8, lanes), 1)

    def by_head(v):
        a = v[0:1] + v[1:2] + v[2:3] + v[3:4]
        b = v[4:5] + v[5:6] + v[6:7] + v[7:8]
        return jnp.where(iota(v.shape, 0) < nb, a, b)

    cells = float(s.cells)
    mean_row = jnp.sum(jnp.where(valid, p8, 0.0), axis=1, keepdims=True) / cells
    dev = jnp.where(valid, p8 - mean_row, 0.0)
    square_row = jnp.sum(dev * dev, axis=1, keepdims=True)
    r.st3[...] = jnp.where(lane1 < 64, mean_row, square_row)
    x_send(2, r.st3, r.t3)
    x_wait(2, r.t3)
    v = r.t3[...]
    mean_p = by_head(jnp.sum(v, axis=0))[:, 0:1] / float(nb * s.n_dev)
    dev = v - mean_p
    squares = by_head(jnp.sum(jnp.where(lane1 < 64, cells * dev * dev, v), axis=0))
    inv_p = lax.rsqrt((squares[:, 0:1] + squares[:, 64:65]) / s.count + epsilon)
    gain_p = jnp.where(iota((8, 1), 0) < nb, r.hng[0], r.hng[1])
    shift_p = jnp.where(iota((8, 1), 0) < nb, r.hns[0], r.hns[1])
    xhat_p = (p8 - mean_p) * inv_p
    feature, back_p = gelu_both(xhat_p * gain_p + shift_p)
    flat = jnp.where(valid, feature, 0.0).astype(bf16)
    one_lane = first_head & (lane == s.side)
    flat_f = flat.astype(f32)
    lhs0 = jnp.where(one_lane, 1.0, jnp.where(first_head, flat_f, 0.0))
    lhs1 = jnp.where(first_head, 0.0, flat_f)
    pad8 = jnp.zeros((8, s.line), f32)

    def tall(v):
        return jnp.concatenate([v, pad8[:, : v.shape[1]]], axis=0).astype(bf16)

    half = (dot(tall(lhs0), r.dk[0]) + dot(tall(lhs1), r.dk[1]))[0:8]
    logits = half + pltpu.roll(half, nb, 0)
    move = iota((8, s.mp), 1)
    r.legal_v[...] = jnp.zeros_like(r.legal_v)
    r.legal_v[0:nb, 0 : s.moves] = r.legal[...]
    r.legal_v[nb : 2 * nb, 0 : s.moves] = r.legal[...]
    masked = jnp.where(r.legal_v[...] == 1, logits, negative_fill)
    top = jnp.max(masked, axis=1, keepdims=True)
    terms = jnp.exp(masked - top)
    total = jnp.sum(terms, axis=1, keepdims=True)
    row_b = iota((8, 1), 0) & (nb - 1)
    target = jnp.where(
        row_b < 2,
        jnp.where(row_b == 0, r.target[0], r.target[1]),
        jnp.where(row_b == 2, r.target[2], r.target[3]),
    )
    chosen = move == target
    picked = jnp.sum(jnp.where(chosen, logits, 0.0), axis=1, keepdims=True)
    ce = top + jnp.log(total) - picked
    dl = (terms / total - chosen.astype(f32)).astype(bf16).astype(f32)
    first_move = iota((8, s.mp), 0) < nb
    dq = dot_nt(tall(jnp.where(first_move, dl, 0.0)), r.dk[0]) + dot_nt(
        tall(jnp.where(first_move, 0.0, dl)), r.dk[1]
    )
    dnh = jnp.where(valid, dq[0:8] * back_p, 0.0)
    gain_row = jnp.sum(dnh * xhat_p, axis=1, keepdims=True)
    shift_row = jnp.sum(dnh, axis=1, keepdims=True)
    r.st4[...] = jnp.where(lane1 < 32, gain_row, jnp.where(lane1 < 64, shift_row, ce))
    x_send(3, r.st4, r.t4)
    r.fd_own[...] = jnp.zeros_like(r.fd_own)
    r.fd_own[0:8, :] = flat_f
    r.fd_own[8:16, 0 : s.mp] = dl
    r.fd_send[...] = r.fd_own[...].astype(bf16)
    x_send(6, r.fd_send, r.fd)
    x_wait(3, r.t4)
    sums = by_head(jnp.sum(r.t4[...], axis=0))
    gain_sum, shift_sum = sums[:, 0:1], sums[:, 32:33]
    r.loss[...] = sums[0:1, 64:65] / float(nb * s.n_dev)
    pair = jnp.where(iota((1, lanes), 1) == 0, sums[0:1, :], sums[4:5, :])
    pair_gain = jnp.where(iota((1, lanes), 1) == 0, sums[0:1, 0:1], sums[4:5, 0:1])
    pair_shift = jnp.where(iota((1, lanes), 1) == 0, sums[0:1, 32:33], sums[4:5, 32:33])
    r.hng_grad[0:1, :] = pair_gain[:, 0:2]
    r.hng_grad[1:2, :] = pair_shift[:, 0:2]
    dp = gain_p * inv_p * (dnh - (shift_sum + xhat_p * gain_sum) / s.count)
    dp = jnp.where(valid, dp, 0.0)
    r.dp_full[0:16, :] = tall(dp)

    spread_p = dot_nt(r.expand[...], r.dp_full[...])
    row, col = iota((s.rows, lanes), 0), iota((s.rows, lanes), 1)
    spread_p = jnp.where((row & (nb - 1)) == (col & (nb - 1)), spread_p, 0.0).astype(bf16)
    r.up[...] = dot(spread_p, r.hc_full[...])

    def sums_back(field, xhat, carry):
        f = field.reshape(br // 8, 8, ch)
        g = (field * xhat).reshape(br // 8, 8, ch)
        return carry[0] + jnp.sum(g, axis=0), carry[1] + jnp.sum(f, axis=0)

    def back2(i, carry):
        at = rows_of(i)
        dz = (r.cot_r[at, :].astype(f32) + r.up[at, :]) * r.dz[at, :]
        dz = jnp.where(inside, dz, 0.0)
        r.dz[at, :] = dz
        return sums_back(dz, (r.h2[at, :] - mean2) * inv2, carry)

    zero = jnp.zeros((8, ch), f32)
    g2, s2 = lax.fori_loop(0, s.side, back2, (zero, zero))
    r.st5[0:1, :] = jnp.sum(g2, axis=0, keepdims=True)
    r.st5[1:2, :] = jnp.sum(s2, axis=0, keepdims=True)
    x_send(4, r.st5, r.t5)

    head_grad = jnp.zeros((16, ch), f32)
    dp_f = r.dp_full[0:16, :].astype(f32)
    for b in range(nb):
        rows_b = jnp.where((iota((16, s.line), 0) & (nb - 1)) == b, dp_f, 0.0).astype(bf16)
        head_grad = head_grad + dot(rows_b, r.outp[b].astype(bf16))
    r.st6[2:3, :] = head_grad[0:1] + head_grad[1:2] + head_grad[2:3] + head_grad[3:4]
    r.st6[3:4, :] = head_grad[4:5] + head_grad[5:6] + head_grad[6:7] + head_grad[7:8]
    x_wait(4, r.t5)
    t5 = jnp.sum(r.t5[...], axis=0)
    g2s, s2s = t5[0:1], t5[1:2]

    def to_field2(i, _):
        at = rows_of(i)
        xhat = (r.h2[at, :] - mean2) * inv2
        d = (gain2 * inv2) * (r.dz[at, :] - (s2s + xhat * g2s) * (1.0 / s.count))
        store3(r.d3, i, jnp.where(inside, d, 0.0))
        return 0

    lax.fori_loop(0, s.side, to_field2, 0)

    def wgrad(planes_t, di):
        start = 2 * br - br * di
        return dot(planes_t[...], r.d3[start : start + s.rows, :])

    for di in range(3):
        rs_fill(di, wgrad(r.at, di), rs2)
        if s.fast:
            rs_cross(rs2, di)
    rs_fill_rest(rs2)
    if not s.fast:
        rs_cross(rs2, 0)
    conv(r.d3, r.wb2, r.h2)
    for part in range(s.nch):
        rs_plane(rs2, part)

    def back1(i, carry):
        at = rows_of(i)
        dn = jnp.where(inside, r.h2[at, :] * r.back1[at, :], 0.0)
        r.h2[at, :] = dn
        return sums_back(dn, (r.h1[at, :] - mean1) * inv1, carry)

    g1, s1 = lax.fori_loop(0, s.side, back1, (zero, zero))
    r.st6[0:1, :] = jnp.sum(g1, axis=0, keepdims=True)
    r.st6[1:2, :] = jnp.sum(s1, axis=0, keepdims=True)
    x_send(5, r.st6, r.t6)
    for part in range(s.nch):
        rs_line(rs2, part)
    x_wait(5, r.t6)
    t6 = jnp.sum(r.t6[...], axis=0)
    g1s, s1s = t6[0:1], t6[1:2]

    def to_field1(i, _):
        at = rows_of(i)
        xhat = (r.h1[at, :] - mean1) * inv1
        d = (gain1 * inv1) * (r.h2[at, :] - (s1s + xhat * g1s) * (1.0 / s.count))
        store3(r.d3, i, jnp.where(inside, d, 0.0))
        return 0

    lax.fori_loop(0, s.side, to_field1, 0)
    for di in range(3):
        rs_fill(di, wgrad(r.xt, di), rs1)
        if s.fast:
            rs_cross(rs1, di)
    rs_fill_rest(rs1)
    if not s.fast:
        rs_cross(rs1, 0)
    for part in range(s.nch):
        rs_plane(rs1, part)
    conv(r.d3, r.wb1, r.h1)
    for part in range(s.nch):
        rs_line(rs1, part)

    def result(i, _):
        at = rows_of(i)
        up = dot(gather_up, (r.dz[at, :] + r.h1[at, :]).astype(bf16))
        for b in range(nb):
            r.in_grad[b, i] = up[gap * b : gap * b + s.side].astype(bf16)
        return 0

    lax.fori_loop(0, s.side, result, 0)
    shares = jnp.concatenate([g1s, g2s, s1s, s2s, t6[2:4], jnp.zeros((2, ch), f32)], axis=0)
    r.share[...] = pltpu.roll(shares, lax.rem(ch - w * me, ch), 1)
    r.gains_grad[...] = r.share[0:2, 0:w]
    r.shifts_grad[...] = r.share[2:4, 0:w]
    r.hc_grad[...] = r.share[4:6, 0:w]

    x_wait(6, r.fd)
    fd = r.fd[...].astype(f32)
    features = fd[:, 0:8, :].reshape(8 * s.n_dev, s.line).astype(bf16)
    dls = fd[:, 8:16, 0 : s.mp].reshape(8 * s.n_dev, s.mp).astype(bf16)
    t = iota((s.rp, 1), 0)
    source = s.rsh * me + t
    mine = (t < s.rsh) & (source < s.head_in)
    col = iota((s.rp, s.line), 1)
    col8 = iota((s.rp, 8 * s.n_dev), 1) & 7
    own = jnp.where((t < s.rsh) & (source == s.head_in) & (col8 < nb), 1.0, 0.0)
    for k in range(2):
        in_k = mine & (source >= k * s.cells) & (source < (k + 1) * s.cells)
        cell = jnp.where(in_k, source - k * s.cells, 0)
        cell_i = divided(cell, s.side, s.cells)
        place = jnp.where(in_k, cell_i * gap + (cell - cell_i * s.side), -1)
        pick = (col == place).astype(f32).astype(bf16)
        rows_k = dot_nt(pick, features)
        own = own + jnp.where((col8 >= nb) if k else (col8 < nb), rows_k, 0.0)
    grad = dot(own.astype(bf16), dls)
    r.dense_v[...] = grad
    r.dense_grad[...] = r.dense_v[0 : s.rsh, 0 : s.moves]

    for part in range(s.nch):
        rs_finish(rs2, part, r.c2_grad)
    for part in range(s.nch):
        rs_finish(rs1, part, r.c1_grad)

    for u in range(len(units)):
        g_drain(u)
    for number, slots in enumerate((r.t1, r.t2, r.t3, r.t4, r.t5, r.t6, r.fd)):
        x_drain(number, slots)
    rs_drain(rs1)
    rs_drain(rs2)


def body(x, w1, w2, gains, shifts, hc, hng, hns, dense, legal, target, cot):
    s = sizes_of(lax.axis_size("gx"), lax.axis_size("gy"), x, w1, dense, legal.shape[1])
    vmem, smem, hbm = pltpu.VMEM, pltpu.SMEM, pl.ANY
    inputs = dict(
        x=(x, hbm), w1=(w1, vmem), w2=(w2, vmem), gains=(gains, vmem), shifts=(shifts, vmem), hc=(hc, vmem),
        hng=(hng, smem), hns=(hns, smem), dense=(dense, vmem), legal=(legal, vmem), target=(target, smem), cot=(cot, hbm),
    )
    outputs = dict(
        out=(x.shape, bf16), loss=((1, 1), f32), in_grad=(x.shape, bf16), c1_grad=(w1.shape, f32),
        c2_grad=(w2.shape, f32), gains_grad=(gains.shape, f32), shifts_grad=(shifts.shape, f32),
        hc_grad=(hc.shape, f32), hng_grad=((2, 2), f32), dense_grad=(dense.shape, f32),
    )
    gxn, qn, n, ch = s.gx_n, s.q_n, s.n_dev, s.ch
    field = pltpu.VMEM((s.rows, ch), f32)
    planes = pltpu.VMEM((s.padded, 3 * ch), bf16)
    turned = pltpu.VMEM((ch, s.rows), bf16)
    weight = pltpu.VMEM((3, 3 * ch, ch), bf16)
    two = pltpu.VMEM((2, ch), f32)
    four = pltpu.VMEM((4, ch), f32)
    tile = pltpu.VMEM((8, lanes), f32)
    dma = pltpu.SemaphoreType.DMA
    scratch = dict(
        local_sem=dma((2,)), g_sem=dma((2 * s.nch + 1, 7)), x_sem=dma((7, 2)),
        rs_sem1=dma((s.nch, 6)), rs_sem2=dma((s.nch, 6)),
        x_v=pltpu.VMEM(x.shape, bf16), cot_v=pltpu.VMEM(x.shape, bf16),
        stage=pltpu.VMEM((s.blk1, lanes), f32), small=pltpu.VMEM((8, lanes), f32),
        s1=pltpu.VMEM((gxn, qn, 2, s.blk1, lanes), bf16), s2=pltpu.VMEM((gxn, qn, 2, s.blk, lanes), bf16),
        sd=pltpu.VMEM((gxn, qn, 2, s.rp, s.mp), bf16), dense_v=pltpu.VMEM((s.rp, s.mp), f32),
        x3=planes, a3=planes, d3=planes, slab=pltpu.VMEM((s.nb * s.gap, ch), f32),
        outp=pltpu.VMEM((s.nb, s.line, ch), f32), cot_r=pltpu.VMEM((s.rows, ch), bf16),
        xt=turned, at=turned, wt1=weight, wt2=weight, wb1=weight, wb2=weight,
        pars=pltpu.VMEM((8, ch), f32), h1=field, h2=field, dz=field, back1=field, up=field,
        st1=two, t1=pltpu.VMEM((n, 2, ch), f32), st2=two, t2=pltpu.VMEM((n, 2, ch), f32),
        st3=tile, t3=pltpu.VMEM((n, 8, lanes), f32), st4=tile, t4=pltpu.VMEM((n, 8, lanes), f32),
        st5=two, t5=pltpu.VMEM((n, 2, ch), f32), st6=four, t6=pltpu.VMEM((n, 4, ch), f32),
        fd_own=pltpu.VMEM((16, s.line), f32), fd_send=pltpu.VMEM((16, s.line), bf16),
        fd=pltpu.VMEM((n, 16, s.line), bf16),
        dk=pltpu.VMEM((2, s.line, s.mp), bf16), expand=pltpu.VMEM((s.rows, s.line), bf16),
        dp_full=pltpu.VMEM((lanes, s.line), bf16), hc_full=pltpu.VMEM((lanes, ch), bf16),
        legal_v=pltpu.VMEM((8, s.mp), jnp.int32), share=pltpu.VMEM((8, ch), f32),
    )
    if not s.fast:
        scratch["flat"] = pltpu.VMEM((9, ch, ch), f32)
        scratch["eight"] = pltpu.VMEM((9, 8, ch), f32)
    for number in ("1", "2"):
        scratch["rsb" + number] = pltpu.VMEM((s.nch, 2, gxn, qn, s.crows, lanes), bf16)
        scratch["rc" + number] = pltpu.VMEM((s.nch, gxn, qn, s.crows, lanes), bf16)
        scratch["pb" + number] = pltpu.VMEM((s.nch, qn, gxn, s.crows, lanes), bf16)
        scratch["rp" + number] = pltpu.VMEM((s.nch, qn - 1, gxn, s.crows, lanes), bf16)
        scratch["zb" + number] = pltpu.VMEM((s.nch, gxn, s.crows, lanes), bf16)
        scratch["rz" + number] = pltpu.VMEM((s.nch, gxn - 1, s.crows, lanes), bf16)
    run = pl.pallas_call(
        functools.partial(kernel, s, tuple(inputs), tuple(outputs), tuple(scratch)),
        out_shape=[jax.ShapeDtypeStruct(shape, kind) for shape, kind in outputs.values()],
        in_specs=[pl.BlockSpec(memory_space=space) for _, space in inputs.values()],
        out_specs=[pl.BlockSpec(memory_space=vmem) for _ in outputs],
        scratch_shapes=list(scratch.values()),
        compiler_params=pltpu.CompilerParams(
            collective_id=0, has_side_effects=True, vmem_limit_bytes=60 * 1024 * 1024
        ),
        cost_estimate=pl.CostEstimate(flops=10_500_000_000, bytes_accessed=8_000_000, transcendentals=800_000),
        name="tower",
    )
    results = run(*(value for value, _ in inputs.values()))
    return (results[0], results[1].reshape(()), *results[2:])


def solution(mesh):
    both = ("gx", "gy")
    board = P(both, None, None, None)
    kernels = P(None, both, None)
    pairs = P(None, both)
    return jax.shard_map(
        body,
        mesh=mesh,
        in_specs=(
            board, kernels, kernels, pairs, pairs, pairs, P(), P(), P(both, None), P(both, None), P(both), board,
        ),
        out_specs=(board, P(), board, kernels, kernels, pairs, pairs, pairs, P(), P(both, None)),
        check_vma=False,
    )
```

```python
import functools
import types

import jax
import jax.numpy as jnp
from jax import lax
from jax.experimental import pallas as pl
from jax.experimental.pallas import tpu as pltpu
from jax.sharding import PartitionSpec as P

MESH = pl.DeviceIdType.MESH
f32 = jnp.float32
bf16 = jnp.bfloat16
epsilon = 1e-05
negative_fill = -1e30
root = 0.7978845608028654
cube = 0.044715
lanes = 128


def up_to(value, unit):
    return -(-value // unit) * unit


def divided(values, divisor, limit):
    for shift in range(16, 24):
        factor = -(-(1 << shift) // divisor)
        if all((n * factor) >> shift == n // divisor and n * factor < 2**31 for n in range(limit)):
            return lax.shift_right_logical(values * factor, jnp.int32(shift))
    raise ValueError("no factor")


def iota(shape, axis):
    return lax.broadcasted_iota(jnp.int32, shape, axis)


def gelu_both(v):
    square = v * v
    slope = jnp.tanh(v * (root + (root * cube) * square))
    half = 0.5 + 0.5 * slope
    back = half + (0.5 * v) * (1.0 - slope * slope) * (root + (3.0 * root * cube) * square)
    return v * half, back


def gelu(v):
    half = 0.5 * v
    return half + half * jnp.tanh(v * (root + (root * cube) * (v * v)))


def dot(left, right):
    return jnp.dot(left, right, preferred_element_type=f32)


def dot_nt(left, right):
    return lax.dot_general(left, right, (((1,), (1,)), ((), ())), preferred_element_type=f32)


def sizes_of(gx_n, gy_n, x, w1, dense, moves):
    s = types.SimpleNamespace()
    s.gx_n, s.gy_n, s.q_n, s.n_dev = gx_n, gy_n, gy_n // 2, gx_n * gy_n
    s.side, s.nb, s.ch = x.shape[0], x.shape[2], x.shape[3]
    s.w = w1.shape[1]
    s.wide = s.side + 1
    s.br = s.wide * s.nb
    s.rows = s.side * s.br
    s.padded = s.rows + 2 * s.br
    s.line = up_to(s.side * s.wide, lanes)
    s.long = up_to(s.rows, lanes)
    s.cells = s.side * s.side
    s.moves = moves
    s.mp = up_to(moves, lanes)
    s.rsh = dense.shape[0]
    s.rp = up_to(s.rsh, 16)
    s.head_in = 2 * s.cells
    s.blk = up_to(18 * s.w, 16)
    s.blk1 = up_to(19 * s.w, 16)
    s.fast = s.w == 8
    s.nch = 3 if s.fast else 1
    s.crows = s.blk // s.nch
    s.count = float(s.nb * s.cells * s.n_dev)
    assert s.nb == 4 and s.br % 16 == 0 and 8 % s.w == 0
    assert gx_n & (gx_n - 1) == 0 and gy_n & (gy_n - 1) == 0 and gy_n > 1
    return s


def kernel(s, in_names, out_names, scratch_names, *refs):
    r = types.SimpleNamespace(**dict(zip(in_names + out_names + scratch_names, refs)))
    gx, gy = lax.axis_index("gx"), lax.axis_index("gy")
    q, c = lax.div(gy, 2), lax.rem(gy, 2)
    me = gx * s.gy_n + gy
    other = (gx, gy + 1 - 2 * c)
    gxn, qn, nb, br, wide, ch = s.gx_n, s.q_n, s.nb, s.br, s.wide, s.ch

    def z_peer(k):
        return gx ^ k

    def q_peer(j):
        return q ^ j

    def send(src, dst, out_sem, in_sem, device):
        pltpu.make_async_remote_copy(
            src_ref=src, dst_ref=dst, send_sem=out_sem, recv_sem=in_sem, device_id=device, device_id_type=MESH
        ).start()

    def take(sem, ref):
        pltpu.make_async_copy(ref, ref, sem).wait()

    barrier = pltpu.get_barrier_semaphore()
    partners = [(z_peer(k), gy) for k in range(1, gxn)]
    partners += [(gx, 2 * q_peer(j) + c) for j in range(1, qn)]
    partners += [other]
    for p in partners:
        pl.semaphore_signal(barrier, inc=1, device_id=p, device_id_type=MESH)
    fetch_x = pltpu.make_async_copy(r.x, r.x_v.at[:, pl.ds(0, s.side)], r.local_sem.at[0])
    fetch_x.start()
    fetch_cot = pltpu.make_async_copy(r.cot, r.cot_v.at[:, pl.ds(0, s.side)], r.local_sem.at[1])
    fetch_cot.start()
    for fields in (r.x_v, r.cot_v):
        fields[:, s.side] = jnp.zeros((s.side, nb, ch), bf16)

    w = s.w

    def stage(weight, rows):
        r.stage[...] = jnp.zeros_like(r.stage)
        for t in range(9):
            v = weight[t].astype(f32)
            r.stage[2 * w * t : 2 * w * t + w, :] = v[:, :lanes]
            r.stage[2 * w * t + w : 2 * w * t + 2 * w, :] = v[:, lanes:]

    r.small[...] = jnp.zeros_like(r.small)
    r.small[0:2, 0:w] = r.gains[...].astype(f32)
    r.small[2:4, 0:w] = r.shifts[...].astype(f32)
    r.small[4:6, 0:w] = r.hc[...].astype(f32)
    stage(r.w1, s.blk1)
    r.stage[18 * w : 19 * w, 0:8] = jnp.transpose(r.small[...])[0:w, :]
    r.s1[gx, q, c] = r.stage[...].astype(bf16)
    stage(r.w2, s.blk)
    r.s2[gx, q, c] = r.stage[0 : s.blk, :].astype(bf16)
    r.dense_v[...] = jnp.zeros_like(r.dense_v)
    r.dense_v[0 : s.rsh, 0 : s.moves] = r.dense[...].astype(f32)
    r.sd[gx, q, c] = r.dense_v[...].astype(bf16)

    for planes in (r.x3, r.a3, r.d3):
        planes[0:br, :] = jnp.zeros((br, 3 * ch), bf16)
        planes[s.padded - br :, :] = jnp.zeros((br, 3 * ch), bf16)
    inside = iota((br, ch), 0) < nb * s.side

    def store3(planes, i, block):
        at = pl.ds(pl.multiple_of((i + 1) * br, 16), br)
        planes[at, 0:ch] = pltpu.roll(block, nb, 0).astype(bf16)
        planes[at, ch : 2 * ch] = block.astype(bf16)
        planes[at, 2 * ch :] = pltpu.roll(block, br - nb, 0).astype(bf16)

    def rows_of(i):
        return pl.ds(pl.multiple_of(i * br, 16), br)

    def from_board(block):
        return block.astype(f32).reshape(br, ch)

    def to_board(block):
        return block.reshape(wide, nb, ch)[0 : s.side].astype(bf16)

    def x_rows(i, _):
        store3(r.x3, i, from_board(r.x_v[i]))
        return 0

    fetch_x.wait()
    lax.fori_loop(0, s.side, x_rows, 0)

    pl.semaphore_wait(barrier, len(partners))

    def span(unit):
        store, part = unit
        if store is r.sd or store is r.fd:
            return pl.ds(0, store.shape[3])
        whole = s.blk1 if store is r.s1 else s.blk
        if s.nch == 1:
            return pl.ds(0, whole)
        start = part * s.crows
        return pl.ds(start, whole - start if part == s.nch - 1 else s.crows)

    units = [(r.s1, p) for p in range(s.nch)] + [(r.s2, p) for p in range(s.nch)] + [(r.sd, 0), (r.fd, 0)]

    def g_start(u):
        store, at = units[u][0], span(units[u])
        own = store.at[gx, q, c, at]
        for k in range(1, gxn):
            send(own, own, r.g_sem.at[u, 0], r.g_sem.at[u, 5 + k], (z_peer(k), gy))
        for j in range(qn - 1, 0, -1):
            send(own, own, r.g_sem.at[u, 1], r.g_sem.at[u, 4], (gx, 2 * q_peer(j) + c))

    def g_forward(u):
        store, at = units[u][0], span(units[u])
        for k in range(1, gxn):
            block = store.at[z_peer(k), q, c, at]
            take(r.g_sem.at[u, 5 + k], block)
            for j in range(qn - 1, 0, -1):
                send(block, block, r.g_sem.at[u, 2], r.g_sem.at[u, 4], (gx, 2 * q_peer(j) + c))

    def g_cross(u):
        store, at = units[u][0], span(units[u])
        take(r.g_sem.at[u, 4], store.at[:, pl.ds(0, qn - 1), 0, at])
        block = store.at[:, :, c, at]
        send(block, block, r.g_sem.at[u, 3], r.g_sem.at[u, 5], other)

    def g_done(u):
        store, at = units[u][0], span(units[u])
        take(r.g_sem.at[u, 5], store.at[:, :, 0, at])

    def g_drain(u):
        store, at = units[u][0], span(units[u])
        take(r.g_sem.at[u, 0], store.at[pl.ds(0, gxn - 1), 0, 0, at])
        take(r.g_sem.at[u, 1], store.at[0, pl.ds(0, qn - 1), 0, at])
        take(r.g_sem.at[u, 2], store.at[pl.ds(0, gxn - 1), pl.ds(0, qn - 1), 0, at])
        take(r.g_sem.at[u, 3], store.at[:, :, 0, at])

    def shard_of(store, d):
        return store[lax.div(d, s.gy_n), lax.div(lax.rem(d, s.gy_n), 2), lax.rem(d, 2)]

    def unpack(store, part, weight):
        if s.fast:
            for dj in range(3):
                at = 16 * (3 * part + dj)
                v = store[:, :, :, at : at + 16, :].astype(f32).reshape(s.n_dev, 16, lanes)
                low = v[:, 0:8, :].reshape(ch, lanes)
                high = v[:, 8:16, :].reshape(ch, lanes)
                weight[part, dj * ch : (dj + 1) * ch, :] = jnp.concatenate([low, high], axis=1).astype(bf16)
            return

        def one(g, _):
            for e in range(8 // w):
                r.stage[0 : s.blk, :] = shard_of(store, g * (8 // w) + e)[0 : s.blk].astype(f32)
                for t in range(9):
                    r.eight[t, w * e : w * e + w, 0:lanes] = r.stage[2 * w * t : 2 * w * t + w, :]
                    r.eight[t, w * e : w * e + w, lanes:] = r.stage[2 * w * t + w : 2 * w * t + 2 * w, :]
            for t in range(9):
                r.flat[t, pl.ds(pl.multiple_of(8 * g, 8), 8), :] = r.eight[t]
            return 0

        lax.fori_loop(0, ch // 8, one, 0)
        for t in range(9):
            weight[t // 3, (t % 3) * ch : (t % 3 + 1) * ch, :] = r.flat[t].astype(bf16)

    def unpack_small():
        if s.fast:
            v = r.s1[:, :, :, 18 * w : 18 * w + 16, :].astype(f32).reshape(s.n_dev, 16, lanes)
            rows = v[:, 0:8, :].reshape(ch, lanes)
        else:

            def one(g, _):
                for e in range(8 // w):
                    r.stage[...] = shard_of(r.s1, g * (8 // w) + e).astype(f32)
                    r.eight[0, w * e : w * e + w, 0:lanes] = r.stage[18 * w : 19 * w, :]
                r.flat[0, pl.ds(pl.multiple_of(8 * g, 8), 8), :] = r.eight[0]
                return 0

            lax.fori_loop(0, ch // 8, one, 0)
            rows = r.flat[0, :, 0:lanes]
        r.pars[...] = jnp.transpose(rows)[0:8, :]

    def x_send(number, src, slots):
        def one(k):
            device = (gx ^ lax.div(k, s.gy_n), gy ^ lax.rem(k, s.gy_n))
            send(src, slots.at[me], r.x_sem.at[number, 0], r.x_sem.at[number, 1], device)

        if s.n_dev <= 64:
            hops = {k: k // s.gy_n + bin(k % s.gy_n // 2).count("1") for k in range(1, s.n_dev)}
            for k in sorted(hops, key=lambda k: (-hops[k], k)):
                send(
                    src, slots.at[me], r.x_sem.at[number, 0], r.x_sem.at[number, 1],
                    (gx ^ (k // s.gy_n), gy ^ (k % s.gy_n)),
                )
        else:
            lax.fori_loop(0, s.n_dev - 1, lambda n, _: (one(s.n_dev - 1 - n), 0)[1], 0)
        slots[me] = src[...]

    def x_wait(number, slots):
        take(r.x_sem.at[number, 1], slots.at[pl.ds(0, s.n_dev - 1)])

    def x_drain(number, slots):
        take(r.x_sem.at[number, 0], slots.at[pl.ds(0, s.n_dev - 1)])

    def rs_fill(part, grad, b):
        if s.fast:
            for dj in range(3):
                g = grad[:, (2 - dj) * ch : (3 - dj) * ch]
                low = g[:, :lanes].reshape(s.n_dev, 8, lanes)
                high = g[:, lanes:].reshape(s.n_dev, 8, lanes)
                v = jnp.concatenate([low, high], axis=1).astype(bf16).reshape(gxn, qn, 2, 16, lanes)
                for core in range(2):
                    b.rsb[part, core, :, :, 16 * dj : 16 * dj + 16, :] = v[:, :, core]
        else:
            for dj in range(3):
                r.flat[3 * part + dj] = grad[:, (2 - dj) * ch : (3 - dj) * ch]

    def rs_fill_rest(b):
        if s.fast:
            return
        r.stage[...] = jnp.zeros_like(r.stage)

        def one(g, _):
            for t in range(9):
                r.eight[t] = r.flat[t, pl.ds(pl.multiple_of(8 * g, 8), 8), :]
            for e in range(8 // w):
                d = g * (8 // w) + e
                for t in range(9):
                    v = r.eight[t, w * e : w * e + w, :]
                    r.stage[2 * w * t : 2 * w * t + w, :] = v[:, :lanes]
                    r.stage[2 * w * t + w : 2 * w * t + 2 * w, :] = v[:, lanes:]
                at = (0, lax.rem(d, 2), lax.div(d, s.gy_n), lax.div(lax.rem(d, s.gy_n), 2))
                b.rsb[at] = r.stage[0 : s.blk, :].astype(bf16)
            return 0

        lax.fori_loop(0, ch // 8, one, 0)

    def rs_cross(b, part):
        send(b.rsb.at[part, 1 - c], b.rc.at[part], b.sem.at[part, 0], b.sem.at[part, 1], other)

    def rs_plane(b, part):
        take(b.sem.at[part, 1], b.rc.at[part])
        for p in range(qn):
            total = b.rsb[part, c, :, p].astype(f32) + b.rc[part, :, p].astype(f32)
            b.pb[part, p] = total.astype(bf16)
        for j in range(1, qn):
            to = q_peer(j)
            send(b.pb.at[part, to], b.rp.at[part, j - 1], b.sem.at[part, 2], b.sem.at[part, 3], (gx, 2 * to + c))

    def rs_line(b, part):
        take(b.sem.at[part, 3], b.rp.at[part])
        total = b.pb[part, q].astype(f32)
        for j in range(qn - 1):
            total = total + b.rp[part, j].astype(f32)
        b.zb[part] = total.astype(bf16)
        for k in range(1, gxn):
            to = z_peer(k)
            send(b.zb.at[part, to], b.rz.at[part, k - 1], b.sem.at[part, 4], b.sem.at[part, 5], (to, gy))

    def rs_finish(b, part, out):
        take(b.sem.at[part, 5], b.rz.at[part])
        total = b.zb[part, gx].astype(f32)
        for k in range(gxn - 1):
            total = total + b.rz[part, k].astype(f32)
        taps = 9 // s.nch
        for t in range(taps):
            at = 2 * w * t
            out[part * taps + t] = jnp.concatenate([total[at : at + w], total[at + w : at + 2 * w]], axis=1)

    def rs_drain(b):
        for part in range(s.nch):
            take(b.sem.at[part, 0], b.rc.at[part])
            take(b.sem.at[part, 2], b.rp.at[part])
            take(b.sem.at[part, 4], b.rz.at[part])

    def rs_buffers(number):
        names = ("rsb", "rc", "pb", "rp", "zb", "rz")
        b = types.SimpleNamespace(**{n: getattr(r, n + number) for n in names})
        b.sem = getattr(r, "rs_sem" + number)
        return b

    rs1, rs2 = rs_buffers("1"), rs_buffers("2")

    def local_stats(field, out):
        pivot = field[0:1, :]

        def one(i, carry):
            d = jnp.where(inside, field[rows_of(i), :] - pivot, 0.0).reshape(br // 8, 8, ch)
            return carry[0] + jnp.sum(d, axis=0), carry[1] + jnp.sum(d * d, axis=0)

        zero = jnp.zeros((8, ch), f32)
        first, second = lax.fori_loop(0, s.side, one, (zero, zero))
        n = float(nb * s.cells)
        first = jnp.sum(first, axis=0, keepdims=True) / n
        second = jnp.sum(second, axis=0, keepdims=True) - n * first * first
        out[0:1, :] = pivot + first
        out[1:2, :] = second

    def global_stats(slots):
        v = slots[...]
        n = float(nb * s.cells)
        mean = jnp.sum(v[:, 0:1, :], axis=0) / s.n_dev
        d = v[:, 0:1, :] - mean
        spread_sum = jnp.sum(v[:, 1:2, :] + n * d * d, axis=0)
        return mean, lax.rsqrt(spread_sum / s.count + epsilon)

    n1 = s.nch
    for u in range(n1):
        g_start(u)
    for u in range(n1):
        g_forward(u)
    for u in range(n1, 2 * n1):
        g_start(u)
    r.xt[...] = jnp.transpose(r.x3[br : br + s.rows, ch : 2 * ch])
    for u in range(n1):
        g_cross(u)

    def conv_part(planes, weight, di, out):
        v = dot(planes[br * di : br * di + s.rows, :], weight[di])
        out[...] = v if di == 0 else out[...] + v

    def conv(planes, weight, out):
        v = dot(planes[0 : s.rows, :], weight[0])
        v = v + dot(planes[br : br + s.rows, :], weight[1])
        out[...] = v + dot(planes[2 * br : 2 * br + s.rows, :], weight[2])

    for part in range(n1):
        g_done(part)
        unpack(r.s1, part, r.wt1)
        if s.fast:
            conv_part(r.x3, r.wt1, part, r.h1)
    if not s.fast:
        conv(r.x3, r.wt1, r.h1)
    local_stats(r.h1, r.st1)
    x_send(0, r.st1, r.t1)

    for u in range(n1, 2 * n1):
        g_forward(u)
    g_start(2 * n1)
    unpack_small()

    def flip(weight, back):
        for di in range(3):
            for dj in range(3):
                tap = weight[2 - di, (2 - dj) * ch : (3 - dj) * ch, :]
                back[di, dj * ch : (dj + 1) * ch, :] = jnp.transpose(tap)

    for u in range(n1, 2 * n1):
        g_cross(u)
    g_forward(2 * n1)

    gain1, gain2 = r.pars[0:1, :], r.pars[1:2, :]
    shift1, shift2 = r.pars[2:3, :], r.pars[3:4, :]
    hc0, hc1 = r.pars[4:5, :], r.pars[5:6, :]

    x_wait(0, r.t1)
    mean1, inv1 = global_stats(r.t1)

    def act1(i, _):
        n = (r.h1[rows_of(i), :] - mean1) * (inv1 * gain1) + shift1
        a = gelu(n)
        store3(r.a3, i, jnp.where(inside, a, 0.0))
        return 0

    lax.fori_loop(0, s.side, act1, 0)
    for u in range(n1, 2 * n1):
        g_done(u)
        unpack(r.s2, u - n1, r.wt2)
    conv(r.a3, r.wt2, r.h2)
    local_stats(r.h2, r.st2)
    x_send(1, r.st2, r.t2)

    r.at[...] = jnp.transpose(r.a3[br : br + s.rows, ch : 2 * ch])
    flip(r.wt1, r.wb1)
    flip(r.wt2, r.wb2)

    def slope1(i, _):
        n = (r.h1[rows_of(i), :] - mean1) * (inv1 * gain1) + shift1
        r.back1[rows_of(i), :] = gelu_both(n)[1]
        return 0

    lax.fori_loop(0, s.side, slope1, 0)
    g_cross(2 * n1)
    g_done(2 * n1)
    at = iota((s.line, 1), 0)
    i_of = divided(at, wide, s.line)
    j_of = at - i_of * wide
    used = (i_of < s.side) & (j_of < s.side)
    wide_slots = s.n_dev * s.rp
    shard_rows = iota((s.line, wide_slots), 1)
    dense_all = r.sd[...].reshape(wide_slots, s.mp)
    for k in range(2):
        source = k * s.cells + i_of * s.side + j_of
        if k == 0:
            source = jnp.where(at == s.side, s.head_in, source)
            wanted = used | (at == s.side)
        else:
            wanted = used
        source = jnp.where(wanted, source, 0)
        shard = divided(source, s.rsh, 1024)
        place = jnp.where(wanted, shard * s.rp + (source - shard * s.rsh), -1)
        pick = (shard_rows == place).astype(f32).astype(bf16)
        r.dk[k] = dot(pick, dense_all).astype(bf16)
    row, col = iota((s.long, s.line), 0), iota((s.long, s.line), 1)
    r.expand[...] = (col == lax.shift_right_logical(row, 2)).astype(f32).astype(bf16)
    r.out_r[s.rows :, :] = jnp.zeros((s.long - s.rows, ch), bf16)
    r.dp_full[...] = jnp.zeros_like(r.dp_full)
    r.hc_full[...] = jnp.zeros_like(r.hc_full)
    row = iota((16, ch), 0)
    both = jnp.where(row < nb, hc0, jnp.where(row < 2 * nb, hc1, 0.0))
    r.hc_full[0:16, :] = both.astype(bf16)
    hc_rows = jnp.where(row == 0, hc0, jnp.where(row == 1, hc1, 0.0)).astype(bf16)
    fetch_cot.wait()

    x_wait(1, r.t2)
    mean2, inv2 = global_stats(r.t2)

    def act2(i, _):
        at = rows_of(i)
        xin = r.x3[pl.ds(pl.multiple_of((i + 1) * br, 16), br), ch : 2 * ch].astype(f32)
        z = xin + ((r.h2[at, :] - mean2) * (inv2 * gain2) + shift2)
        r.dz[at, :] = z
        a = jnp.where(inside, gelu(z), 0.0)
        r.out_r[at, :] = a.astype(bf16)
        r.out_v[i] = to_board(a)
        return 0

    lax.fori_loop(0, s.side, act2, 0)
    put_out = pltpu.make_async_copy(r.out_v, r.out, r.local_sem.at[2])
    put_out.start()
    p_long = dot_nt(hc_rows, r.out_r[...])[0:8]
    lane = iota((8, s.long), 1)
    lane_j = lane - divided(lane, br, s.long) * br
    valid_long = (lane_j < nb * s.side) & (lane < s.rows)
    row1, lane1 = iota((8, lanes), 0), iota((8, lanes), 1)

    def by_head(v):
        a = v[0:1] + v[1:2] + v[2:3] + v[3:4]
        b = v[4:5] + v[5:6] + v[6:7] + v[7:8]
        return jnp.where(iota(v.shape, 0) < nb, a, b)

    n_local = float(nb * s.cells)
    mean_row = jnp.sum(jnp.where(valid_long, p_long, 0.0), axis=1, keepdims=True) / n_local
    dev = jnp.where(valid_long, p_long - mean_row, 0.0)
    square_row = jnp.sum(dev * dev, axis=1, keepdims=True)
    lane3 = iota((1, lanes), 1)
    means = jnp.where(lane3 < 32, mean_row[0:1], mean_row[1:2])
    r.st3[...] = jnp.where(lane3 < 64, means, jnp.where(lane3 < 96, square_row[0:1], square_row[1:2]))
    x_send(2, r.st3, r.t3)

    def slope2(i, _):
        r.dz[rows_of(i), :] = gelu_both(r.dz[rows_of(i), :])[1]
        return 0

    lax.fori_loop(0, s.side, slope2, 0)
    row = iota((8, s.long), 0)
    wanted = (lane & (nb - 1)) == (row & (nb - 1))
    rest = jnp.where(wanted, jnp.where(row < nb, p_long[0:1], p_long[1:2]), 0.0)
    parts = []
    for _ in range(3):
        part = rest.astype(bf16).astype(f32)
        parts.append(part)
        rest = rest - part
    parts = jnp.concatenate(parts + [jnp.zeros_like(rest)], axis=0).astype(bf16)
    p8 = dot(parts, r.expand[...])
    p8 = p8[0:8] + p8[8:16] + p8[16:24]
    row = iota((8, s.line), 0)
    lane = iota((8, s.line), 1)
    lane_i = divided(lane, wide, s.line)
    valid = (lane_i < s.side) & (lane - lane_i * wide < s.side)
    first_head = row < nb

    x_wait(2, r.t3)
    v = r.t3[...]
    mean_k = jnp.sum(v, axis=0) / float(s.n_dev)
    dev = v - mean_k
    squares = jnp.sum(jnp.where(lane3 < 64, n_local * dev * dev, v), axis=0)

    def of_head(v, at):
        return jnp.where(iota((8, 1), 0) < nb, v[:, at : at + 1], v[:, at + 32 : at + 33])

    mean_p = of_head(mean_k, 0)
    squares = of_head(squares, 0) + of_head(squares, 64)
    inv_p = lax.rsqrt(squares / s.count + epsilon)
    gain_p = jnp.where(iota((8, 1), 0) < nb, r.hng[0], r.hng[1])
    shift_p = jnp.where(iota((8, 1), 0) < nb, r.hns[0], r.hns[1])
    xhat_p = (p8 - mean_p) * inv_p
    feature, back_p = gelu_both(xhat_p * gain_p + shift_p)
    flat = jnp.where(valid, feature, 0.0).astype(bf16)
    one_lane = first_head & (lane == s.side)
    flat_f = flat.astype(f32)
    lhs0 = jnp.where(one_lane, 1.0, jnp.where(first_head, flat_f, 0.0))
    lhs1 = jnp.where(first_head, 0.0, flat_f)
    pad8 = jnp.zeros((8, s.line), f32)

    def tall(v):
        return jnp.concatenate([v, pad8[:, : v.shape[1]]], axis=0).astype(bf16)

    half = (dot(tall(lhs0), r.dk[0]) + dot(tall(lhs1), r.dk[1]))[0:8]
    logits = half + pltpu.roll(half, nb, 0)
    move = iota((8, s.mp), 1)
    r.legal_v[...] = jnp.zeros_like(r.legal_v)
    r.legal_v[0:nb, 0 : s.moves] = r.legal[...]
    r.legal_v[nb : 2 * nb, 0 : s.moves] = r.legal[...]
    masked = jnp.where(r.legal_v[...] == 1, logits, negative_fill)
    top = jnp.max(masked, axis=1, keepdims=True)
    terms = jnp.exp(masked - top)
    total = jnp.sum(terms, axis=1, keepdims=True)
    row_b = iota((8, 1), 0) & (nb - 1)
    target = jnp.where(
        row_b < 2,
        jnp.where(row_b == 0, r.target[0], r.target[1]),
        jnp.where(row_b == 2, r.target[2], r.target[3]),
    )
    chosen = move == target
    picked = jnp.sum(jnp.where(chosen, logits, 0.0), axis=1, keepdims=True)
    ce = top + jnp.log(total) - picked
    dl = (terms / total - chosen.astype(f32)).astype(bf16).astype(f32)
    first_move = iota((8, s.mp), 0) < nb
    dq = dot_nt(tall(jnp.where(first_move, dl, 0.0)), r.dk[0]) + dot_nt(
        tall(jnp.where(first_move, 0.0, dl)), r.dk[1]
    )
    dnh = jnp.where(valid, dq[0:8] * back_p, 0.0)
    gain_row = jnp.sum(dnh * xhat_p, axis=1, keepdims=True)
    shift_row = jnp.sum(dnh, axis=1, keepdims=True)
    r.st4[...] = jnp.where(lane1 < 32, gain_row, jnp.where(lane1 < 64, shift_row, ce))
    x_send(3, r.st4, r.t4)
    r.fd_own[...] = jnp.zeros_like(r.fd_own)
    r.fd_own[0:8, :] = flat_f
    r.fd_own[8:16, 0 : s.mp] = dl
    r.fd[gx, q, c] = r.fd_own[...].astype(bf16)
    g_start(2 * n1 + 1)
    x_wait(3, r.t4)
    sums = by_head(jnp.sum(r.t4[...], axis=0))
    gain_sum, shift_sum = sums[:, 0:1], sums[:, 32:33]
    r.loss[...] = sums[0:1, 64:65] / float(nb * s.n_dev)
    pair = jnp.where(iota((1, lanes), 1) == 0, sums[0:1, :], sums[4:5, :])
    pair_gain = jnp.where(iota((1, lanes), 1) == 0, sums[0:1, 0:1], sums[4:5, 0:1])
    pair_shift = jnp.where(iota((1, lanes), 1) == 0, sums[0:1, 32:33], sums[4:5, 32:33])
    r.hng_grad[0:1, :] = pair_gain[:, 0:2]
    r.hng_grad[1:2, :] = pair_shift[:, 0:2]
    dp = gain_p * inv_p * (dnh - (shift_sum + xhat_p * gain_sum) / s.count)
    dp = jnp.where(valid, dp, 0.0)
    r.dp_full[0:16, :] = tall(dp)

    spread_p = dot_nt(r.expand[0 : s.rows, :], r.dp_full[...])
    row, col = iota((s.rows, lanes), 0), iota((s.rows, lanes), 1)
    spread_p = jnp.where((row & (nb - 1)) == (col & (nb - 1)), spread_p, 0.0).astype(bf16)
    r.spread[...] = spread_p
    r.up[...] = dot(spread_p, r.hc_full[...])

    def sums_back(field, xhat, carry):
        f = field.reshape(br // 8, 8, ch)
        g = (field * xhat).reshape(br // 8, 8, ch)
        return carry[0] + jnp.sum(g, axis=0), carry[1] + jnp.sum(f, axis=0)

    def back2(i, carry):
        at = rows_of(i)
        dz = (from_board(r.cot_v[i]) + r.up[at, :]) * r.dz[at, :]
        dz = jnp.where(inside, dz, 0.0)
        r.dz[at, :] = dz
        return sums_back(dz, (r.h2[at, :] - mean2) * inv2, carry)

    zero = jnp.zeros((8, ch), f32)
    g2, s2 = lax.fori_loop(0, s.side, back2, (zero, zero))
    r.st5[0:1, :] = jnp.sum(g2, axis=0, keepdims=True)
    r.st5[1:2, :] = jnp.sum(s2, axis=0, keepdims=True)
    x_send(4, r.st5, r.t5)
    g_forward(2 * n1 + 1)

    head_grad = lax.dot_general(
        r.spread[...], r.out_r[0 : s.rows, :], (((0,), (0,)), ((), ())), preferred_element_type=f32
    )
    r.st6[2:3, :] = head_grad[0:1] + head_grad[1:2] + head_grad[2:3] + head_grad[3:4]
    r.st6[3:4, :] = head_grad[4:5] + head_grad[5:6] + head_grad[6:7] + head_grad[7:8]
    x_wait(4, r.t5)
    t5 = jnp.sum(r.t5[...], axis=0)
    g2s, s2s = t5[0:1], t5[1:2]

    def to_field2(i, _):
        at = rows_of(i)
        xhat = (r.h2[at, :] - mean2) * inv2
        d = (gain2 * inv2) * (r.dz[at, :] - (s2s + xhat * g2s) * (1.0 / s.count))
        store3(r.d3, i, jnp.where(inside, d, 0.0))
        return 0

    lax.fori_loop(0, s.side, to_field2, 0)

    def wgrad(planes_t, di):
        start = 2 * br - br * di
        return dot(planes_t[...], r.d3[start : start + s.rows, :])

    conv(r.d3, r.wb2, r.h2)
    g_cross(2 * n1 + 1)

    def back1(i, carry):
        at = rows_of(i)
        dn = jnp.where(inside, r.h2[at, :] * r.back1[at, :], 0.0)
        r.h2[at, :] = dn
        return sums_back(dn, (r.h1[at, :] - mean1) * inv1, carry)

    g1, s1 = lax.fori_loop(0, s.side, back1, (zero, zero))
    r.st6[0:1, :] = jnp.sum(g1, axis=0, keepdims=True)
    r.st6[1:2, :] = jnp.sum(s1, axis=0, keepdims=True)
    x_send(5, r.st6, r.t6)
    for di in range(3):
        rs_fill(di, wgrad(r.at, di), rs2)
        if s.fast:
            rs_cross(rs2, di)
    rs_fill_rest(rs2)
    if not s.fast:
        rs_cross(rs2, 0)
    for part in range(s.nch):
        rs_plane(rs2, part)
    x_wait(5, r.t6)
    t6 = jnp.sum(r.t6[...], axis=0)
    g1s, s1s = t6[0:1], t6[1:2]

    def to_field1(i, _):
        at = rows_of(i)
        xhat = (r.h1[at, :] - mean1) * inv1
        d = (gain1 * inv1) * (r.h2[at, :] - (s1s + xhat * g1s) * (1.0 / s.count))
        store3(r.d3, i, jnp.where(inside, d, 0.0))
        return 0

    lax.fori_loop(0, s.side, to_field1, 0)
    for di in range(3):
        rs_fill(di, wgrad(r.xt, di), rs1)
        if s.fast:
            rs_cross(rs1, di)
    rs_fill_rest(rs1)
    if not s.fast:
        rs_cross(rs1, 0)
    for part in range(s.nch):
        rs_line(rs2, part)
    for part in range(s.nch):
        rs_plane(rs1, part)
    conv(r.d3, r.wb1, r.h1)
    for part in range(s.nch):
        rs_line(rs1, part)

    def result(i, _):
        at = rows_of(i)
        r.in_grad_v[i] = to_board(r.dz[at, :] + r.h1[at, :])
        return 0

    lax.fori_loop(0, s.side, result, 0)
    put_in_grad = pltpu.make_async_copy(r.in_grad_v, r.in_grad, r.local_sem.at[3])
    put_in_grad.start()
    shares = jnp.concatenate([g1s, g2s, s1s, s2s, t6[2:4], jnp.zeros((2, ch), f32)], axis=0)
    r.share[...] = pltpu.roll(shares, lax.rem(ch - w * me, ch), 1)
    r.gains_grad[...] = r.share[0:2, 0:w]
    r.shifts_grad[...] = r.share[2:4, 0:w]
    r.hc_grad[...] = r.share[4:6, 0:w]

    g_done(2 * n1 + 1)
    fd = r.fd[...].astype(f32).reshape(s.n_dev, 16, s.line)
    features = fd[:, 0:8, :].reshape(8 * s.n_dev, s.line).astype(bf16)
    dls = fd[:, 8:16, 0 : s.mp].reshape(8 * s.n_dev, s.mp).astype(bf16)
    t = iota((s.rp, 1), 0)
    source = s.rsh * me + t
    mine = (t < s.rsh) & (source < s.head_in)
    col = iota((s.rp, s.line), 1)
    col8 = iota((s.rp, 8 * s.n_dev), 1) & 7
    own = jnp.where((t < s.rsh) & (source == s.head_in) & (col8 < nb), 1.0, 0.0)
    for k in range(2):
        in_k = mine & (source >= k * s.cells) & (source < (k + 1) * s.cells)
        cell = jnp.where(in_k, source - k * s.cells, 0)
        cell_i = divided(cell, s.side, s.cells)
        place = jnp.where(in_k, cell_i * wide + (cell - cell_i * s.side), -1)
        pick = (col == place).astype(f32).astype(bf16)
        rows_k = dot_nt(pick, features)
        own = own + jnp.where((col8 >= nb) if k else (col8 < nb), rows_k, 0.0)
    grad = dot(own.astype(bf16), dls)
    r.dense_v[...] = grad
    r.dense_grad[...] = r.dense_v[0 : s.rsh, 0 : s.moves]

    for part in range(s.nch):
        rs_finish(rs2, part, r.c2_grad)
    for part in range(s.nch):
        rs_finish(rs1, part, r.c1_grad)

    for u in range(len(units)):
        g_drain(u)
    for number, slots in enumerate((r.t1, r.t2, r.t3, r.t4, r.t5, r.t6)):
        x_drain(number, slots)
    rs_drain(rs1)
    rs_drain(rs2)
    put_out.wait()
    put_in_grad.wait()


def place(n, *refs):
    sources, targets, held, (came, went) = refs[:n], refs[n : 2 * n], refs[2 * n : 3 * n], refs[3 * n :]
    fetch = [pltpu.make_async_copy(sources[i], held[i], came.at[i]) for i in range(n)]
    put = [pltpu.make_async_copy(held[i], targets[i], went.at[i]) for i in range(n)]
    for copy in fetch:
        copy.start()
    for i in range(n):
        fetch[i].wait()
        put[i].start()
    for copy in put:
        copy.wait()


def body(x, w1, w2, gains, shifts, hc, hng, hns, dense, legal, target, cot):
    x, cot = (jnp.transpose(v, (1, 2, 0, 3)) for v in (x, cot))
    s = sizes_of(lax.axis_size("gx"), lax.axis_size("gy"), x, w1, dense, legal.shape[1])
    vmem, smem, hbm = pltpu.VMEM, pltpu.SMEM, pl.ANY
    inputs = dict(
        x=(x, hbm), w1=(w1, vmem), w2=(w2, vmem), gains=(gains, vmem), shifts=(shifts, vmem), hc=(hc, vmem),
        hng=(hng, smem), hns=(hns, smem), dense=(dense, vmem), legal=(legal, vmem), target=(target, smem), cot=(cot, hbm),
    )
    outputs = dict(
        out=(x.shape, bf16), loss=((1, 1), f32), in_grad=(x.shape, bf16), c1_grad=(w1.shape, f32),
        c2_grad=(w2.shape, f32), gains_grad=(gains.shape, f32), shifts_grad=(shifts.shape, f32),
        hc_grad=(hc.shape, f32), hng_grad=((2, 2), f32), dense_grad=(dense.shape, f32),
    )
    gxn, qn, n, ch = s.gx_n, s.q_n, s.n_dev, s.ch
    field = pltpu.VMEM((s.rows, ch), f32)
    boards = pltpu.VMEM((s.side, s.wide, s.nb, ch), bf16)
    planes = pltpu.VMEM((s.padded, 3 * ch), bf16)
    turned = pltpu.VMEM((ch, s.rows), bf16)
    weight = pltpu.VMEM((3, 3 * ch, ch), bf16)
    two = pltpu.VMEM((2, ch), f32)
    four = pltpu.VMEM((4, ch), f32)
    tile = pltpu.VMEM((8, lanes), f32)
    dma = pltpu.SemaphoreType.DMA
    scratch = dict(
        local_sem=dma((4,)), g_sem=dma((2 * s.nch + 2, 5 + gxn)), x_sem=dma((6, 2)),
        rs_sem1=dma((s.nch, 6)), rs_sem2=dma((s.nch, 6)),
        x_v=boards, cot_v=boards, out_v=pltpu.VMEM(x.shape, bf16), in_grad_v=pltpu.VMEM(x.shape, bf16),
        stage=pltpu.VMEM((s.blk1, lanes), f32), small=pltpu.VMEM((8, lanes), f32),
        s1=pltpu.VMEM((gxn, qn, 2, s.blk1, lanes), bf16), s2=pltpu.VMEM((gxn, qn, 2, s.blk, lanes), bf16),
        sd=pltpu.VMEM((gxn, qn, 2, s.rp, s.mp), bf16), dense_v=pltpu.VMEM((s.rp, s.mp), f32),
        x3=planes, a3=planes, d3=planes, out_r=pltpu.VMEM((s.long, ch), bf16), spread=pltpu.VMEM((s.rows, lanes), bf16),
        xt=turned, at=turned, wt1=weight, wt2=weight, wb1=weight, wb2=weight,
        pars=pltpu.VMEM((8, ch), f32), h1=field, h2=field, dz=field, back1=field, up=field,
        st1=two, t1=pltpu.VMEM((n, 2, ch), f32), st2=two, t2=pltpu.VMEM((n, 2, ch), f32),
        st3=pltpu.VMEM((1, lanes), f32), t3=pltpu.VMEM((n, 1, lanes), f32), st4=tile, t4=pltpu.VMEM((n, 8, lanes), f32),
        st5=two, t5=pltpu.VMEM((n, 2, ch), f32), st6=four, t6=pltpu.VMEM((n, 4, ch), f32),
        fd_own=pltpu.VMEM((16, s.line), f32), fd=pltpu.VMEM((gxn, qn, 2, 16, s.line), bf16),
        dk=pltpu.VMEM((2, s.line, s.mp), bf16), expand=pltpu.VMEM((s.long, s.line), bf16),
        dp_full=pltpu.VMEM((lanes, s.line), bf16), hc_full=pltpu.VMEM((lanes, ch), bf16),
        legal_v=pltpu.VMEM((8, s.mp), jnp.int32), share=pltpu.VMEM((8, ch), f32),
    )
    if not s.fast:
        scratch["flat"] = pltpu.VMEM((9, ch, ch), f32)
        scratch["eight"] = pltpu.VMEM((9, 8, ch), f32)
    for number in ("1", "2"):
        scratch["rsb" + number] = pltpu.VMEM((s.nch, 2, gxn, qn, s.crows, lanes), bf16)
        scratch["rc" + number] = pltpu.VMEM((s.nch, gxn, qn, s.crows, lanes), bf16)
        scratch["pb" + number] = pltpu.VMEM((s.nch, qn, gxn, s.crows, lanes), bf16)
        scratch["rp" + number] = pltpu.VMEM((s.nch, qn - 1, gxn, s.crows, lanes), bf16)
        scratch["zb" + number] = pltpu.VMEM((s.nch, gxn, s.crows, lanes), bf16)
        scratch["rz" + number] = pltpu.VMEM((s.nch, gxn - 1, s.crows, lanes), bf16)
    run = pl.pallas_call(
        functools.partial(kernel, s, tuple(inputs), tuple(outputs), tuple(scratch)),
        out_shape=[jax.ShapeDtypeStruct(shape, kind) for shape, kind in outputs.values()],
        in_specs=[pl.BlockSpec(memory_space=space) for _, space in inputs.values()],
        out_specs=[pl.BlockSpec(memory_space=hbm if n in ("out", "in_grad") else vmem) for n in outputs],
        scratch_shapes=list(scratch.values()),
        compiler_params=pltpu.CompilerParams(
            collective_id=0, has_side_effects=True, vmem_limit_bytes=60 * 1024 * 1024
        ),
        cost_estimate=pl.CostEstimate(flops=10_500_000_000, bytes_accessed=8_000_000, transcendentals=800_000),
        name="tower",
    )
    results = run(*(value for value, _ in inputs.values()))
    results = pl.pallas_call(
        functools.partial(place, len(results)),
        out_shape=[jax.ShapeDtypeStruct(v.shape, v.dtype) for v in results],
        in_specs=[pl.BlockSpec(memory_space=hbm) for _ in results],
        out_specs=[pl.BlockSpec(memory_space=hbm) for _ in results],
        scratch_shapes=[pltpu.VMEM(v.shape, v.dtype) for v in results] + [dma((len(results),))] * 2,
        name="place",
    )(*results)
    out, loss, in_grad, *rest = results
    out, in_grad = (jnp.transpose(v, (2, 0, 1, 3)) for v in (out, in_grad))
    return (out, loss.reshape(()), in_grad, *rest)


def solution(mesh):
    both = ("gx", "gy")
    board = P(both, None, None, None)
    kernels = P(None, both, None)
    pairs = P(None, both)
    return jax.shard_map(
        body,
        mesh=mesh,
        in_specs=(
            board, kernels, kernels, pairs, pairs, pairs, P(), P(), P(both, None), P(both, None), P(both), board,
        ),
        out_specs=(board, P(), board, kernels, kernels, pairs, pairs, pairs, P(), P(both, None)),
        check_vma=False,
    )
```

```python
import functools
import types

import jax
import jax.numpy as jnp
from jax import lax
from jax.experimental import pallas as pl
from jax.experimental.pallas import tpu as pltpu
from jax.sharding import PartitionSpec as P

MESH = pl.DeviceIdType.MESH
f32 = jnp.float32
bf16 = jnp.bfloat16
epsilon = 1e-05
negative_fill = -1e30
root = 0.7978845608028654
cube = 0.044715
lanes = 128


def up_to(value, unit):
    return -(-value // unit) * unit


def divided(values, divisor, limit):
    for shift in range(16, 24):
        factor = -(-(1 << shift) // divisor)
        if all((n * factor) >> shift == n // divisor and n * factor < 2**31 for n in range(limit)):
            return lax.shift_right_logical(values * factor, jnp.int32(shift))
    raise ValueError("no factor")


def iota(shape, axis):
    return lax.broadcasted_iota(jnp.int32, shape, axis)


def gelu_both(v):
    square = v * v
    slope = jnp.tanh(v * (root + (root * cube) * square))
    half = 0.5 + 0.5 * slope
    back = half + (0.5 * v) * (1.0 - slope * slope) * (root + (3.0 * root * cube) * square)
    return v * half, back


def gelu(v):
    half = 0.5 * v
    return half + half * jnp.tanh(v * (root + (root * cube) * (v * v)))


def dot(left, right):
    return jnp.dot(left, right, preferred_element_type=f32)


def dot_nt(left, right):
    return lax.dot_general(left, right, (((1,), (1,)), ((), ())), preferred_element_type=f32)


def sizes_of(gx_n, gy_n, x, w1, dense, moves):
    s = types.SimpleNamespace()
    s.gx_n, s.gy_n, s.q_n, s.n_dev = gx_n, gy_n, gy_n // 2, gx_n * gy_n
    s.side, s.nb, s.ch = x.shape[0], x.shape[2], x.shape[3]
    s.w = w1.shape[1]
    s.wide = s.side + 1
    s.br = s.wide * s.nb
    s.rows = s.side * s.br
    s.padded = s.rows + 2 * s.br
    s.line = up_to(s.side * s.wide, lanes)
    s.long = up_to(s.rows, lanes)
    s.cells = s.side * s.side
    s.moves = moves
    s.mp = up_to(moves, lanes)
    s.rsh = dense.shape[0]
    s.rp = up_to(s.rsh, 16)
    s.head_in = 2 * s.cells
    s.blk = up_to(18 * s.w, 16)
    s.blk1 = up_to(19 * s.w, 16)
    s.fast = s.w == 8
    s.nch = 3 if s.fast else 1
    s.crows = s.blk // s.nch
    s.count = float(s.nb * s.cells * s.n_dev)
    assert s.nb == 4 and s.br % 16 == 0 and 8 % s.w == 0
    assert gx_n & (gx_n - 1) == 0 and gy_n & (gy_n - 1) == 0 and gy_n > 1
    return s


def kernel(s, in_names, out_names, scratch_names, *refs):
    r = types.SimpleNamespace(**dict(zip(in_names + out_names + scratch_names, refs)))
    gx, gy = lax.axis_index("gx"), lax.axis_index("gy")
    q, c = lax.div(gy, 2), lax.rem(gy, 2)
    me = gx * s.gy_n + gy
    other = (gx, gy + 1 - 2 * c)
    gxn, qn, nb, br, wide, ch = s.gx_n, s.q_n, s.nb, s.br, s.wide, s.ch

    def z_peer(k):
        return gx ^ k

    def q_peer(j):
        return q ^ j

    def send(src, dst, out_sem, in_sem, device):
        pltpu.make_async_remote_copy(
            src_ref=src, dst_ref=dst, send_sem=out_sem, recv_sem=in_sem, device_id=device, device_id_type=MESH
        ).start()

    def take(sem, ref):
        pltpu.make_async_copy(ref, ref, sem).wait()

    barrier = pltpu.get_barrier_semaphore()
    partners = [(z_peer(k), gy) for k in range(1, gxn)]
    partners += [(gx, 2 * q_peer(j) + c) for j in range(1, qn)]
    partners += [other]
    for p in partners:
        pl.semaphore_signal(barrier, inc=1, device_id=p, device_id_type=MESH)
    names = ("x", "w1", "w2", "gains", "shifts", "hc", "dense", "cot", "legal", "hng", "hns", "target")
    fetch = {}
    for n, name in enumerate(names):
        held = getattr(r, name + "_v")
        held = held.at[:, pl.ds(0, s.side)] if name in ("x", "cot") else held
        fetch[name] = pltpu.make_async_copy(getattr(r, name), held, r.local_sem.at[n])
        fetch[name].start()
    for fields in (r.x_v, r.cot_v):
        fields[:, s.side] = jnp.zeros((s.side, nb, ch), bf16)

    w = s.w

    def stage(weight):
        r.stage[...] = jnp.zeros_like(r.stage)
        for t in range(9):
            v = weight[t].astype(f32)
            r.stage[2 * w * t : 2 * w * t + w, :] = v[:, :lanes]
            r.stage[2 * w * t + w : 2 * w * t + 2 * w, :] = v[:, lanes:]

    def stage_all():
        for name in names[1:7]:
            fetch[name].wait()
        r.small[...] = jnp.zeros_like(r.small)
        r.small[0:2, 0:w] = r.gains_v[...].astype(f32)
        r.small[2:4, 0:w] = r.shifts_v[...].astype(f32)
        r.small[4:6, 0:w] = r.hc_v[...].astype(f32)
        stage(r.w1_v)
        r.stage[18 * w : 19 * w, 0:8] = jnp.transpose(r.small[...])[0:w, :]
        r.s1[gx, q, c] = r.stage[...].astype(bf16)
        stage(r.w2_v)
        r.s2[gx, q, c] = r.stage[0 : s.blk, :].astype(bf16)
        r.dense_f[...] = jnp.zeros_like(r.dense_f)
        r.dense_f[0 : s.rsh, 0 : s.moves] = r.dense_v[...].astype(f32)
        r.sd[gx, q, c] = r.dense_f[...].astype(bf16)

    for planes in (r.x3, r.a3, r.d3):
        planes[0:br, :] = jnp.zeros((br, 3 * ch), bf16)
        planes[s.padded - br :, :] = jnp.zeros((br, 3 * ch), bf16)
    inside = iota((br, ch), 0) < nb * s.side

    def store3(planes, i, block):
        at = pl.ds(pl.multiple_of((i + 1) * br, 16), br)
        planes[at, 0:ch] = pltpu.roll(block, nb, 0).astype(bf16)
        planes[at, ch : 2 * ch] = block.astype(bf16)
        planes[at, 2 * ch :] = pltpu.roll(block, br - nb, 0).astype(bf16)

    def rows_of(i):
        return pl.ds(pl.multiple_of(i * br, 16), br)

    def from_board(block):
        return block.astype(f32).reshape(br, ch)

    def to_board(block):
        return block.reshape(wide, nb, ch)[0 : s.side].astype(bf16)

    def x_rows(i, _):
        store3(r.x3, i, from_board(r.x_v[i]))
        return 0

    fetch["x"].wait()
    lax.fori_loop(0, s.side, x_rows, 0)
    stage_all()

    pl.semaphore_wait(barrier, len(partners))

    def span(unit):
        store, part = unit
        if store is r.sd or store is r.fd:
            return pl.ds(0, store.shape[3])
        whole = s.blk1 if store is r.s1 else s.blk
        if s.nch == 1:
            return pl.ds(0, whole)
        start = part * s.crows
        return pl.ds(start, whole - start if part == s.nch - 1 else s.crows)

    units = [(r.s1, p) for p in range(s.nch)] + [(r.s2, p) for p in range(s.nch)] + [(r.sd, 0), (r.fd, 0)]

    def g_start(u):
        store, at = units[u][0], span(units[u])
        own = store.at[gx, q, c, at]
        for k in range(1, gxn):
            send(own, own, r.g_sem.at[u, 0], r.g_sem.at[u, 5 + k], (z_peer(k), gy))
        for j in range(qn - 1, 0, -1):
            send(own, own, r.g_sem.at[u, 1], r.g_sem.at[u, 4], (gx, 2 * q_peer(j) + c))

    def g_forward(u):
        store, at = units[u][0], span(units[u])
        for k in range(1, gxn):
            block = store.at[z_peer(k), q, c, at]
            take(r.g_sem.at[u, 5 + k], block)
            for j in range(qn - 1, 0, -1):
                send(block, block, r.g_sem.at[u, 2], r.g_sem.at[u, 4], (gx, 2 * q_peer(j) + c))

    def g_cross(u):
        store, at = units[u][0], span(units[u])
        take(r.g_sem.at[u, 4], store.at[:, pl.ds(0, qn - 1), 0, at])
        block = store.at[:, :, c, at]
        send(block, block, r.g_sem.at[u, 3], r.g_sem.at[u, 5], other)

    def g_done(u):
        store, at = units[u][0], span(units[u])
        take(r.g_sem.at[u, 5], store.at[:, :, 0, at])

    def g_drain(u):
        store, at = units[u][0], span(units[u])
        take(r.g_sem.at[u, 0], store.at[pl.ds(0, gxn - 1), 0, 0, at])
        take(r.g_sem.at[u, 1], store.at[0, pl.ds(0, qn - 1), 0, at])
        take(r.g_sem.at[u, 2], store.at[pl.ds(0, gxn - 1), pl.ds(0, qn - 1), 0, at])
        take(r.g_sem.at[u, 3], store.at[:, :, 0, at])

    def shard_of(store, d):
        return store[lax.div(d, s.gy_n), lax.div(lax.rem(d, s.gy_n), 2), lax.rem(d, 2)]

    def unpack(store, part, weight):
        if s.fast:
            for dj in range(3):
                at = 16 * (3 * part + dj)
                v = store[:, :, :, at : at + 16, :].astype(f32).reshape(s.n_dev, 16, lanes)
                low = v[:, 0:8, :].reshape(ch, lanes)
                high = v[:, 8:16, :].reshape(ch, lanes)
                weight[part, dj * ch : (dj + 1) * ch, :] = jnp.concatenate([low, high], axis=1).astype(bf16)
            return

        def one(g, _):
            for e in range(8 // w):
                r.stage[0 : s.blk, :] = shard_of(store, g * (8 // w) + e)[0 : s.blk].astype(f32)
                for t in range(9):
                    r.eight[t, w * e : w * e + w, 0:lanes] = r.stage[2 * w * t : 2 * w * t + w, :]
                    r.eight[t, w * e : w * e + w, lanes:] = r.stage[2 * w * t + w : 2 * w * t + 2 * w, :]
            for t in range(9):
                r.flat[t, pl.ds(pl.multiple_of(8 * g, 8), 8), :] = r.eight[t]
            return 0

        lax.fori_loop(0, ch // 8, one, 0)
        for t in range(9):
            weight[t // 3, (t % 3) * ch : (t % 3 + 1) * ch, :] = r.flat[t].astype(bf16)

    def unpack_small():
        if s.fast:
            v = r.s1[:, :, :, 18 * w : 18 * w + 16, :].astype(f32).reshape(s.n_dev, 16, lanes)
            rows = v[:, 0:8, :].reshape(ch, lanes)
        else:

            def one(g, _):
                for e in range(8 // w):
                    r.stage[...] = shard_of(r.s1, g * (8 // w) + e).astype(f32)
                    r.eight[0, w * e : w * e + w, 0:lanes] = r.stage[18 * w : 19 * w, :]
                r.flat[0, pl.ds(pl.multiple_of(8 * g, 8), 8), :] = r.eight[0]
                return 0

            lax.fori_loop(0, ch // 8, one, 0)
            rows = r.flat[0, :, 0:lanes]
        r.pars[...] = jnp.transpose(rows)[0:8, :]

    def x_send(number, src, slots):
        def one(k):
            device = (gx ^ lax.div(k, s.gy_n), gy ^ lax.rem(k, s.gy_n))
            send(src, slots.at[me], r.x_sem.at[number, 0], r.x_sem.at[number, 1], device)

        if s.n_dev <= 64:
            hops = {k: k // s.gy_n + bin(k % s.gy_n // 2).count("1") for k in range(1, s.n_dev)}
            for k in sorted(hops, key=lambda k: (-hops[k], k)):
                send(
                    src, slots.at[me], r.x_sem.at[number, 0], r.x_sem.at[number, 1],
                    (gx ^ (k // s.gy_n), gy ^ (k % s.gy_n)),
                )
        else:
            lax.fori_loop(0, s.n_dev - 1, lambda n, _: (one(s.n_dev - 1 - n), 0)[1], 0)
        slots[me] = src[...]

    def x_wait(number, slots):
        take(r.x_sem.at[number, 1], slots.at[pl.ds(0, s.n_dev - 1)])

    def x_drain(number, slots):
        take(r.x_sem.at[number, 0], slots.at[pl.ds(0, s.n_dev - 1)])

    def plane_send(number, src, slots):
        for k in range(s.gy_n - 1, 0, -1):
            send(src, slots.at[gy], r.x_sem.at[number, 0], r.x_sem.at[number, 1], (gx, gy ^ k))
        slots[gy] = src[...]

    def line_send(number, src, slots):
        for k in range(gxn - 1, 0, -1):
            send(src, slots.at[gx], r.x_sem.at[number, 0], r.x_sem.at[number, 1], (gx ^ k, gy))
        slots[gx] = src[...]

    def group_wait(number, slots, way=1):
        take(r.x_sem.at[number, way], slots.at[pl.ds(0, slots.shape[0] - 1)])

    def rs_fill(part, grad, b):
        if s.fast:
            for dj in range(3):
                g = grad[:, (2 - dj) * ch : (3 - dj) * ch]
                low = g[:, :lanes].reshape(s.n_dev, 8, lanes)
                high = g[:, lanes:].reshape(s.n_dev, 8, lanes)
                v = jnp.concatenate([low, high], axis=1).astype(bf16).reshape(gxn, qn, 2, 16, lanes)
                for core in range(2):
                    b.rsb[part, core, :, :, 16 * dj : 16 * dj + 16, :] = v[:, :, core]
        else:
            for dj in range(3):
                r.flat[3 * part + dj] = grad[:, (2 - dj) * ch : (3 - dj) * ch]

    def rs_fill_rest(b):
        if s.fast:
            return
        r.stage[...] = jnp.zeros_like(r.stage)

        def one(g, _):
            for t in range(9):
                r.eight[t] = r.flat[t, pl.ds(pl.multiple_of(8 * g, 8), 8), :]
            for e in range(8 // w):
                d = g * (8 // w) + e
                for t in range(9):
                    v = r.eight[t, w * e : w * e + w, :]
                    r.stage[2 * w * t : 2 * w * t + w, :] = v[:, :lanes]
                    r.stage[2 * w * t + w : 2 * w * t + 2 * w, :] = v[:, lanes:]
                at = (0, lax.rem(d, 2), lax.div(d, s.gy_n), lax.div(lax.rem(d, s.gy_n), 2))
                b.rsb[at] = r.stage[0 : s.blk, :].astype(bf16)
            return 0

        lax.fori_loop(0, ch // 8, one, 0)

    def rs_cross(b, part):
        send(b.rsb.at[part, 1 - c], b.rc.at[part], b.sem.at[part, 0], b.sem.at[part, 1], other)

    def rs_plane(b, part):
        take(b.sem.at[part, 1], b.rc.at[part])
        for p in range(qn):
            total = b.rsb[part, c, :, p].astype(f32) + b.rc[part, :, p].astype(f32)
            b.pb[part, p] = total.astype(bf16)
        if s.nch > 1 and part == s.nch - 1:
            for k in range(gxn - 1, -1, -1):
                for j in range(qn - 1, -1, -1):
                    if k + j:
                        block = b.pb.at[part, q_peer(j), z_peer(k)]
                        device = (z_peer(k), 2 * q_peer(j) + c)
                        send(block, b.rd.at[k * qn + j - 1], b.sem.at[part, 2], b.sem.at[part, 3], device)
            return
        for j in range(1, qn):
            to = q_peer(j)
            send(b.pb.at[part, to], b.rp.at[part, j - 1], b.sem.at[part, 2], b.sem.at[part, 3], (gx, 2 * to + c))

    def rs_line(b, part):
        if s.nch > 1 and part == s.nch - 1:
            return
        take(b.sem.at[part, 3], b.rp.at[part])
        total = b.pb[part, q].astype(f32)
        for j in range(qn - 1):
            total = total + b.rp[part, j].astype(f32)
        b.zb[part] = total.astype(bf16)
        for k in range(1, gxn):
            to = z_peer(k)
            send(b.zb.at[part, to], b.rz.at[part, k - 1], b.sem.at[part, 4], b.sem.at[part, 5], (to, gy))

    def rs_finish(b, part, out):
        if s.nch > 1 and part == s.nch - 1:
            take(b.sem.at[part, 3], b.rd)
            total = b.pb[part, q, gx].astype(f32) + jnp.sum(b.rd[...].astype(f32), axis=0)
        else:
            take(b.sem.at[part, 5], b.rz.at[part])
            total = b.zb[part, gx].astype(f32)
            for k in range(gxn - 1):
                total = total + b.rz[part, k].astype(f32)
        taps = 9 // s.nch
        for t in range(taps):
            at = 2 * w * t
            out[part * taps + t] = jnp.concatenate([total[at : at + w], total[at + w : at + 2 * w]], axis=1)

    def rs_drain(b):
        for part in range(s.nch):
            take(b.sem.at[part, 0], b.rc.at[part])
            if s.nch > 1 and part == s.nch - 1:
                take(b.sem.at[part, 2], b.rd)
                continue
            take(b.sem.at[part, 2], b.rp.at[part])
            take(b.sem.at[part, 4], b.rz.at[part])

    def rs_buffers(number):
        names = ("rsb", "rc", "pb", "rp", "zb", "rz", "rd")
        b = types.SimpleNamespace(**{n: getattr(r, n + number) for n in names})
        b.sem = getattr(r, "rs_sem" + number)
        return b

    rs1, rs2 = rs_buffers("1"), rs_buffers("2")

    def local_stats(field, out):
        pivot = field[0:1, :]

        def one(i, carry):
            d = jnp.where(inside, field[rows_of(i), :] - pivot, 0.0).reshape(br // 8, 8, ch)
            return carry[0] + jnp.sum(d, axis=0), carry[1] + jnp.sum(d * d, axis=0)

        zero = jnp.zeros((8, ch), f32)
        first, second = lax.fori_loop(0, s.side, one, (zero, zero))
        n = float(nb * s.cells)
        first = jnp.sum(first, axis=0, keepdims=True) / n
        second = jnp.sum(second, axis=0, keepdims=True) - n * first * first
        out[0:1, :] = pivot + first
        out[1:2, :] = second

    def global_stats(slots):
        v = slots[...]
        n = float(nb * s.cells)
        mean = jnp.sum(v[:, 0:1, :], axis=0) / s.n_dev
        d = v[:, 0:1, :] - mean
        spread_sum = jnp.sum(v[:, 1:2, :] + n * d * d, axis=0)
        return mean, lax.rsqrt(spread_sum / s.count + epsilon)

    n1 = s.nch
    for u in range(n1):
        g_start(u)
    g_forward(0)
    for u in range(n1, 2 * n1):
        g_start(u)
    for u in range(1, 2 * n1):
        g_forward(u)
    g_start(2 * n1)
    row, col = iota((s.long, s.line), 0), iota((s.long, s.line), 1)
    r.expand[...] = (col == lax.shift_right_logical(row, 2)).astype(f32).astype(bf16)
    r.out_r[s.rows :, :] = jnp.zeros((s.long - s.rows, ch), bf16)
    r.vu[s.rows :, :] = jnp.zeros((s.long - s.rows, 2 * ch), bf16)
    r.xt[...] = jnp.transpose(r.x3[br : br + s.rows, ch : 2 * ch])
    for u in range(n1):
        g_cross(u)

    def conv_part(planes, weight, di, out):
        v = dot(planes[br * di : br * di + s.rows, :], weight[di])
        out[...] = v if di == 0 else out[...] + v

    def conv(planes, weight, out):
        v = dot(planes[0 : s.rows, :], weight[0])
        v = v + dot(planes[br : br + s.rows, :], weight[1])
        out[...] = v + dot(planes[2 * br : 2 * br + s.rows, :], weight[2])

    for part in range(n1):
        g_done(part)
        unpack(r.s1, part, r.wt1)
        if s.fast:
            conv_part(r.x3, r.wt1, part, r.h1)
    if not s.fast:
        conv(r.x3, r.wt1, r.h1)
    local_stats(r.h1, r.st1)
    x_send(0, r.st1, r.t1)

    g_forward(2 * n1)
    unpack_small()
    fetch["cot"].wait()

    def flip(weight, back):
        for di in range(3):
            for dj in range(3):
                tap = weight[2 - di, (2 - dj) * ch : (3 - dj) * ch, :]
                back[di, dj * ch : (dj + 1) * ch, :] = jnp.transpose(tap)

    for u in range(n1, 2 * n1):
        g_cross(u)
    flip(r.wt1, r.wb1)

    gain1, gain2 = r.pars[0:1, :], r.pars[1:2, :]
    shift1, shift2 = r.pars[2:3, :], r.pars[3:4, :]
    hc0, hc1 = r.pars[4:5, :], r.pars[5:6, :]

    x_wait(0, r.t1)
    mean1, inv1 = global_stats(r.t1)

    def act1(i, _):
        n = (r.h1[rows_of(i), :] - mean1) * (inv1 * gain1) + shift1
        a = gelu(n)
        store3(r.a3, i, jnp.where(inside, a, 0.0))
        return 0

    lax.fori_loop(0, s.side, act1, 0)
    for u in range(n1, 2 * n1):
        g_done(u)
        unpack(r.s2, u - n1, r.wt2)
    conv(r.a3, r.wt2, r.h2)
    local_stats(r.h2, r.st2)
    x_send(1, r.st2, r.t2)

    r.at[...] = jnp.transpose(r.a3[br : br + s.rows, ch : 2 * ch])

    def slope1(i, _):
        n = (r.h1[rows_of(i), :] - mean1) * (inv1 * gain1) + shift1
        r.back1[rows_of(i), :] = gelu_both(n)[1]
        return 0

    lax.fori_loop(0, s.side, slope1, 0)
    g_cross(2 * n1)
    g_done(2 * n1)
    at = iota((s.line, 1), 0)
    i_of = divided(at, wide, s.line)
    j_of = at - i_of * wide
    used = (i_of < s.side) & (j_of < s.side)
    wide_slots = s.n_dev * s.rp
    shard_rows = iota((s.line, wide_slots), 1)
    dense_all = r.sd[...].reshape(wide_slots, s.mp)
    for k in range(2):
        source = k * s.cells + i_of * s.side + j_of
        if k == 0:
            source = jnp.where(at == s.side, s.head_in, source)
            wanted = used | (at == s.side)
        else:
            wanted = used
        source = jnp.where(wanted, source, 0)
        shard = divided(source, s.rsh, 1024)
        place = jnp.where(wanted, shard * s.rp + (source - shard * s.rsh), -1)
        pick = (shard_rows == place).astype(f32).astype(bf16)
        r.dk[k] = dot(pick, dense_all).astype(bf16)
    r.dp_full[...] = jnp.zeros_like(r.dp_full)
    r.hc_full[...] = jnp.zeros_like(r.hc_full)
    row = iota((16, ch), 0)
    both = jnp.where(row < nb, hc0, jnp.where(row < 2 * nb, hc1, 0.0))
    r.hc_full[0:16, :] = both.astype(bf16)
    hc_rows = jnp.where(row == 0, hc0, jnp.where(row == 1, hc1, 0.0)).astype(bf16)

    x_wait(1, r.t2)
    mean2, inv2 = global_stats(r.t2)

    def act2(i, _):
        at = rows_of(i)
        xin = r.x3[pl.ds(pl.multiple_of((i + 1) * br, 16), br), ch : 2 * ch].astype(f32)
        z = xin + ((r.h2[at, :] - mean2) * (inv2 * gain2) + shift2)
        r.dz[at, :] = z
        a = jnp.where(inside, gelu(z), 0.0)
        r.out_r[at, :] = a.astype(bf16)
        r.out_v[i] = to_board(a)
        return 0

    lax.fori_loop(0, s.side, act2, 0)
    put_out = pltpu.make_async_copy(r.out_v, r.out, r.local_sem.at[len(names)])
    put_out.start()
    p_long = dot_nt(hc_rows, r.out_r[...])[0:8]
    lane = iota((8, s.long), 1)
    lane_j = lane - divided(lane, br, s.long) * br
    valid_long = (lane_j < nb * s.side) & (lane < s.rows)
    row1, lane1 = iota((8, lanes), 0), iota((8, lanes), 1)

    def by_head(v):
        a = v[0:1] + v[1:2] + v[2:3] + v[3:4]
        b = v[4:5] + v[5:6] + v[6:7] + v[7:8]
        return jnp.where(iota(v.shape, 0) < nb, a, b)

    n_local = float(nb * s.cells)
    mean_row = jnp.sum(jnp.where(valid_long, p_long, 0.0), axis=1, keepdims=True) / n_local
    dev = jnp.where(valid_long, p_long - mean_row, 0.0)
    square_row = jnp.sum(dev * dev, axis=1, keepdims=True)
    lane3 = iota((1, lanes), 1)
    means = jnp.where(lane3 < 32, mean_row[0:1], mean_row[1:2])
    r.st3[...] = jnp.where(lane3 < 64, means, jnp.where(lane3 < 96, square_row[0:1], square_row[1:2]))
    x_send(2, r.st3, r.t3)

    for name in names[8:]:
        fetch[name].wait()
    r.legal_both[...] = jnp.zeros_like(r.legal_both)
    r.legal_both[0:nb, 0 : s.moves] = r.legal_v[...]
    r.legal_both[nb : 2 * nb, 0 : s.moves] = r.legal_v[...]

    def slope2(i, carry):
        at = rows_of(i)
        slope = jnp.where(inside, gelu_both(r.dz[at, :])[1], 0.0)
        r.dz[at, :] = slope
        scaled = slope * ((r.h2[at, :] - mean2) * inv2)
        r.vu[at, 0:ch] = slope.astype(bf16)
        r.vu[at, ch:] = scaled.astype(bf16)
        cot = from_board(r.cot_v[i])
        a = (cot * scaled).reshape(br // 8, 8, ch)
        b = (cot * slope).reshape(br // 8, 8, ch)
        return carry[0] + jnp.sum(a, axis=0), carry[1] + jnp.sum(b, axis=0)

    zero = jnp.zeros((8, ch), f32)
    cot_g, cot_s = lax.fori_loop(0, s.side, slope2, (zero, zero))
    cot_g, cot_s = jnp.sum(cot_g, axis=0, keepdims=True), jnp.sum(cot_s, axis=0, keepdims=True)
    row = iota((16, s.long), 0)
    centred = jnp.where(valid_long[0:1], p_long[0:2] - mean_row[0:2], 0.0)
    against = jnp.where(
        row == 0, jnp.where(valid_long[0:1], 1.0, 0.0), jnp.where(row == 1, centred[0:1], jnp.where(row == 2, centred[1:2], 0.0))
    ).astype(bf16)
    early = dot(against, r.vu[...])
    for half in range(2):
        part = early[:, half * ch : (half + 1) * ch]
        ones = part[0:1]
        r.ste[4 * half : 4 * half + 1, :] = ones
        r.ste[4 * half + 1 : 4 * half + 2, :] = part[1:2] + mean_row[0:1] * ones
        r.ste[4 * half + 2 : 4 * half + 3, :] = part[2:3] + mean_row[1:2] * ones
        r.ste[4 * half + 3 : 4 * half + 4, :] = jnp.zeros((1, ch), f32)
    plane_send(3, r.ste, r.te)
    row = iota((8, s.long), 0)
    wanted = (lane & (nb - 1)) == (row & (nb - 1))
    rest = jnp.where(wanted, jnp.where(row < nb, p_long[0:1], p_long[1:2]), 0.0)
    parts = []
    for _ in range(3):
        part = rest.astype(bf16).astype(f32)
        parts.append(part)
        rest = rest - part
    parts = jnp.concatenate(parts + [jnp.zeros_like(rest)], axis=0).astype(bf16)
    p8 = dot(parts, r.expand[...])
    p8 = p8[0:8] + p8[8:16] + p8[16:24]
    row = iota((8, s.line), 0)
    lane = iota((8, s.line), 1)
    lane_i = divided(lane, wide, s.line)
    valid = (lane_i < s.side) & (lane - lane_i * wide < s.side)
    first_head = row < nb

    x_wait(2, r.t3)
    v = r.t3[...]
    mean_k = jnp.sum(v, axis=0) / float(s.n_dev)
    dev = v - mean_k
    squares = jnp.sum(jnp.where(lane3 < 64, n_local * dev * dev, v), axis=0)

    def of_head(v, at):
        return jnp.where(iota((8, 1), 0) < nb, v[:, at : at + 1], v[:, at + 32 : at + 33])

    mean_p = of_head(mean_k, 0)
    squares = of_head(squares, 0) + of_head(squares, 64)
    inv_p = lax.rsqrt(squares / s.count + epsilon)
    gain_p = jnp.where(iota((8, 1), 0) < nb, r.hng_v[0], r.hng_v[1])
    shift_p = jnp.where(iota((8, 1), 0) < nb, r.hns_v[0], r.hns_v[1])
    xhat_p = (p8 - mean_p) * inv_p
    feature, back_p = gelu_both(xhat_p * gain_p + shift_p)
    flat = jnp.where(valid, feature, 0.0).astype(bf16)
    one_lane = first_head & (lane == s.side)
    flat_f = flat.astype(f32)
    lhs0 = jnp.where(one_lane, 1.0, jnp.where(first_head, flat_f, 0.0))
    lhs1 = jnp.where(first_head, 0.0, flat_f)
    pad8 = jnp.zeros((8, s.line), f32)

    def tall(v):
        return jnp.concatenate([v, pad8[:, : v.shape[1]]], axis=0).astype(bf16)

    half = (dot(tall(lhs0), r.dk[0]) + dot(tall(lhs1), r.dk[1]))[0:8]
    logits = half + pltpu.roll(half, nb, 0)
    move = iota((8, s.mp), 1)
    masked = jnp.where(r.legal_both[...] == 1, logits, negative_fill)
    top = jnp.max(masked, axis=1, keepdims=True)
    terms = jnp.exp(masked - top)
    total = jnp.sum(terms, axis=1, keepdims=True)
    row_b = iota((8, 1), 0) & (nb - 1)
    target = jnp.where(
        row_b < 2,
        jnp.where(row_b == 0, r.target_v[0], r.target_v[1]),
        jnp.where(row_b == 2, r.target_v[2], r.target_v[3]),
    )
    chosen = move == target
    picked = jnp.sum(jnp.where(chosen, logits, 0.0), axis=1, keepdims=True)
    ce = top + jnp.log(total) - picked
    dl = (terms / total - chosen.astype(f32)).astype(bf16).astype(f32)
    first_move = iota((8, s.mp), 0) < nb
    dq = dot_nt(tall(jnp.where(first_move, dl, 0.0)), r.dk[0]) + dot_nt(
        tall(jnp.where(first_move, 0.0, dl)), r.dk[1]
    )
    dnh = jnp.where(valid, dq[0:8] * back_p, 0.0)
    gain_row = jnp.sum(dnh * xhat_p, axis=1, keepdims=True)
    shift_row = jnp.sum(dnh, axis=1, keepdims=True)
    scale_p = gain_p * inv_p
    long_row, long_lane = iota((8, s.long), 0), iota((8, s.long), 1)
    dnh_long = dot_nt(tall(dnh), r.expand[...])[0:8]
    dnh_long = jnp.where((long_lane & (nb - 1)) == (long_row & (nb - 1)), dnh_long, 0.0)
    late = dot(jnp.concatenate([dnh_long, jnp.zeros_like(dnh_long)], axis=0).astype(bf16), r.vu[...])[0:8]
    head_rows = jnp.where(iota((8, ch), 0) < nb, hc0, hc1) * scale_p
    late_s = jnp.sum(late[:, 0:ch] * head_rows, axis=0, keepdims=True)
    late_g = jnp.sum(late[:, ch:] * head_rows, axis=0, keepdims=True)
    r.st5[0:1, :] = cot_g + late_g
    r.st5[1:2, :] = cot_s + late_s

    def heads(v):
        return v[0:1] + v[1:2] + v[2:3] + v[3:4], v[4:5] + v[5:6] + v[6:7] + v[7:8]

    gain_heads, shift_heads, ce_sum = heads(gain_row), heads(shift_row), heads(ce)[0]
    lane5 = iota((1, ch), 1)
    low = jnp.where(lane5 < 32, gain_heads[0], gain_heads[1])
    high = jnp.where(lane5 < 96, shift_heads[0], shift_heads[1])
    r.st5[2:3, :] = jnp.where(lane5 < 64, low, jnp.where(lane5 < 128, high, ce_sum))
    x_send(4, r.st5, r.t5)
    group_wait(3, r.te)
    r.stl[...] = jnp.sum(r.te[...], axis=0)
    line_send(7, r.stl, r.tl)
    r.fd_own[...] = jnp.zeros_like(r.fd_own)
    r.fd_own[0:8, :] = flat_f
    r.fd_own[8:16, 0 : s.mp] = dl
    r.fd[gx, q, c] = r.fd_own[...].astype(bf16)
    g_start(2 * n1 + 1)
    flip(r.wt2, r.wb2)
    x_wait(4, r.t5)
    group_wait(7, r.tl)
    te = jnp.sum(r.tl[...], axis=0)
    t5 = jnp.sum(r.t5[...], axis=0)
    sums = t5[2:3]
    gain_sums, shift_sums = (sums[:, 0:1], sums[:, 32:33]), (sums[:, 64:65], sums[:, 96:97])
    r.tiny[0:1, :] = jnp.broadcast_to(sums[:, 128:129] / float(nb * s.n_dev), (1, lanes))
    first_lane = iota((1, lanes), 1) == 0
    r.tiny[1:2, :] = jnp.where(first_lane, *gain_sums)
    r.tiny[2:3, :] = jnp.where(first_lane, *shift_sums)
    gain_sum = jnp.where(iota((8, 1), 0) < nb, *gain_sums)
    shift_sum = jnp.where(iota((8, 1), 0) < nb, *shift_sums)
    g2s, s2s = t5[0:1], t5[1:2]
    for k in range(2):
        weight = (hc0, hc1)[k] * (scale_p[nb * k : nb * k + 1] / s.count)
        gain_part = gain_sums[k] * inv_p[nb * k : nb * k + 1]
        mean_k = mean_p[nb * k : nb * k + 1]
        s2s = s2s - weight * (shift_sums[k] * te[0:1] + gain_part * (te[k + 1 : k + 2] - mean_k * te[0:1]))
        g2s = g2s - weight * (shift_sums[k] * te[4:5] + gain_part * (te[k + 5 : k + 6] - mean_k * te[4:5]))
    dp = scale_p * (dnh - (shift_sum + xhat_p * gain_sum) / s.count)
    dp = jnp.where(valid, dp, 0.0)
    r.dp_full[0:16, :] = tall(dp)

    spread_p = dot_nt(r.expand[0 : s.rows, :], r.dp_full[...])
    row, col = iota((s.rows, lanes), 0), iota((s.rows, lanes), 1)
    spread_p = jnp.where((row & (nb - 1)) == (col & (nb - 1)), spread_p, 0.0).astype(bf16)
    r.spread[...] = spread_p
    r.up[...] = dot(spread_p, r.hc_full[...])

    def sums_back(field, xhat, carry):
        f = field.reshape(br // 8, 8, ch)
        g = (field * xhat).reshape(br // 8, 8, ch)
        return carry[0] + jnp.sum(g, axis=0), carry[1] + jnp.sum(f, axis=0)

    def to_field2(i, _):
        at = rows_of(i)
        xhat = (r.h2[at, :] - mean2) * inv2
        dz = (from_board(r.cot_v[i]) + r.up[at, :]) * r.dz[at, :]
        r.dz[at, :] = dz
        d = (gain2 * inv2) * (dz - (s2s + xhat * g2s) * (1.0 / s.count))
        store3(r.d3, i, jnp.where(inside, d, 0.0))
        return 0

    lax.fori_loop(0, s.side, to_field2, 0)

    def wgrad(planes_t, di):
        start = 2 * br - br * di
        return dot(planes_t[...], r.d3[start : start + s.rows, :])

    early = 1 if s.fast else 0
    for di in range(early):
        rs_fill(di, wgrad(r.at, di), rs2)
        rs_cross(rs2, di)
    g_forward(2 * n1 + 1)
    conv(r.d3, r.wb2, r.h2)

    def back1(i, carry):
        at = rows_of(i)
        dn = jnp.where(inside, r.h2[at, :] * r.back1[at, :], 0.0)
        r.h2[at, :] = dn
        return sums_back(dn, (r.h1[at, :] - mean1) * inv1, carry)

    g1, s1 = lax.fori_loop(0, s.side, back1, (zero, zero))
    r.st6[0:1, :] = jnp.sum(g1, axis=0, keepdims=True)
    r.st6[1:2, :] = jnp.sum(s1, axis=0, keepdims=True)
    x_send(5, r.st6, r.t6)
    head_grad = lax.dot_general(
        r.spread[...], r.out_r[0 : s.rows, :], (((0,), (0,)), ((), ())), preferred_element_type=f32
    )
    r.sth[0:1, :] = head_grad[0:1] + head_grad[1:2] + head_grad[2:3] + head_grad[3:4]
    r.sth[1:2, :] = head_grad[4:5] + head_grad[5:6] + head_grad[6:7] + head_grad[7:8]
    x_send(6, r.sth, r.th)
    for part in range(early):
        rs_plane(rs2, part)
    for di in range(early, 3):
        rs_fill(di, wgrad(r.at, di), rs2)
        if s.fast:
            rs_cross(rs2, di)
    rs_fill_rest(rs2)
    if not s.fast:
        rs_cross(rs2, 0)
    for part in range(early, s.nch - 1):
        rs_plane(rs2, part)
    g_cross(2 * n1 + 1)
    x_wait(5, r.t6)
    t6 = jnp.sum(r.t6[...], axis=0)
    g1s, s1s = t6[0:1], t6[1:2]

    def to_field1(i, _):
        at = rows_of(i)
        xhat = (r.h1[at, :] - mean1) * inv1
        d = (gain1 * inv1) * (r.h2[at, :] - (s1s + xhat * g1s) * (1.0 / s.count))
        store3(r.d3, i, jnp.where(inside, d, 0.0))
        return 0

    rs_plane(rs2, s.nch - 1)
    lax.fori_loop(0, s.side, to_field1, 0)
    for di in range(3):
        rs_fill(di, wgrad(r.xt, di), rs1)
        if s.fast:
            rs_cross(rs1, di)
            if di:
                rs_plane(rs1, di - 1)
    rs_fill_rest(rs1)
    if not s.fast:
        rs_cross(rs1, 0)
    rs_plane(rs1, s.nch - 1)
    conv(r.d3, r.wb1, r.h1)
    for part in range(s.nch):
        rs_line(rs2, part)

    def result(i, _):
        at = rows_of(i)
        r.in_grad_v[i] = to_board(r.dz[at, :] + r.h1[at, :])
        return 0

    lax.fori_loop(0, s.side, result, 0)
    put_in_grad = pltpu.make_async_copy(r.in_grad_v, r.in_grad, r.local_sem.at[len(names) + 1])
    put_in_grad.start()
    x_wait(6, r.th)
    shares = jnp.concatenate([g1s, g2s, s1s, s2s, jnp.sum(r.th[...], axis=0), jnp.zeros((2, ch), f32)], axis=0)
    r.tiny[8:16, :] = pltpu.roll(shares, lax.rem(ch - w * me, ch), 1)[:, 0:lanes]

    for part in range(s.nch):
        rs_line(rs1, part)

    g_done(2 * n1 + 1)
    fd = r.fd[...].astype(f32).reshape(s.n_dev, 16, s.line)
    features = fd[:, 0:8, :].reshape(8 * s.n_dev, s.line).astype(bf16)
    dls = fd[:, 8:16, 0 : s.mp].reshape(8 * s.n_dev, s.mp).astype(bf16)
    t = iota((s.rp, 1), 0)
    source = s.rsh * me + t
    mine = (t < s.rsh) & (source < s.head_in)
    col = iota((s.rp, s.line), 1)
    col8 = iota((s.rp, 8 * s.n_dev), 1) & 7
    own = jnp.where((t < s.rsh) & (source == s.head_in) & (col8 < nb), 1.0, 0.0)
    for k in range(2):
        in_k = mine & (source >= k * s.cells) & (source < (k + 1) * s.cells)
        cell = jnp.where(in_k, source - k * s.cells, 0)
        cell_i = divided(cell, s.side, s.cells)
        place = jnp.where(in_k, cell_i * wide + (cell - cell_i * s.side), -1)
        pick = (col == place).astype(f32).astype(bf16)
        rows_k = dot_nt(pick, features)
        own = own + jnp.where((col8 >= nb) if k else (col8 < nb), rows_k, 0.0)
    grad = dot(own.astype(bf16), dls)
    r.dense_grad[...] = grad

    for part in range(s.nch):
        rs_finish(rs2, part, r.c2_grad)
    for part in range(s.nch):
        rs_finish(rs1, part, r.c1_grad)

    for u in range(len(units)):
        g_drain(u)
    for number, slots in enumerate((r.t1, r.t2, r.t3, None, r.t5, r.t6, r.th)):
        if number != 3:
            x_drain(number, slots)
    group_wait(3, r.te, 0)
    group_wait(7, r.tl, 0)
    rs_drain(rs1)
    rs_drain(rs2)
    put_out.wait()
    put_in_grad.wait()


def place(w, x_ref, in_x_ref, c1, c2, dense, tiny, *refs):
    (out, loss, in_grad, c1_out, c2_out, gains, shifts, hc, hng, dense_out), refs = refs[:10], refs[10:]
    (out_v, in_v, c1_v, c2_v, dense_v, tiny_v), (came, went) = refs[:6], refs[6:]
    sources, held = (tiny, dense, c1, c2, x_ref, in_x_ref), (tiny_v, dense_v, c1_v, c2_v, out_v, in_v)
    fetch = [pltpu.make_async_copy(a, b, came.at[i]) for i, (a, b) in enumerate(zip(sources, held))]
    put = [
        pltpu.make_async_copy(a, b, went.at[i])
        for i, (a, b) in enumerate(((c1_v, c1_out), (c2_v, c2_out), (out_v, out), (in_v, in_grad)))
    ]
    for copy in fetch:
        copy.start()
    for i in range(4):
        fetch[i + 2].wait()
        put[i].start()
    fetch[0].wait()
    fetch[1].wait()
    loss[...] = tiny_v[0:1, 0:1]
    hng[...] = tiny_v[1:3, 0:2]
    gains[...] = tiny_v[8:10, 0:w]
    shifts[...] = tiny_v[10:12, 0:w]
    hc[...] = tiny_v[12:14, 0:w]
    dense_out[...] = dense_v[0 : dense_out.shape[0], 0 : dense_out.shape[1]]
    for copy in put:
        copy.wait()


def body(x, w1, w2, gains, shifts, hc, hng, hns, dense, legal, target, cot):
    x, cot = (jnp.transpose(v, (1, 2, 0, 3)) for v in (x, cot))
    s = sizes_of(lax.axis_size("gx"), lax.axis_size("gy"), x, w1, dense, legal.shape[1])
    vmem, hbm = pltpu.VMEM, pl.ANY
    inputs = dict(
        x=x, w1=w1, w2=w2, gains=gains, shifts=shifts, hc=hc, hng=hng, hns=hns, dense=dense, legal=legal,
        target=target, cot=cot,
    )
    outputs = dict(
        out=(x.shape, bf16), in_grad=(x.shape, bf16), c1_grad=(w1.shape, f32), c2_grad=(w2.shape, f32),
        dense_grad=((s.rp, s.mp), f32), tiny=((16, lanes), f32),
    )
    gxn, qn, n, ch = s.gx_n, s.q_n, s.n_dev, s.ch
    field = pltpu.VMEM((s.rows, ch), f32)
    boards = pltpu.VMEM((s.side, s.wide, s.nb, ch), bf16)
    planes = pltpu.VMEM((s.padded, 3 * ch), bf16)
    turned = pltpu.VMEM((ch, s.rows), bf16)
    weight = pltpu.VMEM((3, 3 * ch, ch), bf16)
    two = pltpu.VMEM((2, ch), f32)
    eight = pltpu.VMEM((8, ch), f32)
    dma = pltpu.SemaphoreType.DMA
    scratch = dict(
        local_sem=dma((14,)), g_sem=dma((2 * s.nch + 2, 5 + gxn)), x_sem=dma((8, 2)),
        rs_sem1=dma((s.nch, 6)), rs_sem2=dma((s.nch, 6)),
        x_v=boards, cot_v=boards, out_v=pltpu.VMEM(x.shape, bf16), in_grad_v=pltpu.VMEM(x.shape, bf16),
        stage=pltpu.VMEM((s.blk1, lanes), f32), small=pltpu.VMEM((8, lanes), f32),
        s1=pltpu.VMEM((gxn, qn, 2, s.blk1, lanes), bf16), s2=pltpu.VMEM((gxn, qn, 2, s.blk, lanes), bf16),
        sd=pltpu.VMEM((gxn, qn, 2, s.rp, s.mp), bf16), dense_f=pltpu.VMEM((s.rp, s.mp), f32),
        x3=planes, a3=planes, d3=planes, out_r=pltpu.VMEM((s.long, ch), bf16), spread=pltpu.VMEM((s.rows, lanes), bf16),
        xt=turned, at=turned, wt1=weight, wt2=weight, wb1=weight, wb2=weight,
        pars=pltpu.VMEM((8, ch), f32), h1=field, h2=field, dz=field, back1=field, up=field,
        st1=two, t1=pltpu.VMEM((n, 2, ch), f32), st2=two, t2=pltpu.VMEM((n, 2, ch), f32),
        st3=pltpu.VMEM((1, lanes), f32), t3=pltpu.VMEM((n, 1, lanes), f32), ste=eight, te=pltpu.VMEM((s.gy_n, 8, ch), f32), stl=eight, tl=pltpu.VMEM((gxn, 8, ch), f32),
        st5=pltpu.VMEM((3, ch), f32), t5=pltpu.VMEM((n, 3, ch), f32), st6=two, t6=pltpu.VMEM((n, 2, ch), f32),
        sth=two, th=pltpu.VMEM((n, 2, ch), f32), vu=pltpu.VMEM((s.long, 2 * ch), bf16),
        fd_own=pltpu.VMEM((16, s.line), f32), fd=pltpu.VMEM((gxn, qn, 2, 16, s.line), bf16),
        dk=pltpu.VMEM((2, s.line, s.mp), bf16), expand=pltpu.VMEM((s.long, s.line), bf16),
        dp_full=pltpu.VMEM((lanes, s.line), bf16), hc_full=pltpu.VMEM((lanes, ch), bf16),
        legal_both=pltpu.VMEM((8, s.mp), jnp.int32),
    )
    for name in ("w1", "w2", "gains", "shifts", "hc", "dense", "legal"):
        scratch[name + "_v"] = pltpu.VMEM(inputs[name].shape, inputs[name].dtype)
    for name in ("hng", "hns", "target"):
        scratch[name + "_v"] = pltpu.SMEM(inputs[name].shape, inputs[name].dtype)
    if not s.fast:
        scratch["flat"] = pltpu.VMEM((9, ch, ch), f32)
        scratch["eight"] = pltpu.VMEM((9, 8, ch), f32)
    for number in ("1", "2"):
        scratch["rsb" + number] = pltpu.VMEM((s.nch, 2, gxn, qn, s.crows, lanes), bf16)
        scratch["rc" + number] = pltpu.VMEM((s.nch, gxn, qn, s.crows, lanes), bf16)
        scratch["pb" + number] = pltpu.VMEM((s.nch, qn, gxn, s.crows, lanes), bf16)
        scratch["rp" + number] = pltpu.VMEM((s.nch, qn - 1, gxn, s.crows, lanes), bf16)
        scratch["zb" + number] = pltpu.VMEM((s.nch, gxn, s.crows, lanes), bf16)
        scratch["rd" + number] = pltpu.VMEM((gxn * qn - 1, s.crows, lanes), bf16)
        scratch["rz" + number] = pltpu.VMEM((s.nch, gxn - 1, s.crows, lanes), bf16)
    run = pl.pallas_call(
        functools.partial(kernel, s, tuple(inputs), tuple(outputs), tuple(scratch)),
        out_shape=[jax.ShapeDtypeStruct(shape, kind) for shape, kind in outputs.values()],
        in_specs=[pl.BlockSpec(memory_space=hbm) for _ in inputs],
        out_specs=[pl.BlockSpec(memory_space=hbm if n in ("out", "in_grad") else vmem) for n in outputs],
        scratch_shapes=list(scratch.values()),
        compiler_params=pltpu.CompilerParams(
            collective_id=0, has_side_effects=True, vmem_limit_bytes=60 * 1024 * 1024
        ),
        cost_estimate=pl.CostEstimate(flops=10_500_000_000, bytes_accessed=8_000_000, transcendentals=800_000),
        name="tower",
    )
    results = run(*inputs.values())
    kinds = [jax.ShapeDtypeStruct(v.shape, v.dtype) for v in results]
    out, in_grad, c1_grad, c2_grad, dense_grad, _ = kinds
    small = [jax.ShapeDtypeStruct(v.shape, f32) for v in (gains, shifts, hc)]
    loss, pair = (jax.ShapeDtypeStruct(shape, f32) for shape in ((1, 1), (2, 2)))
    shapes = [out, loss, in_grad, c1_grad, c2_grad, *small, pair, jax.ShapeDtypeStruct(dense.shape, f32)]
    results = pl.pallas_call(
        functools.partial(place, s.w),
        out_shape=shapes,
        in_specs=[pl.BlockSpec(memory_space=hbm) for _ in kinds],
        out_specs=[pl.BlockSpec(memory_space=hbm if n in (0, 2, 3, 4) else vmem) for n in range(len(shapes))],
        scratch_shapes=[pltpu.VMEM(v.shape, v.dtype) for v in kinds] + [dma((len(kinds),))] * 2,
        name="place",
    )(*results)
    out, loss, in_grad, *rest = results
    out, in_grad = (jnp.transpose(v, (2, 0, 1, 3)) for v in (out, in_grad))
    return (out, loss.reshape(()), in_grad, *rest)


def solution(mesh):
    both = ("gx", "gy")
    board = P(both, None, None, None)
    kernels = P(None, both, None)
    pairs = P(None, both)
    return jax.shard_map(
        body,
        mesh=mesh,
        in_specs=(
            board, kernels, kernels, pairs, pairs, pairs, P(), P(), P(both, None), P(both, None), P(both), board,
        ),
        out_specs=(board, P(), board, kernels, kernels, pairs, pairs, pairs, P(), P(both, None)),
        check_vma=False,
    )
```

```python
import functools
import types

import jax
import jax.numpy as jnp
from jax import lax
from jax.experimental import pallas as pl
from jax.experimental.pallas import tpu as pltpu
from jax.sharding import PartitionSpec as P

MESH = pl.DeviceIdType.MESH
f32 = jnp.float32
bf16 = jnp.bfloat16
epsilon = 1e-05
negative_fill = -1e30
root = 0.7978845608028654
cube = 0.044715
lanes = 128


def up_to(value, unit):
    return -(-value // unit) * unit


def divided(values, divisor, limit):
    for shift in range(16, 24):
        factor = -(-(1 << shift) // divisor)
        if all((n * factor) >> shift == n // divisor and n * factor < 2**31 for n in range(limit)):
            return lax.shift_right_logical(values * factor, jnp.int32(shift))
    raise ValueError("no factor")


def iota(shape, axis):
    return lax.broadcasted_iota(jnp.int32, shape, axis)


def gelu_both(v):
    square = v * v
    slope = jnp.tanh(v * (root + (root * cube) * square))
    half = 0.5 + 0.5 * slope
    back = half + (0.5 * v) * (1.0 - slope * slope) * (root + (3.0 * root * cube) * square)
    return v * half, back


def gelu(v):
    half = 0.5 * v
    return half + half * jnp.tanh(v * (root + (root * cube) * (v * v)))


def dot(left, right):
    return jnp.dot(left, right, preferred_element_type=f32)


def dot_nt(left, right):
    return lax.dot_general(left, right, (((1,), (1,)), ((), ())), preferred_element_type=f32)


def sizes_of(gx_n, gy_n, x, w1, dense, moves):
    s = types.SimpleNamespace()
    s.gx_n, s.gy_n, s.q_n, s.n_dev = gx_n, gy_n, gy_n // 2, gx_n * gy_n
    s.side, s.nb, s.ch = x.shape[0], x.shape[2], x.shape[3]
    s.w = w1.shape[1]
    s.wide = s.side + 1
    s.br = s.wide * s.nb
    s.rows = s.side * s.br
    s.line = up_to(s.side * s.wide, lanes)
    s.long = up_to(s.rows, 3 * lanes)
    s.padded = s.long + 2 * s.br
    s.cells = s.side * s.side
    s.moves = moves
    s.mp = up_to(moves, lanes)
    s.rsh = dense.shape[0]
    s.rp = up_to(s.rsh, 16)
    s.head_in = 2 * s.cells
    s.blk = up_to(18 * s.w, 16)
    s.blk1 = up_to(19 * s.w, 16)
    s.fast = s.w == 8
    s.nch = 3 if s.fast else 1
    s.crows = s.blk // s.nch
    s.count = float(s.nb * s.cells * s.n_dev)
    assert s.nb == 4 and s.br % 16 == 0 and 8 % s.w == 0
    assert gx_n & (gx_n - 1) == 0 and gy_n & (gy_n - 1) == 0 and gy_n > 1
    return s


def kernel(s, in_names, out_names, scratch_names, *refs):
    r = types.SimpleNamespace(**dict(zip(in_names + out_names + scratch_names, refs)))
    gx, gy = lax.axis_index("gx"), lax.axis_index("gy")
    q, c = lax.div(gy, 2), lax.rem(gy, 2)
    me = gx * s.gy_n + gy
    other = (gx, gy + 1 - 2 * c)
    gxn, qn, nb, br, wide, ch = s.gx_n, s.q_n, s.nb, s.br, s.wide, s.ch

    def z_peer(k):
        return gx ^ k

    def q_peer(j):
        return q ^ j

    def send(src, dst, out_sem, in_sem, device):
        pltpu.make_async_remote_copy(
            src_ref=src, dst_ref=dst, send_sem=out_sem, recv_sem=in_sem, device_id=device, device_id_type=MESH
        ).start()

    def take(sem, ref):
        pltpu.make_async_copy(ref, ref, sem).wait()

    barrier = pltpu.get_barrier_semaphore()
    partners = [(z_peer(k), gy) for k in range(1, gxn)]
    partners += [(gx, 2 * q_peer(j) + c) for j in range(1, qn)]
    partners += [other]
    for p in partners:
        pl.semaphore_signal(barrier, inc=1, device_id=p, device_id_type=MESH)
    names = ("x", "w1", "w2", "gains", "shifts", "hc", "dense", "cot", "legal", "hng", "hns", "target")
    fetch = {}
    for n, name in enumerate(names):
        held = getattr(r, name + "_v")
        held = held.at[:, pl.ds(0, s.side)] if name in ("x", "cot") else held
        fetch[name] = pltpu.make_async_copy(getattr(r, name), held, r.local_sem.at[n])
        fetch[name].start()
    for fields in (r.x_v, r.cot_v):
        fields[:, s.side] = jnp.zeros((s.side, nb, ch), bf16)

    w = s.w

    def stage(weight):
        r.stage[...] = jnp.zeros_like(r.stage)
        for t in range(9):
            v = weight[t].astype(f32)
            r.stage[2 * w * t : 2 * w * t + w, :] = v[:, :lanes]
            r.stage[2 * w * t + w : 2 * w * t + 2 * w, :] = v[:, lanes:]

    def stage_all():
        for name in names[1:7]:
            fetch[name].wait()
        r.small[...] = jnp.zeros_like(r.small)
        r.small[0:2, 0:w] = r.gains_v[...].astype(f32)
        r.small[2:4, 0:w] = r.shifts_v[...].astype(f32)
        r.small[4:6, 0:w] = r.hc_v[...].astype(f32)
        stage(r.w1_v)
        r.stage[18 * w : 19 * w, 0:8] = jnp.transpose(r.small[...])[0:w, :]
        r.s1[gx, q, c] = r.stage[...].astype(bf16)
        stage(r.w2_v)
        r.s2[gx, q, c] = r.stage[0 : s.blk, :].astype(bf16)
        r.dense_f[...] = jnp.zeros_like(r.dense_f)
        r.dense_f[0 : s.rsh, 0 : s.moves] = r.dense_v[...].astype(f32)
        r.sd[gx, q, c] = r.dense_f[...].astype(bf16)

    for planes in (r.x3, r.a3, r.d3):
        planes[0:br, :] = jnp.zeros((br, 3 * ch), bf16)
        planes[br + s.rows :, :] = jnp.zeros((s.padded - br - s.rows, 3 * ch), bf16)
    inside = iota((br, ch), 0) < nb * s.side

    def store3(planes, i, block):
        at = pl.ds(pl.multiple_of((i + 1) * br, 16), br)
        planes[at, 0:ch] = pltpu.roll(block, nb, 0).astype(bf16)
        planes[at, ch : 2 * ch] = block.astype(bf16)
        planes[at, 2 * ch :] = pltpu.roll(block, br - nb, 0).astype(bf16)

    def rows_of(i):
        return pl.ds(pl.multiple_of(i * br, 16), br)

    def from_board(block):
        return block.astype(f32).reshape(br, ch)

    def to_board(block):
        return block.reshape(wide, nb, ch)[0 : s.side].astype(bf16)

    def x_rows(i, _):
        store3(r.x3, i, from_board(r.x_v[i]))
        return 0

    fetch["x"].wait()
    lax.fori_loop(0, s.side, x_rows, 0)
    stage_all()

    pl.semaphore_wait(barrier, len(partners))

    def span(unit):
        store, part = unit
        if store is r.sd or store is r.fd:
            return pl.ds(0, store.shape[3])
        whole = s.blk1 if store is r.s1 else s.blk
        if s.nch == 1:
            return pl.ds(0, whole)
        start = part * s.crows
        return pl.ds(start, whole - start if part == s.nch - 1 else s.crows)

    units = [(r.s1, p) for p in range(s.nch)] + [(r.s2, p) for p in range(s.nch)] + [(r.sd, 0), (r.fd, 0)]

    turned = {s.nch} if s.nch > 1 else set()

    def g_start(u):
        store, at = units[u][0], span(units[u])
        own = store.at[gx, q, c, at]
        for k in range(1, gxn):
            if u not in turned:
                send(own, own, r.g_sem.at[u, 0], r.g_sem.at[u, 5 + k], (z_peer(k), gy))
        for j in range(qn - 1, 0, -1):
            send(own, own, r.g_sem.at[u, 1], r.g_sem.at[u, 4], (gx, 2 * q_peer(j) + c))

    def g_forward(u):
        store, at = units[u][0], span(units[u])
        if u in turned:
            take(r.g_sem.at[u, 4], store.at[gx, pl.ds(0, qn - 1), 0, at])
            block = store.at[gx, :, c, at]
            for k in range(gxn - 1, 0, -1):
                send(block, block, r.g_sem.at[u, 2], r.g_sem.at[u, 5 + k], (z_peer(k), gy))
            return
        for k in range(1, gxn):
            block = store.at[z_peer(k), q, c, at]
            take(r.g_sem.at[u, 5 + k], block)
            for j in range(qn - 1, 0, -1):
                send(block, block, r.g_sem.at[u, 2], r.g_sem.at[u, 4], (gx, 2 * q_peer(j) + c))

    def g_cross(u):
        store, at = units[u][0], span(units[u])
        if u in turned:
            for k in range(1, gxn):
                take(r.g_sem.at[u, 5 + k], store.at[z_peer(k), :, c, at])
        else:
            take(r.g_sem.at[u, 4], store.at[:, pl.ds(0, qn - 1), 0, at])
        block = store.at[:, :, c, at]
        send(block, block, r.g_sem.at[u, 3], r.g_sem.at[u, 5], other)

    def g_done(u):
        store, at = units[u][0], span(units[u])
        take(r.g_sem.at[u, 5], store.at[:, :, 0, at])

    def g_drain(u):
        store, at = units[u][0], span(units[u])
        take(r.g_sem.at[u, 1], store.at[0, pl.ds(0, qn - 1), 0, at])
        if u in turned:
            take(r.g_sem.at[u, 2], store.at[pl.ds(0, gxn - 1), :, 0, at])
        else:
            take(r.g_sem.at[u, 0], store.at[pl.ds(0, gxn - 1), 0, 0, at])
            take(r.g_sem.at[u, 2], store.at[pl.ds(0, gxn - 1), pl.ds(0, qn - 1), 0, at])
        take(r.g_sem.at[u, 3], store.at[:, :, 0, at])

    def shard_of(store, d):
        return store[lax.div(d, s.gy_n), lax.div(lax.rem(d, s.gy_n), 2), lax.rem(d, 2)]

    def unpack(store, part, weight):
        if s.fast:
            for dj in range(3):
                at = 16 * (3 * part + dj)
                v = store[:, :, :, at : at + 16, :].astype(f32).reshape(s.n_dev, 16, lanes)
                low = v[:, 0:8, :].reshape(ch, lanes)
                high = v[:, 8:16, :].reshape(ch, lanes)
                weight[part, dj * ch : (dj + 1) * ch, :] = jnp.concatenate([low, high], axis=1).astype(bf16)
            return

        def one(g, _):
            for e in range(8 // w):
                r.stage[0 : s.blk, :] = shard_of(store, g * (8 // w) + e)[0 : s.blk].astype(f32)
                for t in range(9):
                    r.eight[t, w * e : w * e + w, 0:lanes] = r.stage[2 * w * t : 2 * w * t + w, :]
                    r.eight[t, w * e : w * e + w, lanes:] = r.stage[2 * w * t + w : 2 * w * t + 2 * w, :]
            for t in range(9):
                r.flat[t, pl.ds(pl.multiple_of(8 * g, 8), 8), :] = r.eight[t]
            return 0

        lax.fori_loop(0, ch // 8, one, 0)
        for t in range(9):
            weight[t // 3, (t % 3) * ch : (t % 3 + 1) * ch, :] = r.flat[t].astype(bf16)

    def unpack_small():
        if s.fast:
            v = r.s1[:, :, :, 18 * w : 18 * w + 16, :].astype(f32).reshape(s.n_dev, 16, lanes)
            rows = v[:, 0:8, :].reshape(ch, lanes)
        else:

            def one(g, _):
                for e in range(8 // w):
                    r.stage[...] = shard_of(r.s1, g * (8 // w) + e).astype(f32)
                    r.eight[0, w * e : w * e + w, 0:lanes] = r.stage[18 * w : 19 * w, :]
                r.flat[0, pl.ds(pl.multiple_of(8 * g, 8), 8), :] = r.eight[0]
                return 0

            lax.fori_loop(0, ch // 8, one, 0)
            rows = r.flat[0, :, 0:lanes]
        r.pars[...] = jnp.transpose(rows)[0:8, :]

    def x_send(number, src, slots):
        def one(k):
            device = (gx ^ lax.div(k, s.gy_n), gy ^ lax.rem(k, s.gy_n))
            send(src, slots.at[me], r.x_sem.at[number, 0], r.x_sem.at[number, 1], device)

        if s.n_dev <= 64:
            hops = {k: k // s.gy_n + bin(k % s.gy_n // 2).count("1") for k in range(1, s.n_dev)}
            for k in sorted(hops, key=lambda k: (-hops[k], k)):
                send(
                    src, slots.at[me], r.x_sem.at[number, 0], r.x_sem.at[number, 1],
                    (gx ^ (k // s.gy_n), gy ^ (k % s.gy_n)),
                )
        else:
            lax.fori_loop(0, s.n_dev - 1, lambda n, _: (one(s.n_dev - 1 - n), 0)[1], 0)
        slots[me] = src[...]

    def x_wait(number, slots):
        take(r.x_sem.at[number, 1], slots.at[pl.ds(0, s.n_dev - 1)])

    def x_drain(number, slots):
        take(r.x_sem.at[number, 0], slots.at[pl.ds(0, s.n_dev - 1)])

    def plane_send(number, src, slots):
        for k in range(s.gy_n - 1, 0, -1):
            send(src, slots.at[gy], r.x_sem.at[number, 0], r.x_sem.at[number, 1], (gx, gy ^ k))
        slots[gy] = src[...]

    def line_send(number, src, slots):
        for k in range(gxn - 1, 0, -1):
            send(src, slots.at[gx], r.x_sem.at[number, 0], r.x_sem.at[number, 1], (gx ^ k, gy))
        slots[gx] = src[...]

    def group_wait(number, slots, way=1):
        take(r.x_sem.at[number, way], slots.at[pl.ds(0, slots.shape[0] - 1)])

    def rs_fill(part, grad, b):
        if s.fast:
            for dj in range(3):
                g = grad[:, (2 - dj) * ch : (3 - dj) * ch]
                low = g[:, :lanes].reshape(s.n_dev, 8, lanes)
                high = g[:, lanes:].reshape(s.n_dev, 8, lanes)
                v = jnp.concatenate([low, high], axis=1).astype(bf16).reshape(gxn, qn, 2, 16, lanes)
                for core in range(2):
                    b.rsb[part, core, :, :, 16 * dj : 16 * dj + 16, :] = v[:, :, core]
        else:
            for dj in range(3):
                r.flat[3 * part + dj] = grad[:, (2 - dj) * ch : (3 - dj) * ch]

    def rs_fill_rest(b):
        if s.fast:
            return
        r.stage[...] = jnp.zeros_like(r.stage)

        def one(g, _):
            for t in range(9):
                r.eight[t] = r.flat[t, pl.ds(pl.multiple_of(8 * g, 8), 8), :]
            for e in range(8 // w):
                d = g * (8 // w) + e
                for t in range(9):
                    v = r.eight[t, w * e : w * e + w, :]
                    r.stage[2 * w * t : 2 * w * t + w, :] = v[:, :lanes]
                    r.stage[2 * w * t + w : 2 * w * t + 2 * w, :] = v[:, lanes:]
                at = (0, lax.rem(d, 2), lax.div(d, s.gy_n), lax.div(lax.rem(d, s.gy_n), 2))
                b.rsb[at] = r.stage[0 : s.blk, :].astype(bf16)
            return 0

        lax.fori_loop(0, ch // 8, one, 0)

    def rs_cross(b, part):
        send(b.rsb.at[part, 1 - c], b.rc.at[part], b.sem.at[part, 0], b.sem.at[part, 1], other)

    def rs_plane(b, part):
        take(b.sem.at[part, 1], b.rc.at[part])
        for p in range(qn):
            total = b.rsb[part, c, :, p].astype(f32) + b.rc[part, :, p].astype(f32)
            b.pb[part, p] = total.astype(bf16)
        if s.nch > 1 and part == s.nch - 1:
            for k in range(gxn - 1, -1, -1):
                for j in range(qn - 1, -1, -1):
                    if k + j:
                        block = b.pb.at[part, q_peer(j), z_peer(k)]
                        device = (z_peer(k), 2 * q_peer(j) + c)
                        send(block, b.rd.at[k * qn + j - 1], b.sem.at[part, 2], b.sem.at[part, 3], device)
            return
        for j in range(1, qn):
            to = q_peer(j)
            send(b.pb.at[part, to], b.rp.at[part, j - 1], b.sem.at[part, 2], b.sem.at[part, 3], (gx, 2 * to + c))

    def rs_line(b, part):
        if s.nch > 1 and part == s.nch - 1:
            return
        take(b.sem.at[part, 3], b.rp.at[part])
        total = b.pb[part, q].astype(f32)
        for j in range(qn - 1):
            total = total + b.rp[part, j].astype(f32)
        b.zb[part] = total.astype(bf16)
        for k in range(1, gxn):
            to = z_peer(k)
            send(b.zb.at[part, to], b.rz.at[part, k - 1], b.sem.at[part, 4], b.sem.at[part, 5], (to, gy))

    def rs_finish(b, part, out):
        if s.nch > 1 and part == s.nch - 1:
            take(b.sem.at[part, 3], b.rd)
            total = b.pb[part, q, gx].astype(f32) + jnp.sum(b.rd[...].astype(f32), axis=0)
        else:
            take(b.sem.at[part, 5], b.rz.at[part])
            total = b.zb[part, gx].astype(f32)
            for k in range(gxn - 1):
                total = total + b.rz[part, k].astype(f32)
        taps = 9 // s.nch
        for t in range(taps):
            at = 2 * w * t
            out[part * taps + t] = jnp.concatenate([total[at : at + w], total[at + w : at + 2 * w]], axis=1)

    def rs_drain(b):
        for part in range(s.nch):
            take(b.sem.at[part, 0], b.rc.at[part])
            if s.nch > 1 and part == s.nch - 1:
                take(b.sem.at[part, 2], b.rd)
                continue
            take(b.sem.at[part, 2], b.rp.at[part])
            take(b.sem.at[part, 4], b.rz.at[part])

    def rs_buffers(number):
        names = ("rsb", "rc", "pb", "rp", "zb", "rz", "rd")
        b = types.SimpleNamespace(**{n: getattr(r, n + number) for n in names})
        b.sem = getattr(r, "rs_sem" + number)
        return b

    rs1, rs2 = rs_buffers("1"), rs_buffers("2")

    def local_stats(field, out):
        pivot = field[0:1, :]

        def one(i, carry):
            d = jnp.where(inside, field[rows_of(i), :] - pivot, 0.0).reshape(br // 8, 8, ch)
            return carry[0] + jnp.sum(d, axis=0), carry[1] + jnp.sum(d * d, axis=0)

        zero = jnp.zeros((8, ch), f32)
        first, second = lax.fori_loop(0, s.side, one, (zero, zero))
        n = float(nb * s.cells)
        first = jnp.sum(first, axis=0, keepdims=True) / n
        second = jnp.sum(second, axis=0, keepdims=True) - n * first * first
        out[0:1, :] = pivot + first
        out[1:2, :] = second

    def global_stats(slots):
        v = slots[...]
        n = float(nb * s.cells)
        mean = jnp.sum(v[:, 0:1, :], axis=0) / s.n_dev
        d = v[:, 0:1, :] - mean
        spread_sum = jnp.sum(v[:, 1:2, :] + n * d * d, axis=0)
        return mean, lax.rsqrt(spread_sum / s.count + epsilon)

    n1 = s.nch
    for u in range(n1):
        g_start(u)
    for u in turned:
        g_start(u)
    g_forward(0)
    for u in range(n1, 2 * n1):
        if u not in turned:
            g_start(u)
    for u in range(1, 2 * n1):
        g_forward(u)
    g_start(2 * n1)
    row, col = iota((s.long, s.line), 0), iota((s.long, s.line), 1)
    r.expand[...] = (col == lax.shift_right_logical(row, 2)).astype(f32).astype(bf16)
    r.out_r[s.rows :, :] = jnp.zeros((s.long - s.rows, ch), bf16)
    r.vu[s.rows :, :] = jnp.zeros((s.long - s.rows, 2 * ch), bf16)
    r.xt[...] = jnp.transpose(r.x3[br : br + s.rows, ch : 2 * ch])
    for u in range(n1):
        g_cross(u)

    def conv_part(planes, weight, di, out):
        v = dot(planes[br * di : br * di + s.rows, :], weight[di])
        out[0 : s.rows, :] = v if di == 0 else out[0 : s.rows, :] + v

    chunk = s.long // 3

    def conv(planes, weight, out):
        def one(k, _):
            at = pl.multiple_of(k * chunk, 16)
            v = dot(planes[pl.ds(at, chunk), :], weight[0])
            v = v + dot(planes[pl.ds(at + br, chunk), :], weight[1])
            out[pl.ds(at, chunk), :] = v + dot(planes[pl.ds(at + 2 * br, chunk), :], weight[2])
            return 0

        lax.fori_loop(0, 3, one, 0)

    for part in range(n1):
        g_done(part)
        unpack(r.s1, part, r.wt1)
        if s.fast:
            conv_part(r.x3, r.wt1, part, r.h1)
    if not s.fast:
        conv(r.x3, r.wt1, r.h1)
    local_stats(r.h1, r.st1)
    x_send(0, r.st1, r.t1)

    g_forward(2 * n1)
    unpack_small()
    fetch["cot"].wait()

    def flip(weight, back):
        def one(n, _):
            di, dj = lax.div(n, 3), lax.rem(n, 3)
            tap = weight[2 - di, pl.ds(pl.multiple_of((2 - dj) * ch, ch), ch), :]
            back[di, pl.ds(pl.multiple_of(dj * ch, ch), ch), :] = jnp.transpose(tap)
            return 0

        lax.fori_loop(0, 9, one, 0)

    for u in range(n1, 2 * n1):
        g_cross(u)
    flip(r.wt1, r.wb1)

    gain1, gain2 = r.pars[0:1, :], r.pars[1:2, :]
    shift1, shift2 = r.pars[2:3, :], r.pars[3:4, :]
    hc0, hc1 = r.pars[4:5, :], r.pars[5:6, :]

    x_wait(0, r.t1)
    mean1, inv1 = global_stats(r.t1)

    def act1(i, _):
        n = (r.h1[rows_of(i), :] - mean1) * (inv1 * gain1) + shift1
        a = gelu(n)
        store3(r.a3, i, jnp.where(inside, a, 0.0))
        return 0

    lax.fori_loop(0, s.side, act1, 0)
    for u in range(n1, 2 * n1):
        g_done(u)
        unpack(r.s2, u - n1, r.wt2)
    conv(r.a3, r.wt2, r.h2)
    local_stats(r.h2, r.st2)
    x_send(1, r.st2, r.t2)

    r.at[...] = jnp.transpose(r.a3[br : br + s.rows, ch : 2 * ch])

    def slope1(i, _):
        n = (r.h1[rows_of(i), :] - mean1) * (inv1 * gain1) + shift1
        r.back1[rows_of(i), :] = gelu_both(n)[1]
        return 0

    lax.fori_loop(0, s.side, slope1, 0)
    g_cross(2 * n1)
    g_done(2 * n1)
    at = iota((s.line, 1), 0)
    i_of = divided(at, wide, s.line)
    j_of = at - i_of * wide
    used = (i_of < s.side) & (j_of < s.side)
    wide_slots = s.n_dev * s.rp
    shard_rows = iota((s.line, wide_slots), 1)
    dense_all = r.sd[...].reshape(wide_slots, s.mp)
    for k in range(2):
        source = k * s.cells + i_of * s.side + j_of
        if k == 0:
            source = jnp.where(at == s.side, s.head_in, source)
            wanted = used | (at == s.side)
        else:
            wanted = used
        source = jnp.where(wanted, source, 0)
        shard = divided(source, s.rsh, 1024)
        place = jnp.where(wanted, shard * s.rp + (source - shard * s.rsh), -1)
        pick = (shard_rows == place).astype(f32).astype(bf16)
        r.dk[k] = dot(pick, dense_all).astype(bf16)
    row = iota((16, ch), 0)
    hc_rows = jnp.where(row == 0, hc0, jnp.where(row == 1, hc1, 0.0)).astype(bf16)

    x_wait(1, r.t2)
    mean2, inv2 = global_stats(r.t2)

    def act2(i, _):
        at = rows_of(i)
        xin = r.x3[pl.ds(pl.multiple_of((i + 1) * br, 16), br), ch : 2 * ch].astype(f32)
        z = xin + ((r.h2[at, :] - mean2) * (inv2 * gain2) + shift2)
        r.dz[at, :] = z
        a = jnp.where(inside, gelu(z), 0.0)
        r.out_r[at, :] = a.astype(bf16)
        r.out_v[i] = to_board(a)
        return 0

    lax.fori_loop(0, s.side, act2, 0)
    put_out = pltpu.make_async_copy(r.out_v, r.out, r.local_sem.at[len(names)])
    put_out.start()
    p_long = dot_nt(hc_rows, r.out_r[...])[0:8]
    lane = iota((8, s.long), 1)
    lane_j = lane - divided(lane, br, s.long) * br
    valid_long = (lane_j < nb * s.side) & (lane < s.rows)
    row1, lane1 = iota((8, lanes), 0), iota((8, lanes), 1)

    def by_head(v):
        a = v[0:1] + v[1:2] + v[2:3] + v[3:4]
        b = v[4:5] + v[5:6] + v[6:7] + v[7:8]
        return jnp.where(iota(v.shape, 0) < nb, a, b)

    n_local = float(nb * s.cells)
    mean_row = jnp.sum(jnp.where(valid_long, p_long, 0.0), axis=1, keepdims=True) / n_local
    dev = jnp.where(valid_long, p_long - mean_row, 0.0)
    square_row = jnp.sum(dev * dev, axis=1, keepdims=True)
    lane3 = iota((1, lanes), 1)
    means = jnp.where(lane3 < 32, mean_row[0:1], mean_row[1:2])
    r.st3[...] = jnp.where(lane3 < 64, means, jnp.where(lane3 < 96, square_row[0:1], square_row[1:2]))
    x_send(2, r.st3, r.t3)

    for name in names[8:]:
        fetch[name].wait()
    r.legal_both[...] = jnp.zeros_like(r.legal_both)
    r.legal_both[0:nb, 0 : s.moves] = r.legal_v[...]
    r.legal_both[nb : 2 * nb, 0 : s.moves] = r.legal_v[...]

    def slope2(i, carry):
        at = rows_of(i)
        slope = jnp.where(inside, gelu_both(r.dz[at, :])[1], 0.0)
        r.dz[at, :] = slope
        scaled = slope * ((r.h2[at, :] - mean2) * inv2)
        r.vu[at, 0:ch] = slope.astype(bf16)
        r.vu[at, ch:] = scaled.astype(bf16)
        cot = from_board(r.cot_v[i])
        a = (cot * scaled).reshape(br // 8, 8, ch)
        b = (cot * slope).reshape(br // 8, 8, ch)
        return carry[0] + jnp.sum(a, axis=0), carry[1] + jnp.sum(b, axis=0)

    zero = jnp.zeros((8, ch), f32)
    cot_g, cot_s = lax.fori_loop(0, s.side, slope2, (zero, zero))
    cot_g, cot_s = jnp.sum(cot_g, axis=0, keepdims=True), jnp.sum(cot_s, axis=0, keepdims=True)
    row = iota((16, s.long), 0)
    centred = jnp.where(valid_long[0:1], p_long[0:2] - mean_row[0:2], 0.0)
    against = jnp.where(
        row == 0, jnp.where(valid_long[0:1], 1.0, 0.0), jnp.where(row == 1, centred[0:1], jnp.where(row == 2, centred[1:2], 0.0))
    ).astype(bf16)
    early = dot(against, r.vu[...])
    for half in range(2):
        part = early[:, half * ch : (half + 1) * ch]
        ones = part[0:1]
        r.ste[4 * half : 4 * half + 1, :] = ones
        r.ste[4 * half + 1 : 4 * half + 2, :] = part[1:2] + mean_row[0:1] * ones
        r.ste[4 * half + 2 : 4 * half + 3, :] = part[2:3] + mean_row[1:2] * ones
        r.ste[4 * half + 3 : 4 * half + 4, :] = jnp.zeros((1, ch), f32)
    plane_send(3, r.ste, r.te)
    row = iota((8, s.long), 0)
    wanted = (lane & (nb - 1)) == (row & (nb - 1))
    rest = jnp.where(wanted, jnp.where(row < nb, p_long[0:1], p_long[1:2]), 0.0)
    parts = []
    for _ in range(3):
        part = rest.astype(bf16).astype(f32)
        parts.append(part)
        rest = rest - part
    parts = jnp.concatenate(parts + [jnp.zeros_like(rest)], axis=0).astype(bf16)
    p8 = dot(parts, r.expand[...])
    p8 = p8[0:8] + p8[8:16] + p8[16:24]
    row = iota((8, s.line), 0)
    lane = iota((8, s.line), 1)
    lane_i = divided(lane, wide, s.line)
    valid = (lane_i < s.side) & (lane - lane_i * wide < s.side)
    first_head = row < nb

    x_wait(2, r.t3)
    v = r.t3[...]
    mean_k = jnp.sum(v, axis=0) / float(s.n_dev)
    dev = v - mean_k
    squares = jnp.sum(jnp.where(lane3 < 64, n_local * dev * dev, v), axis=0)

    def of_head(v, at):
        return jnp.where(iota((8, 1), 0) < nb, v[:, at : at + 1], v[:, at + 32 : at + 33])

    mean_long = jnp.concatenate([mean_k[:, 0:1], mean_k[:, 32:33]], axis=0)
    mean_p = of_head(mean_k, 0)
    squares = of_head(squares, 0) + of_head(squares, 64)
    inv_p = lax.rsqrt(squares / s.count + epsilon)
    inv_long = jnp.concatenate([inv_p[0:1], inv_p[nb : nb + 1]], axis=0)
    gain_p = jnp.where(iota((8, 1), 0) < nb, r.hng_v[0], r.hng_v[1])
    shift_p = jnp.where(iota((8, 1), 0) < nb, r.hns_v[0], r.hns_v[1])
    xhat_p = (p8 - mean_p) * inv_p
    feature, back_p = gelu_both(xhat_p * gain_p + shift_p)
    flat = jnp.where(valid, feature, 0.0).astype(bf16)
    one_lane = first_head & (lane == s.side)
    flat_f = flat.astype(f32)
    lhs0 = jnp.where(one_lane, 1.0, jnp.where(first_head, flat_f, 0.0))
    lhs1 = jnp.where(first_head, 0.0, flat_f)
    pad8 = jnp.zeros((8, s.line), f32)

    def tall(v):
        return jnp.concatenate([v, pad8[:, : v.shape[1]]], axis=0).astype(bf16)

    half = (dot(tall(lhs0), r.dk[0]) + dot(tall(lhs1), r.dk[1]))[0:8]
    logits = half + pltpu.roll(half, nb, 0)
    move = iota((8, s.mp), 1)
    masked = jnp.where(r.legal_both[...] == 1, logits, negative_fill)
    top = jnp.max(masked, axis=1, keepdims=True)
    terms = jnp.exp(masked - top)
    total = jnp.sum(terms, axis=1, keepdims=True)
    row_b = iota((8, 1), 0) & (nb - 1)
    target = jnp.where(
        row_b < 2,
        jnp.where(row_b == 0, r.target_v[0], r.target_v[1]),
        jnp.where(row_b == 2, r.target_v[2], r.target_v[3]),
    )
    chosen = move == target
    picked = jnp.sum(jnp.where(chosen, logits, 0.0), axis=1, keepdims=True)
    ce = top + jnp.log(total) - picked
    dl = (terms / total - chosen.astype(f32)).astype(bf16).astype(f32)
    first_move = iota((8, s.mp), 0) < nb
    dq = dot_nt(tall(jnp.where(first_move, dl, 0.0)), r.dk[0]) + dot_nt(
        tall(jnp.where(first_move, 0.0, dl)), r.dk[1]
    )
    dnh = jnp.where(valid, dq[0:8] * back_p, 0.0)
    gain_row = jnp.sum(dnh * xhat_p, axis=1, keepdims=True)
    shift_row = jnp.sum(dnh, axis=1, keepdims=True)
    scale_p = gain_p * inv_p
    long_row, long_lane = iota((8, s.long), 0), iota((8, s.long), 1)
    dnh_long = dot_nt(tall(dnh), r.expand[...])[0:8]
    dnh_long = jnp.where((long_lane & (nb - 1)) == (long_row & (nb - 1)), dnh_long, 0.0)
    late = dot(jnp.concatenate([dnh_long, jnp.zeros_like(dnh_long)], axis=0).astype(bf16), r.vu[...])[0:8]
    head_rows = jnp.where(iota((8, ch), 0) < nb, hc0, hc1) * scale_p
    late_s = jnp.sum(late[:, 0:ch] * head_rows, axis=0, keepdims=True)
    late_g = jnp.sum(late[:, ch:] * head_rows, axis=0, keepdims=True)
    r.st5[0:1, :] = cot_g + late_g
    r.st5[1:2, :] = cot_s + late_s

    def heads(v):
        return v[0:1] + v[1:2] + v[2:3] + v[3:4], v[4:5] + v[5:6] + v[6:7] + v[7:8]

    gain_heads, shift_heads, ce_sum = heads(gain_row), heads(shift_row), heads(ce)[0]
    lane5 = iota((1, ch), 1)
    low = jnp.where(lane5 < 32, gain_heads[0], gain_heads[1])
    high = jnp.where(lane5 < 96, shift_heads[0], shift_heads[1])
    r.st5[2:3, :] = jnp.where(lane5 < 64, low, jnp.where(lane5 < 128, high, ce_sum))
    x_send(4, r.st5, r.t5)
    group_wait(3, r.te)
    r.stl[...] = jnp.sum(r.te[...], axis=0)
    line_send(7, r.stl, r.tl)
    r.fd_own[...] = jnp.zeros_like(r.fd_own)
    r.fd_own[0:8, :] = flat_f
    r.fd_own[8:16, 0 : s.mp] = dl
    r.fd[gx, q, c] = r.fd_own[...].astype(bf16)
    g_start(2 * n1 + 1)
    flip(r.wt2, r.wb2)
    scaled_long = dnh_long * scale_p
    dnh_heads = [jnp.sum(scaled_long[nb * k : nb * k + nb], axis=0, keepdims=True) for k in range(2)]
    xhat_long = (p_long[0:2] - mean_long) * inv_long
    xhat_long = jnp.where(valid_long[0:1], xhat_long, 0.0)
    row = iota((16, s.long), 0)
    terms_long = jnp.where(valid_long[0:1], 1.0, 0.0)
    for n, value in ((0, dnh_heads[0]), (1, dnh_heads[1]), (3, xhat_long[0:1]), (4, xhat_long[1:2])):
        terms_long = jnp.where(row == n, value, terms_long)
    terms_long = jnp.where(row < 5, terms_long, 0.0)
    r.terms[...] = terms_long.astype(bf16)
    tall_terms = jnp.concatenate([terms_long, jnp.zeros((lanes - 16, s.long), f32)], axis=0)
    r.terms_t[...] = jnp.transpose(tall_terms).astype(bf16)
    x_wait(4, r.t5)
    group_wait(7, r.tl)
    te = jnp.sum(r.tl[...], axis=0)
    t5 = jnp.sum(r.t5[...], axis=0)
    sums = t5[2:3]
    gain_sums, shift_sums = (sums[:, 0:1], sums[:, 32:33]), (sums[:, 64:65], sums[:, 96:97])
    r.tiny[0:1, :] = jnp.broadcast_to(sums[:, 128:129] / float(nb * s.n_dev), (1, lanes))
    first_lane = iota((1, lanes), 1) == 0
    r.tiny[1:2, :] = jnp.where(first_lane, *gain_sums)
    r.tiny[2:3, :] = jnp.where(first_lane, *shift_sums)
    g2s, s2s = t5[0:1], t5[1:2]
    for k in range(2):
        weight = (hc0, hc1)[k] * (scale_p[nb * k : nb * k + 1] / s.count)
        gain_part = gain_sums[k] * inv_p[nb * k : nb * k + 1]
        mean_k = mean_p[nb * k : nb * k + 1]
        s2s = s2s - weight * (shift_sums[k] * te[0:1] + gain_part * (te[k + 1 : k + 2] - mean_k * te[0:1]))
        g2s = g2s - weight * (shift_sums[k] * te[4:5] + gain_part * (te[k + 5 : k + 6] - mean_k * te[4:5]))
    scales = [scale_p[nb * k : nb * k + 1] / s.count for k in range(2)]
    ones_of = [shift_sums[k] * scales[k] for k in range(2)]
    xhat_of = [gain_sums[k] * scales[k] for k in range(2)]

    row = iota((lanes, ch), 0)
    mix = jnp.where(row == 0, hc0, jnp.where(row == 1, hc1, 0.0))
    mix = jnp.where(row == 2, -(hc0 * ones_of[0] + hc1 * ones_of[1]), mix)
    mix = jnp.where(row == 3, -hc0 * xhat_of[0], jnp.where(row == 4, -hc1 * xhat_of[1], mix))
    r.up[...] = dot(r.terms_t[...], mix.astype(bf16))

    def sums_back(field, xhat, carry):
        f = field.reshape(br // 8, 8, ch)
        g = (field * xhat).reshape(br // 8, 8, ch)
        return carry[0] + jnp.sum(g, axis=0), carry[1] + jnp.sum(f, axis=0)

    def to_field2(i, _):
        at = rows_of(i)
        xhat = (r.h2[at, :] - mean2) * inv2
        dz = (from_board(r.cot_v[i]) + r.up[at, :]) * r.dz[at, :]
        r.dz[at, :] = dz
        d = (gain2 * inv2) * (dz - (s2s + xhat * g2s) * (1.0 / s.count))
        store3(r.d3, i, jnp.where(inside, d, 0.0))
        return 0

    lax.fori_loop(0, s.side, to_field2, 0)

    def wgrad(planes_t, di):
        start = 2 * br - br * di
        return dot(planes_t[...], r.d3[start : start + s.rows, :])

    early = 1 if s.fast else 0
    for di in range(early):
        rs_fill(di, wgrad(r.at, di), rs2)
        rs_cross(rs2, di)
    g_forward(2 * n1 + 1)
    conv(r.d3, r.wb2, r.h2)

    def back1(i, carry):
        at = rows_of(i)
        dn = jnp.where(inside, r.h2[at, :] * r.back1[at, :], 0.0)
        r.h2[at, :] = dn
        return sums_back(dn, (r.h1[at, :] - mean1) * inv1, carry)

    g1, s1 = lax.fori_loop(0, s.side, back1, (zero, zero))
    r.st6[0:1, :] = jnp.sum(g1, axis=0, keepdims=True)
    r.st6[1:2, :] = jnp.sum(s1, axis=0, keepdims=True)
    x_send(5, r.st6, r.t6)
    against_out = dot(r.terms[...], r.out_r[...])
    for k in range(2):
        r.sth[k : k + 1, :] = (
            against_out[k : k + 1] - ones_of[k] * against_out[2:3] - xhat_of[k] * against_out[k + 3 : k + 4]
        )
    x_send(6, r.sth, r.th)
    for part in range(early):
        rs_plane(rs2, part)
    for di in range(early, 3):
        rs_fill(di, wgrad(r.at, di), rs2)
        if s.fast:
            rs_cross(rs2, di)
    rs_fill_rest(rs2)
    if not s.fast:
        rs_cross(rs2, 0)
    for part in range(early, s.nch - 1):
        rs_plane(rs2, part)
    g_cross(2 * n1 + 1)
    x_wait(5, r.t6)
    t6 = jnp.sum(r.t6[...], axis=0)
    g1s, s1s = t6[0:1], t6[1:2]

    def to_field1(i, _):
        at = rows_of(i)
        xhat = (r.h1[at, :] - mean1) * inv1
        d = (gain1 * inv1) * (r.h2[at, :] - (s1s + xhat * g1s) * (1.0 / s.count))
        store3(r.d3, i, jnp.where(inside, d, 0.0))
        return 0

    rs_plane(rs2, s.nch - 1)
    lax.fori_loop(0, s.side, to_field1, 0)
    for di in range(3):
        rs_fill(di, wgrad(r.xt, di), rs1)
        if s.fast:
            rs_cross(rs1, di)
            if di:
                rs_plane(rs1, di - 1)
    rs_fill_rest(rs1)
    if not s.fast:
        rs_cross(rs1, 0)
    rs_plane(rs1, s.nch - 1)
    conv(r.d3, r.wb1, r.h1)
    for part in range(s.nch):
        rs_line(rs2, part)

    def result(i, _):
        at = rows_of(i)
        r.in_grad_v[i] = to_board(r.dz[at, :] + r.h1[at, :])
        return 0

    lax.fori_loop(0, s.side, result, 0)
    put_in_grad = pltpu.make_async_copy(r.in_grad_v, r.in_grad, r.local_sem.at[len(names) + 1])
    put_in_grad.start()
    x_wait(6, r.th)
    shares = jnp.concatenate([g1s, g2s, s1s, s2s, jnp.sum(r.th[...], axis=0), jnp.zeros((2, ch), f32)], axis=0)
    r.tiny[8:16, :] = pltpu.roll(shares, lax.rem(ch - w * me, ch), 1)[:, 0:lanes]

    for part in range(s.nch):
        rs_line(rs1, part)

    g_done(2 * n1 + 1)
    fd = r.fd[...].astype(f32).reshape(s.n_dev, 16, s.line)
    features = fd[:, 0:8, :].reshape(8 * s.n_dev, s.line).astype(bf16)
    dls = fd[:, 8:16, 0 : s.mp].reshape(8 * s.n_dev, s.mp).astype(bf16)
    t = iota((s.rp, 1), 0)
    source = s.rsh * me + t
    mine = (t < s.rsh) & (source < s.head_in)
    col = iota((s.rp, s.line), 1)
    col8 = iota((s.rp, 8 * s.n_dev), 1) & 7
    own = jnp.where((t < s.rsh) & (source == s.head_in) & (col8 < nb), 1.0, 0.0)
    for k in range(2):
        in_k = mine & (source >= k * s.cells) & (source < (k + 1) * s.cells)
        cell = jnp.where(in_k, source - k * s.cells, 0)
        cell_i = divided(cell, s.side, s.cells)
        place = jnp.where(in_k, cell_i * wide + (cell - cell_i * s.side), -1)
        pick = (col == place).astype(f32).astype(bf16)
        rows_k = dot_nt(pick, features)
        own = own + jnp.where((col8 >= nb) if k else (col8 < nb), rows_k, 0.0)
    grad = dot(own.astype(bf16), dls)
    r.dense_grad[...] = grad

    for part in range(s.nch):
        rs_finish(rs2, part, r.c2_grad)
    for part in range(s.nch):
        rs_finish(rs1, part, r.c1_grad)

    for u in range(len(units)):
        g_drain(u)
    for number, slots in enumerate((r.t1, r.t2, r.t3, None, r.t5, r.t6, r.th)):
        if number != 3:
            x_drain(number, slots)
    group_wait(3, r.te, 0)
    group_wait(7, r.tl, 0)
    rs_drain(rs1)
    rs_drain(rs2)
    put_out.wait()
    put_in_grad.wait()


def place(w, x_ref, in_x_ref, c1, c2, dense, tiny, *refs):
    (out, loss, in_grad, c1_out, c2_out, gains, shifts, hc, hng, dense_out), refs = refs[:10], refs[10:]
    (out_v, in_v, c1_v, c2_v, dense_v, tiny_v), (came, went) = refs[:6], refs[6:]
    sources, held = (tiny, dense, c1, c2, x_ref, in_x_ref), (tiny_v, dense_v, c1_v, c2_v, out_v, in_v)
    fetch = [pltpu.make_async_copy(a, b, came.at[i]) for i, (a, b) in enumerate(zip(sources, held))]
    put = [
        pltpu.make_async_copy(a, b, went.at[i])
        for i, (a, b) in enumerate(((c1_v, c1_out), (c2_v, c2_out), (out_v, out), (in_v, in_grad)))
    ]
    for copy in fetch:
        copy.start()
    for i in range(4):
        fetch[i + 2].wait()
        put[i].start()
    fetch[0].wait()
    fetch[1].wait()
    loss[...] = tiny_v[0:1, 0:1]
    hng[...] = tiny_v[1:3, 0:2]
    gains[...] = tiny_v[8:10, 0:w]
    shifts[...] = tiny_v[10:12, 0:w]
    hc[...] = tiny_v[12:14, 0:w]
    dense_out[...] = dense_v[0 : dense_out.shape[0], 0 : dense_out.shape[1]]
    for copy in put:
        copy.wait()


def body(x, w1, w2, gains, shifts, hc, hng, hns, dense, legal, target, cot):
    x, cot = (jnp.transpose(v, (1, 2, 0, 3)) for v in (x, cot))
    s = sizes_of(lax.axis_size("gx"), lax.axis_size("gy"), x, w1, dense, legal.shape[1])
    vmem, hbm = pltpu.VMEM, pl.ANY
    inputs = dict(
        x=x, w1=w1, w2=w2, gains=gains, shifts=shifts, hc=hc, hng=hng, hns=hns, dense=dense, legal=legal,
        target=target, cot=cot,
    )
    outputs = dict(
        out=(x.shape, bf16), in_grad=(x.shape, bf16), c1_grad=(w1.shape, f32), c2_grad=(w2.shape, f32),
        dense_grad=((s.rp, s.mp), f32), tiny=((16, lanes), f32),
    )
    gxn, qn, n, ch = s.gx_n, s.q_n, s.n_dev, s.ch
    field = pltpu.VMEM((s.long, ch), f32)
    boards = pltpu.VMEM((s.side, s.wide, s.nb, ch), bf16)
    planes = pltpu.VMEM((s.padded, 3 * ch), bf16)
    turned = pltpu.VMEM((ch, s.rows), bf16)
    weight = pltpu.VMEM((3, 3 * ch, ch), bf16)
    two = pltpu.VMEM((2, ch), f32)
    eight = pltpu.VMEM((8, ch), f32)
    dma = pltpu.SemaphoreType.DMA
    scratch = dict(
        local_sem=dma((14,)), g_sem=dma((2 * s.nch + 2, 5 + gxn)), x_sem=dma((8, 2)),
        rs_sem1=dma((s.nch, 6)), rs_sem2=dma((s.nch, 6)),
        x_v=boards, cot_v=boards, out_v=pltpu.VMEM(x.shape, bf16), in_grad_v=pltpu.VMEM(x.shape, bf16),
        stage=pltpu.VMEM((s.blk1, lanes), f32), small=pltpu.VMEM((8, lanes), f32),
        s1=pltpu.VMEM((gxn, qn, 2, s.blk1, lanes), bf16), s2=pltpu.VMEM((gxn, qn, 2, s.blk, lanes), bf16),
        sd=pltpu.VMEM((gxn, qn, 2, s.rp, s.mp), bf16), dense_f=pltpu.VMEM((s.rp, s.mp), f32),
        x3=planes, a3=planes, d3=planes, out_r=pltpu.VMEM((s.long, ch), bf16), terms=pltpu.VMEM((16, s.long), bf16), terms_t=pltpu.VMEM((s.long, lanes), bf16),
        xt=turned, at=turned, wt1=weight, wt2=weight, wb1=weight, wb2=weight,
        pars=pltpu.VMEM((8, ch), f32), h1=field, h2=field, dz=field, back1=field, up=field,
        st1=two, t1=pltpu.VMEM((n, 2, ch), f32), st2=two, t2=pltpu.VMEM((n, 2, ch), f32),
        st3=pltpu.VMEM((1, lanes), f32), t3=pltpu.VMEM((n, 1, lanes), f32), ste=eight, te=pltpu.VMEM((s.gy_n, 8, ch), f32), stl=eight, tl=pltpu.VMEM((gxn, 8, ch), f32),
        st5=pltpu.VMEM((3, ch), f32), t5=pltpu.VMEM((n, 3, ch), f32), st6=two, t6=pltpu.VMEM((n, 2, ch), f32),
        sth=two, th=pltpu.VMEM((n, 2, ch), f32), vu=pltpu.VMEM((s.long, 2 * ch), bf16),
        fd_own=pltpu.VMEM((16, s.line), f32), fd=pltpu.VMEM((gxn, qn, 2, 16, s.line), bf16),
        dk=pltpu.VMEM((2, s.line, s.mp), bf16), expand=pltpu.VMEM((s.long, s.line), bf16),
        legal_both=pltpu.VMEM((8, s.mp), jnp.int32),
    )
    for name in ("w1", "w2", "gains", "shifts", "hc", "dense", "legal"):
        scratch[name + "_v"] = pltpu.VMEM(inputs[name].shape, inputs[name].dtype)
    for name in ("hng", "hns", "target"):
        scratch[name + "_v"] = pltpu.SMEM(inputs[name].shape, inputs[name].dtype)
    if not s.fast:
        scratch["flat"] = pltpu.VMEM((9, ch, ch), f32)
        scratch["eight"] = pltpu.VMEM((9, 8, ch), f32)
    for number in ("1", "2"):
        scratch["rsb" + number] = pltpu.VMEM((s.nch, 2, gxn, qn, s.crows, lanes), bf16)
        scratch["rc" + number] = pltpu.VMEM((s.nch, gxn, qn, s.crows, lanes), bf16)
        scratch["pb" + number] = pltpu.VMEM((s.nch, qn, gxn, s.crows, lanes), bf16)
        scratch["rp" + number] = pltpu.VMEM((s.nch, qn - 1, gxn, s.crows, lanes), bf16)
        scratch["zb" + number] = pltpu.VMEM((s.nch, gxn, s.crows, lanes), bf16)
        scratch["rd" + number] = pltpu.VMEM((gxn * qn - 1, s.crows, lanes), bf16)
        scratch["rz" + number] = pltpu.VMEM((s.nch, gxn - 1, s.crows, lanes), bf16)
    run = pl.pallas_call(
        functools.partial(kernel, s, tuple(inputs), tuple(outputs), tuple(scratch)),
        out_shape=[jax.ShapeDtypeStruct(shape, kind) for shape, kind in outputs.values()],
        in_specs=[pl.BlockSpec(memory_space=hbm) for _ in inputs],
        out_specs=[pl.BlockSpec(memory_space=hbm if n in ("out", "in_grad") else vmem) for n in outputs],
        scratch_shapes=list(scratch.values()),
        compiler_params=pltpu.CompilerParams(
            collective_id=0, has_side_effects=True, vmem_limit_bytes=60 * 1024 * 1024
        ),
        cost_estimate=pl.CostEstimate(flops=10_500_000_000, bytes_accessed=8_000_000, transcendentals=800_000),
        name="tower",
    )
    results = run(*inputs.values())
    kinds = [jax.ShapeDtypeStruct(v.shape, v.dtype) for v in results]
    out, in_grad, c1_grad, c2_grad, dense_grad, _ = kinds
    small = [jax.ShapeDtypeStruct(v.shape, f32) for v in (gains, shifts, hc)]
    loss, pair = (jax.ShapeDtypeStruct(shape, f32) for shape in ((1, 1), (2, 2)))
    shapes = [out, loss, in_grad, c1_grad, c2_grad, *small, pair, jax.ShapeDtypeStruct(dense.shape, f32)]
    results = pl.pallas_call(
        functools.partial(place, s.w),
        out_shape=shapes,
        in_specs=[pl.BlockSpec(memory_space=hbm) for _ in kinds],
        out_specs=[pl.BlockSpec(memory_space=hbm if n in (0, 2, 3, 4) else vmem) for n in range(len(shapes))],
        scratch_shapes=[pltpu.VMEM(v.shape, v.dtype) for v in kinds] + [dma((len(kinds),))] * 2,
        name="place",
    )(*results)
    out, loss, in_grad, *rest = results
    out, in_grad = (jnp.transpose(v, (2, 0, 1, 3)) for v in (out, in_grad))
    return (out, loss.reshape(()), in_grad, *rest)


def solution(mesh):
    both = ("gx", "gy")
    board = P(both, None, None, None)
    kernels = P(None, both, None)
    pairs = P(None, both)
    return jax.shard_map(
        body,
        mesh=mesh,
        in_specs=(
            board, kernels, kernels, pairs, pairs, pairs, P(), P(), P(both, None), P(both, None), P(both), board,
        ),
        out_specs=(board, P(), board, kernels, kernels, pairs, pairs, pairs, P(), P(both, None)),
        check_vma=False,
    )
```

```python
import functools
import types

import jax
import jax.numpy as jnp
from jax import lax
from jax.experimental import pallas as pl
from jax.experimental.pallas import tpu as pltpu
from jax.sharding import PartitionSpec as P

MESH = pl.DeviceIdType.MESH
f32 = jnp.float32
bf16 = jnp.bfloat16
epsilon = 1e-05
negative_fill = -1e30
root = 0.7978845608028654
cube = 0.044715
lanes = 128


def up_to(value, unit):
    return -(-value // unit) * unit


def divided(values, divisor, limit):
    for shift in range(16, 24):
        factor = -(-(1 << shift) // divisor)
        if all((n * factor) >> shift == n // divisor and n * factor < 2**31 for n in range(limit)):
            return lax.shift_right_logical(values * factor, jnp.int32(shift))
    raise ValueError("no factor")


def iota(shape, axis):
    return lax.broadcasted_iota(jnp.int32, shape, axis)


def gelu_both(v):
    square = v * v
    slope = jnp.tanh(v * (root + (root * cube) * square))
    half = 0.5 + 0.5 * slope
    back = half + (0.5 * v) * (1.0 - slope * slope) * (root + (3.0 * root * cube) * square)
    return v * half, back


def gelu(v):
    half = 0.5 * v
    return half + half * jnp.tanh(v * (root + (root * cube) * (v * v)))


def dot(left, right):
    return jnp.dot(left, right, preferred_element_type=f32)


def dot_nt(left, right):
    return lax.dot_general(left, right, (((1,), (1,)), ((), ())), preferred_element_type=f32)


def sizes_of(gx_n, gy_n, x, w1, dense, moves):
    s = types.SimpleNamespace()
    s.gx_n, s.gy_n, s.q_n, s.n_dev = gx_n, gy_n, gy_n // 2, gx_n * gy_n
    s.side, s.nb, s.ch = x.shape[0], x.shape[2], x.shape[3]
    s.w = w1.shape[1]
    s.wide = s.side + 1
    s.br = s.wide * s.nb
    s.rows = s.side * s.br
    s.line = up_to(s.side * s.wide, lanes)
    s.long = up_to(s.rows, 3 * lanes)
    s.padded = s.long + 2 * s.br
    s.cells = s.side * s.side
    s.moves = moves
    s.mp = up_to(moves, lanes)
    s.rsh = dense.shape[0]
    s.rp = up_to(s.rsh, 16)
    s.head_in = 2 * s.cells
    s.blk = up_to(18 * s.w, 16)
    s.blk1 = up_to(19 * s.w, 16)
    s.fast = s.w == 8
    s.nch = 3 if s.fast else 1
    s.crows = s.blk // s.nch
    s.count = float(s.nb * s.cells * s.n_dev)
    assert s.nb == 4 and s.br % 16 == 0 and 8 % s.w == 0
    assert gx_n & (gx_n - 1) == 0 and gy_n & (gy_n - 1) == 0 and gy_n > 1
    return s


def kernel(s, in_names, out_names, scratch_names, *refs):
    r = types.SimpleNamespace(**dict(zip(in_names + out_names + scratch_names, refs)))
    gx, gy = lax.axis_index("gx"), lax.axis_index("gy")
    q, c = lax.div(gy, 2), lax.rem(gy, 2)
    me = gx * s.gy_n + gy
    other = (gx, gy + 1 - 2 * c)
    gxn, qn, nb, br, wide, ch = s.gx_n, s.q_n, s.nb, s.br, s.wide, s.ch

    def z_peer(k):
        return gx ^ k

    def q_peer(j):
        return q ^ j

    def send(src, dst, out_sem, in_sem, device):
        pltpu.make_async_remote_copy(
            src_ref=src, dst_ref=dst, send_sem=out_sem, recv_sem=in_sem, device_id=device, device_id_type=MESH
        ).start()

    def take(sem, ref):
        pltpu.make_async_copy(ref, ref, sem).wait()

    barrier = pltpu.get_barrier_semaphore()
    partners = [(z_peer(k), gy) for k in range(1, gxn)]
    partners += [(gx, 2 * q_peer(j) + c) for j in range(1, qn)]
    partners += [other]
    for p in partners:
        pl.semaphore_signal(barrier, inc=1, device_id=p, device_id_type=MESH)
    names = ("x", "w1", "w2", "gains", "shifts", "hc", "dense", "cot", "legal", "hng", "hns", "target")
    fetch = {}
    for n, name in enumerate(names):
        held = getattr(r, name + "_v")
        held = held.at[:, pl.ds(0, s.side)] if name in ("x", "cot") else held
        fetch[name] = pltpu.make_async_copy(getattr(r, name), held, r.local_sem.at[n])
        fetch[name].start()
    for fields in (r.x_v, r.cot_v):
        fields[:, s.side] = jnp.zeros((s.side, nb, ch), bf16)

    w = s.w

    def stage(weight):
        r.stage[...] = jnp.zeros_like(r.stage)
        for t in range(9):
            v = weight[t].astype(f32)
            r.stage[2 * w * t : 2 * w * t + w, :] = v[:, :lanes]
            r.stage[2 * w * t + w : 2 * w * t + 2 * w, :] = v[:, lanes:]

    def stage_all():
        for name in names[1:7]:
            fetch[name].wait()
        r.small[...] = jnp.zeros_like(r.small)
        r.small[0:2, 0:w] = r.gains_v[...].astype(f32)
        r.small[2:4, 0:w] = r.shifts_v[...].astype(f32)
        r.small[4:6, 0:w] = r.hc_v[...].astype(f32)
        stage(r.w1_v)
        r.stage[18 * w : 19 * w, 0:8] = jnp.transpose(r.small[...])[0:w, :]
        r.s1[gx, q, c] = r.stage[...].astype(bf16)
        stage(r.w2_v)
        r.s2[gx, q, c] = r.stage[0 : s.blk, :].astype(bf16)
        r.dense_f[...] = jnp.zeros_like(r.dense_f)
        r.dense_f[0 : s.rsh, 0 : s.moves] = r.dense_v[...].astype(f32)
        r.sd[gx, q, c] = r.dense_f[...].astype(bf16)

    for planes in (r.x3, r.a3, r.d3):
        planes[0:br, :] = jnp.zeros((br, 3 * ch), bf16)
        planes[br + s.rows :, :] = jnp.zeros((s.padded - br - s.rows, 3 * ch), bf16)
    inside = iota((br, ch), 0) < nb * s.side

    def store3(planes, i, block):
        at = pl.ds(pl.multiple_of((i + 1) * br, 16), br)
        planes[at, 0:ch] = pltpu.roll(block, nb, 0).astype(bf16)
        planes[at, ch : 2 * ch] = block.astype(bf16)
        planes[at, 2 * ch :] = pltpu.roll(block, br - nb, 0).astype(bf16)

    def rows_of(i):
        return pl.ds(pl.multiple_of(i * br, 16), br)

    def from_board(block):
        return block.astype(f32).reshape(br, ch)

    def to_board(block):
        return block.reshape(wide, nb, ch)[0 : s.side].astype(bf16)

    def x_rows(i, _):
        store3(r.x3, i, from_board(r.x_v[i]))
        return 0

    fetch["x"].wait()
    lax.fori_loop(0, s.side, x_rows, 0)
    stage_all()

    pl.semaphore_wait(barrier, len(partners))

    def span(unit):
        store, part = unit
        if store is r.sd or store is r.fd:
            return pl.ds(0, store.shape[3])
        whole = s.blk1 if store is r.s1 else s.blk
        if s.nch == 1:
            return pl.ds(0, whole)
        start = part * s.crows
        return pl.ds(start, whole - start if part == s.nch - 1 else s.crows)

    units = [(r.s1, p) for p in range(s.nch)] + [(r.s2, p) for p in range(s.nch)] + [(r.sd, 0), (r.fd, 0)]

    turned = {s.nch} if s.nch > 1 else set()

    def g_start(u):
        store, at = units[u][0], span(units[u])
        own = store.at[gx, q, c, at]
        for k in range(1, gxn):
            if u not in turned:
                send(own, own, r.g_sem.at[u, 0], r.g_sem.at[u, 5 + k], (z_peer(k), gy))
        for j in range(qn - 1, 0, -1):
            send(own, own, r.g_sem.at[u, 1], r.g_sem.at[u, 4], (gx, 2 * q_peer(j) + c))

    def g_forward(u):
        store, at = units[u][0], span(units[u])
        if u in turned:
            take(r.g_sem.at[u, 4], store.at[gx, pl.ds(0, qn - 1), 0, at])
            block = store.at[gx, :, c, at]
            for k in range(gxn - 1, 0, -1):
                send(block, block, r.g_sem.at[u, 2], r.g_sem.at[u, 5 + k], (z_peer(k), gy))
            return
        for k in range(1, gxn):
            block = store.at[z_peer(k), q, c, at]
            take(r.g_sem.at[u, 5 + k], block)
            for j in range(qn - 1, 0, -1):
                send(block, block, r.g_sem.at[u, 2], r.g_sem.at[u, 4], (gx, 2 * q_peer(j) + c))

    def g_cross(u):
        store, at = units[u][0], span(units[u])
        if u in turned:
            for k in range(1, gxn):
                take(r.g_sem.at[u, 5 + k], store.at[z_peer(k), :, c, at])
        else:
            take(r.g_sem.at[u, 4], store.at[:, pl.ds(0, qn - 1), 0, at])
        block = store.at[:, :, c, at]
        send(block, block, r.g_sem.at[u, 3], r.g_sem.at[u, 5], other)

    def g_done(u):
        store, at = units[u][0], span(units[u])
        take(r.g_sem.at[u, 5], store.at[:, :, 0, at])

    def g_drain(u):
        store, at = units[u][0], span(units[u])
        take(r.g_sem.at[u, 1], store.at[0, pl.ds(0, qn - 1), 0, at])
        if u in turned:
            take(r.g_sem.at[u, 2], store.at[pl.ds(0, gxn - 1), :, 0, at])
        else:
            take(r.g_sem.at[u, 0], store.at[pl.ds(0, gxn - 1), 0, 0, at])
            take(r.g_sem.at[u, 2], store.at[pl.ds(0, gxn - 1), pl.ds(0, qn - 1), 0, at])
        take(r.g_sem.at[u, 3], store.at[:, :, 0, at])

    def shard_of(store, d):
        return store[lax.div(d, s.gy_n), lax.div(lax.rem(d, s.gy_n), 2), lax.rem(d, 2)]

    def unpack(store, part, weight):
        if s.fast:
            for dj in range(3):
                at = 16 * (3 * part + dj)
                v = store[:, :, :, at : at + 16, :].astype(f32).reshape(s.n_dev, 16, lanes)
                low = v[:, 0:8, :].reshape(ch, lanes)
                high = v[:, 8:16, :].reshape(ch, lanes)
                weight[part, dj * ch : (dj + 1) * ch, :] = jnp.concatenate([low, high], axis=1).astype(bf16)
            return

        def one(g, _):
            for e in range(8 // w):
                r.stage[0 : s.blk, :] = shard_of(store, g * (8 // w) + e)[0 : s.blk].astype(f32)
                for t in range(9):
                    r.eight[t, w * e : w * e + w, 0:lanes] = r.stage[2 * w * t : 2 * w * t + w, :]
                    r.eight[t, w * e : w * e + w, lanes:] = r.stage[2 * w * t + w : 2 * w * t + 2 * w, :]
            for t in range(9):
                r.flat[t, pl.ds(pl.multiple_of(8 * g, 8), 8), :] = r.eight[t]
            return 0

        lax.fori_loop(0, ch // 8, one, 0)
        for t in range(9):
            weight[t // 3, (t % 3) * ch : (t % 3 + 1) * ch, :] = r.flat[t].astype(bf16)

    def unpack_small():
        if s.fast:
            v = r.s1[:, :, :, 18 * w : 18 * w + 16, :].astype(f32).reshape(s.n_dev, 16, lanes)
            rows = v[:, 0:8, :].reshape(ch, lanes)
        else:

            def one(g, _):
                for e in range(8 // w):
                    r.stage[...] = shard_of(r.s1, g * (8 // w) + e).astype(f32)
                    r.eight[0, w * e : w * e + w, 0:lanes] = r.stage[18 * w : 19 * w, :]
                r.flat[0, pl.ds(pl.multiple_of(8 * g, 8), 8), :] = r.eight[0]
                return 0

            lax.fori_loop(0, ch // 8, one, 0)
            rows = r.flat[0, :, 0:lanes]
        r.pars[...] = jnp.transpose(rows)[0:8, :]

    def x_send(number, src, slots):
        def one(k):
            device = (gx ^ lax.div(k, s.gy_n), gy ^ lax.rem(k, s.gy_n))
            send(src, slots.at[me], r.x_sem.at[number, 0], r.x_sem.at[number, 1], device)

        if s.n_dev <= 64:
            hops = {k: k // s.gy_n + bin(k % s.gy_n // 2).count("1") for k in range(1, s.n_dev)}
            for k in sorted(hops, key=lambda k: (-hops[k], k)):
                send(
                    src, slots.at[me], r.x_sem.at[number, 0], r.x_sem.at[number, 1],
                    (gx ^ (k // s.gy_n), gy ^ (k % s.gy_n)),
                )
        else:
            lax.fori_loop(0, s.n_dev - 1, lambda n, _: (one(s.n_dev - 1 - n), 0)[1], 0)
        slots[me] = src[...]

    def x_wait(number, slots):
        take(r.x_sem.at[number, 1], slots.at[pl.ds(0, s.n_dev - 1)])

    def x_drain(number, slots):
        take(r.x_sem.at[number, 0], slots.at[pl.ds(0, s.n_dev - 1)])

    def plane_send(number, src, slots):
        for k in range(s.gy_n - 1, 0, -1):
            send(src, slots.at[gy], r.x_sem.at[number, 0], r.x_sem.at[number, 1], (gx, gy ^ k))
        slots[gy] = src[...]

    def line_send(number, src, slots):
        for k in range(gxn - 1, 0, -1):
            send(src, slots.at[gx], r.x_sem.at[number, 0], r.x_sem.at[number, 1], (gx ^ k, gy))
        slots[gx] = src[...]

    def group_wait(number, slots, way=1):
        take(r.x_sem.at[number, way], slots.at[pl.ds(0, slots.shape[0] - 1)])

    def rs_fill(part, grad, b):
        if s.fast:
            for dj in range(3):
                g = grad[:, (2 - dj) * ch : (3 - dj) * ch]
                low = g[:, :lanes].reshape(s.n_dev, 8, lanes)
                high = g[:, lanes:].reshape(s.n_dev, 8, lanes)
                v = jnp.concatenate([low, high], axis=1).astype(bf16).reshape(gxn, qn, 2, 16, lanes)
                for core in range(2):
                    b.rsb[part, core, :, :, 16 * dj : 16 * dj + 16, :] = v[:, :, core]
        else:
            for dj in range(3):
                r.flat[3 * part + dj] = grad[:, (2 - dj) * ch : (3 - dj) * ch]

    def rs_fill_rest(b):
        if s.fast:
            return
        r.stage[...] = jnp.zeros_like(r.stage)

        def one(g, _):
            for t in range(9):
                r.eight[t] = r.flat[t, pl.ds(pl.multiple_of(8 * g, 8), 8), :]
            for e in range(8 // w):
                d = g * (8 // w) + e
                for t in range(9):
                    v = r.eight[t, w * e : w * e + w, :]
                    r.stage[2 * w * t : 2 * w * t + w, :] = v[:, :lanes]
                    r.stage[2 * w * t + w : 2 * w * t + 2 * w, :] = v[:, lanes:]
                at = (0, lax.rem(d, 2), lax.div(d, s.gy_n), lax.div(lax.rem(d, s.gy_n), 2))
                b.rsb[at] = r.stage[0 : s.blk, :].astype(bf16)
            return 0

        lax.fori_loop(0, ch // 8, one, 0)

    def rs_cross(b, part):
        send(b.rsb.at[part, 1 - c], b.rc.at[part], b.sem.at[part, 0], b.sem.at[part, 1], other)

    def rs_plane(b, part):
        take(b.sem.at[part, 1], b.rc.at[part])
        for p in range(qn):
            total = b.rsb[part, c, :, p].astype(f32) + b.rc[part, :, p].astype(f32)
            b.pb[part, p] = total.astype(bf16)
        if s.nch > 1 and part == s.nch - 1:
            for k in range(gxn - 1, -1, -1):
                for j in range(qn - 1, -1, -1):
                    if k + j:
                        block = b.pb.at[part, q_peer(j), z_peer(k)]
                        device = (z_peer(k), 2 * q_peer(j) + c)
                        send(block, b.rd.at[k * qn + j - 1], b.sem.at[part, 2], b.sem.at[part, 3], device)
            return
        for j in range(1, qn):
            to = q_peer(j)
            send(b.pb.at[part, to], b.rp.at[part, j - 1], b.sem.at[part, 2], b.sem.at[part, 3], (gx, 2 * to + c))

    def rs_line(b, part):
        if s.nch > 1 and part == s.nch - 1:
            return
        take(b.sem.at[part, 3], b.rp.at[part])
        total = b.pb[part, q].astype(f32)
        for j in range(qn - 1):
            total = total + b.rp[part, j].astype(f32)
        b.zb[part] = total.astype(bf16)
        for k in range(1, gxn):
            to = z_peer(k)
            send(b.zb.at[part, to], b.rz.at[part, k - 1], b.sem.at[part, 4], b.sem.at[part, 5], (to, gy))

    def rs_finish(b, part, out):
        if s.nch > 1 and part == s.nch - 1:
            take(b.sem.at[part, 3], b.rd)
            total = b.pb[part, q, gx].astype(f32) + jnp.sum(b.rd[...].astype(f32), axis=0)
        else:
            take(b.sem.at[part, 5], b.rz.at[part])
            total = b.zb[part, gx].astype(f32)
            for k in range(gxn - 1):
                total = total + b.rz[part, k].astype(f32)
        taps = 9 // s.nch
        for t in range(taps):
            at = 2 * w * t
            out[part * taps + t] = jnp.concatenate([total[at : at + w], total[at + w : at + 2 * w]], axis=1)

    def rs_drain(b):
        for part in range(s.nch):
            take(b.sem.at[part, 0], b.rc.at[part])
            if s.nch > 1 and part == s.nch - 1:
                take(b.sem.at[part, 2], b.rd)
                continue
            take(b.sem.at[part, 2], b.rp.at[part])
            take(b.sem.at[part, 4], b.rz.at[part])

    def rs_buffers(number):
        names = ("rsb", "rc", "pb", "rp", "zb", "rz", "rd")
        b = types.SimpleNamespace(**{n: getattr(r, n + number) for n in names})
        b.sem = getattr(r, "rs_sem" + number)
        return b

    rs1, rs2 = rs_buffers("1"), rs_buffers("2")

    def local_stats(field, out):
        pivot = field[0:1, :]

        def one(i, carry):
            d = jnp.where(inside, field[rows_of(i), :] - pivot, 0.0).reshape(br // 8, 8, ch)
            return carry[0] + jnp.sum(d, axis=0), carry[1] + jnp.sum(d * d, axis=0)

        zero = jnp.zeros((8, ch), f32)
        first, second = lax.fori_loop(0, s.side, one, (zero, zero))
        n = float(nb * s.cells)
        first = jnp.sum(first, axis=0, keepdims=True) / n
        second = jnp.sum(second, axis=0, keepdims=True) - n * first * first
        out[0:1, :] = pivot + first
        out[1:2, :] = second

    def global_stats(slots):
        v = slots[...]
        n = float(nb * s.cells)
        mean = jnp.sum(v[:, 0:1, :], axis=0) / s.n_dev
        d = v[:, 0:1, :] - mean
        spread_sum = jnp.sum(v[:, 1:2, :] + n * d * d, axis=0)
        return mean, lax.rsqrt(spread_sum / s.count + epsilon)

    n1 = s.nch
    for u in range(n1):
        g_start(u)
    for u in turned:
        g_start(u)
    g_forward(0)
    for u in range(n1, 2 * n1):
        if u not in turned:
            g_start(u)
    for u in range(1, 2 * n1):
        g_forward(u)
    g_start(2 * n1)
    row, col = iota((s.long, s.line), 0), iota((s.long, s.line), 1)
    r.expand[...] = (col == lax.shift_right_logical(row, 2)).astype(f32).astype(bf16)
    r.out_r[s.rows :, :] = jnp.zeros((s.long - s.rows, ch), bf16)
    r.vu[s.rows :, :] = jnp.zeros((s.long - s.rows, 2 * ch), bf16)
    r.xt[...] = jnp.transpose(r.x3[br : br + s.rows, ch : 2 * ch])
    for u in range(n1):
        g_cross(u)

    def conv_part(planes, weight, di, out):
        v = dot(planes[br * di : br * di + s.rows, :], weight[di])
        out[0 : s.rows, :] = v if di == 0 else out[0 : s.rows, :] + v

    chunk = s.long // 3

    def conv(planes, weight, out):
        def one(k, _):
            at = pl.multiple_of(k * chunk, 16)
            v = dot(planes[pl.ds(at, chunk), :], weight[0])
            v = v + dot(planes[pl.ds(at + br, chunk), :], weight[1])
            out[pl.ds(at, chunk), :] = v + dot(planes[pl.ds(at + 2 * br, chunk), :], weight[2])
            return 0

        lax.fori_loop(0, 3, one, 0)

    for part in range(n1):
        g_done(part)
        unpack(r.s1, part, r.wt1)
        if s.fast:
            conv_part(r.x3, r.wt1, part, r.h1)
    if not s.fast:
        conv(r.x3, r.wt1, r.h1)
    local_stats(r.h1, r.st1)
    x_send(0, r.st1, r.t1)

    g_forward(2 * n1)
    unpack_small()
    fetch["cot"].wait()

    def flip(weight, back):
        def one(n, _):
            di, dj = lax.div(n, 3), lax.rem(n, 3)
            tap = weight[2 - di, pl.ds(pl.multiple_of((2 - dj) * ch, ch), ch), :]
            back[di, pl.ds(pl.multiple_of(dj * ch, ch), ch), :] = jnp.transpose(tap)
            return 0

        lax.fori_loop(0, 9, one, 0)

    for u in range(n1, 2 * n1):
        g_cross(u)
    flip(r.wt1, r.wb1)

    gain1, gain2 = r.pars[0:1, :], r.pars[1:2, :]
    shift1, shift2 = r.pars[2:3, :], r.pars[3:4, :]
    hc0, hc1 = r.pars[4:5, :], r.pars[5:6, :]

    x_wait(0, r.t1)
    mean1, inv1 = global_stats(r.t1)

    def act1(i, _):
        n = (r.h1[rows_of(i), :] - mean1) * (inv1 * gain1) + shift1
        a = gelu(n)
        store3(r.a3, i, jnp.where(inside, a, 0.0))
        return 0

    lax.fori_loop(0, s.side, act1, 0)
    for u in range(n1, 2 * n1):
        g_done(u)
        unpack(r.s2, u - n1, r.wt2)
    conv(r.a3, r.wt2, r.h2)
    local_stats(r.h2, r.st2)
    x_send(1, r.st2, r.t2)

    r.at[...] = jnp.transpose(r.a3[br : br + s.rows, ch : 2 * ch])

    def slope1(i, _):
        n = (r.h1[rows_of(i), :] - mean1) * (inv1 * gain1) + shift1
        r.back1[rows_of(i), :] = gelu_both(n)[1]
        return 0

    lax.fori_loop(0, s.side, slope1, 0)
    g_cross(2 * n1)
    g_done(2 * n1)
    at = iota((s.line, 1), 0)
    i_of = divided(at, wide, s.line)
    j_of = at - i_of * wide
    used = (i_of < s.side) & (j_of < s.side)
    wide_slots = s.n_dev * s.rp
    shard_rows = iota((s.line, wide_slots), 1)
    dense_all = r.sd[...].reshape(wide_slots, s.mp)
    for k in range(2):
        source = k * s.cells + i_of * s.side + j_of
        if k == 0:
            source = jnp.where(at == s.side, s.head_in, source)
            wanted = used | (at == s.side)
        else:
            wanted = used
        source = jnp.where(wanted, source, 0)
        shard = divided(source, s.rsh, 1024)
        place = jnp.where(wanted, shard * s.rp + (source - shard * s.rsh), -1)
        pick = (shard_rows == place).astype(f32).astype(bf16)
        r.dk[k] = dot(pick, dense_all).astype(bf16)
    row = iota((16, ch), 0)
    hc_rows = jnp.where(row == 0, hc0, jnp.where(row == 1, hc1, 0.0)).astype(bf16)

    x_wait(1, r.t2)
    mean2, inv2 = global_stats(r.t2)

    def act2(i, _):
        at = rows_of(i)
        xin = r.x3[pl.ds(pl.multiple_of((i + 1) * br, 16), br), ch : 2 * ch].astype(f32)
        z = xin + ((r.h2[at, :] - mean2) * (inv2 * gain2) + shift2)
        r.dz[at, :] = z
        a = jnp.where(inside, gelu(z), 0.0)
        r.out_r[at, :] = a.astype(bf16)
        return 0

    lax.fori_loop(0, s.side, act2, 0)
    p_long = dot_nt(hc_rows, r.out_r[...])[0:8]
    lane = iota((8, s.long), 1)
    lane_j = lane - divided(lane, br, s.long) * br
    valid_long = (lane_j < nb * s.side) & (lane < s.rows)
    row1, lane1 = iota((8, lanes), 0), iota((8, lanes), 1)

    def by_head(v):
        a = v[0:1] + v[1:2] + v[2:3] + v[3:4]
        b = v[4:5] + v[5:6] + v[6:7] + v[7:8]
        return jnp.where(iota(v.shape, 0) < nb, a, b)

    n_local = float(nb * s.cells)
    mean_row = jnp.sum(jnp.where(valid_long, p_long, 0.0), axis=1, keepdims=True) / n_local
    dev = jnp.where(valid_long, p_long - mean_row, 0.0)
    square_row = jnp.sum(dev * dev, axis=1, keepdims=True)
    lane3 = iota((1, lanes), 1)
    means = jnp.where(lane3 < 32, mean_row[0:1], mean_row[1:2])
    r.st3[...] = jnp.where(lane3 < 64, means, jnp.where(lane3 < 96, square_row[0:1], square_row[1:2]))
    x_send(2, r.st3, r.t3)

    for name in names[8:]:
        fetch[name].wait()
    r.legal_both[...] = jnp.zeros_like(r.legal_both)
    r.legal_both[0:nb, 0 : s.moves] = r.legal_v[...]
    r.legal_both[nb : 2 * nb, 0 : s.moves] = r.legal_v[...]

    def slope2(i, carry):
        at = rows_of(i)
        slope = jnp.where(inside, gelu_both(r.dz[at, :])[1], 0.0)
        r.dz[at, :] = slope
        scaled = slope * ((r.h2[at, :] - mean2) * inv2)
        r.vu[at, 0:ch] = slope.astype(bf16)
        r.vu[at, ch:] = scaled.astype(bf16)
        r.out_v[i] = to_board(r.out_r[at, :].astype(f32))
        cot = from_board(r.cot_v[i])
        r.cot_s[at, :] = cot * slope
        a = (cot * scaled).reshape(br // 8, 8, ch)
        b = (cot * slope).reshape(br // 8, 8, ch)
        return carry[0] + jnp.sum(a, axis=0), carry[1] + jnp.sum(b, axis=0)

    zero = jnp.zeros((8, ch), f32)
    cot_g, cot_s = lax.fori_loop(0, s.side, slope2, (zero, zero))
    put_out = pltpu.make_async_copy(r.out_v, r.out, r.local_sem.at[len(names)])
    put_out.start()
    cot_g, cot_s = jnp.sum(cot_g, axis=0, keepdims=True), jnp.sum(cot_s, axis=0, keepdims=True)
    row = iota((16, s.long), 0)
    centred = jnp.where(valid_long[0:1], p_long[0:2] - mean_row[0:2], 0.0)
    against = jnp.where(
        row == 0, jnp.where(valid_long[0:1], 1.0, 0.0), jnp.where(row == 1, centred[0:1], jnp.where(row == 2, centred[1:2], 0.0))
    ).astype(bf16)
    early = dot(against, r.vu[...])
    for half in range(2):
        part = early[:, half * ch : (half + 1) * ch]
        ones = part[0:1]
        r.ste[4 * half : 4 * half + 1, :] = ones
        r.ste[4 * half + 1 : 4 * half + 2, :] = part[1:2] + mean_row[0:1] * ones
        r.ste[4 * half + 2 : 4 * half + 3, :] = part[2:3] + mean_row[1:2] * ones
        r.ste[4 * half + 3 : 4 * half + 4, :] = jnp.zeros((1, ch), f32)
    plane_send(3, r.ste, r.te)
    row = iota((8, s.long), 0)
    wanted = (lane & (nb - 1)) == (row & (nb - 1))
    rest = jnp.where(wanted, jnp.where(row < nb, p_long[0:1], p_long[1:2]), 0.0)
    parts = []
    for _ in range(3):
        part = rest.astype(bf16).astype(f32)
        parts.append(part)
        rest = rest - part
    parts = jnp.concatenate(parts + [jnp.zeros_like(rest)], axis=0).astype(bf16)
    p8 = dot(parts, r.expand[...])
    p8 = p8[0:8] + p8[8:16] + p8[16:24]
    row = iota((8, s.line), 0)
    lane = iota((8, s.line), 1)
    lane_i = divided(lane, wide, s.line)
    valid = (lane_i < s.side) & (lane - lane_i * wide < s.side)
    first_head = row < nb

    x_wait(2, r.t3)
    v = r.t3[...]
    mean_k = jnp.sum(v, axis=0) / float(s.n_dev)
    dev = v - mean_k
    squares = jnp.sum(jnp.where(lane3 < 64, n_local * dev * dev, v), axis=0)

    def of_head(v, at):
        return jnp.where(iota((8, 1), 0) < nb, v[:, at : at + 1], v[:, at + 32 : at + 33])

    mean_long = jnp.concatenate([mean_k[:, 0:1], mean_k[:, 32:33]], axis=0)
    mean_p = of_head(mean_k, 0)
    squares = of_head(squares, 0) + of_head(squares, 64)
    inv_p = lax.rsqrt(squares / s.count + epsilon)
    inv_long = jnp.concatenate([inv_p[0:1], inv_p[nb : nb + 1]], axis=0)
    gain_p = jnp.where(iota((8, 1), 0) < nb, r.hng_v[0], r.hng_v[1])
    shift_p = jnp.where(iota((8, 1), 0) < nb, r.hns_v[0], r.hns_v[1])
    xhat_p = (p8 - mean_p) * inv_p
    feature, back_p = gelu_both(xhat_p * gain_p + shift_p)
    flat = jnp.where(valid, feature, 0.0).astype(bf16)
    one_lane = first_head & (lane == s.side)
    flat_f = flat.astype(f32)
    lhs0 = jnp.where(one_lane, 1.0, jnp.where(first_head, flat_f, 0.0))
    lhs1 = jnp.where(first_head, 0.0, flat_f)
    pad8 = jnp.zeros((8, s.line), f32)

    def tall(v):
        return jnp.concatenate([v, pad8[:, : v.shape[1]]], axis=0).astype(bf16)

    half = (dot(tall(lhs0), r.dk[0]) + dot(tall(lhs1), r.dk[1]))[0:8]
    logits = half + pltpu.roll(half, nb, 0)
    move = iota((8, s.mp), 1)
    masked = jnp.where(r.legal_both[...] == 1, logits, negative_fill)
    top = jnp.max(masked, axis=1, keepdims=True)
    terms = jnp.exp(masked - top)
    total = jnp.sum(terms, axis=1, keepdims=True)
    row_b = iota((8, 1), 0) & (nb - 1)
    target = jnp.where(
        row_b < 2,
        jnp.where(row_b == 0, r.target_v[0], r.target_v[1]),
        jnp.where(row_b == 2, r.target_v[2], r.target_v[3]),
    )
    chosen = move == target
    picked = jnp.sum(jnp.where(chosen, logits, 0.0), axis=1, keepdims=True)
    ce = top + jnp.log(total) - picked
    dl = (terms / total - chosen.astype(f32)).astype(bf16).astype(f32)
    first_move = iota((8, s.mp), 0) < nb
    dq = dot_nt(tall(jnp.where(first_move, dl, 0.0)), r.dk[0]) + dot_nt(
        tall(jnp.where(first_move, 0.0, dl)), r.dk[1]
    )
    dnh = jnp.where(valid, dq[0:8] * back_p, 0.0)
    gain_row = jnp.sum(dnh * xhat_p, axis=1, keepdims=True)
    shift_row = jnp.sum(dnh, axis=1, keepdims=True)
    scale_p = gain_p * inv_p
    long_row, long_lane = iota((8, s.long), 0), iota((8, s.long), 1)
    dnh_long = dot_nt(tall(dnh), r.expand[...])[0:8]
    dnh_long = jnp.where((long_lane & (nb - 1)) == (long_row & (nb - 1)), dnh_long, 0.0)
    late = dot(jnp.concatenate([dnh_long, jnp.zeros_like(dnh_long)], axis=0).astype(bf16), r.vu[...])[0:8]
    head_rows = jnp.where(iota((8, ch), 0) < nb, hc0, hc1) * scale_p
    late_s = jnp.sum(late[:, 0:ch] * head_rows, axis=0, keepdims=True)
    late_g = jnp.sum(late[:, ch:] * head_rows, axis=0, keepdims=True)
    r.st5[0:1, :] = cot_g + late_g
    r.st5[1:2, :] = cot_s + late_s

    def heads(v):
        return v[0:1] + v[1:2] + v[2:3] + v[3:4], v[4:5] + v[5:6] + v[6:7] + v[7:8]

    gain_heads, shift_heads, ce_sum = heads(gain_row), heads(shift_row), heads(ce)[0]
    lane5 = iota((1, ch), 1)
    low = jnp.where(lane5 < 32, gain_heads[0], gain_heads[1])
    high = jnp.where(lane5 < 96, shift_heads[0], shift_heads[1])
    r.st5[2:3, :] = jnp.where(lane5 < 64, low, jnp.where(lane5 < 128, high, ce_sum))
    x_send(4, r.st5, r.t5)
    group_wait(3, r.te)
    r.stl[...] = jnp.sum(r.te[...], axis=0)
    line_send(7, r.stl, r.tl)
    r.fd_own[...] = jnp.zeros_like(r.fd_own)
    r.fd_own[0:8, :] = flat_f
    r.fd_own[8:16, 0 : s.mp] = dl
    r.fd[gx, q, c] = r.fd_own[...].astype(bf16)
    g_start(2 * n1 + 1)
    flip(r.wt2, r.wb2)
    scaled_long = dnh_long * scale_p
    dnh_heads = [jnp.sum(scaled_long[nb * k : nb * k + nb], axis=0, keepdims=True) for k in range(2)]
    xhat_long = (p_long[0:2] - mean_long) * inv_long
    xhat_long = jnp.where(valid_long[0:1], xhat_long, 0.0)
    row = iota((16, s.long), 0)
    terms_long = jnp.where(valid_long[0:1], 1.0, 0.0)
    for n, value in ((0, dnh_heads[0]), (1, dnh_heads[1]), (3, xhat_long[0:1]), (4, xhat_long[1:2])):
        terms_long = jnp.where(row == n, value, terms_long)
    terms_long = jnp.where(row < 5, terms_long, 0.0)
    r.terms[...] = terms_long.astype(bf16)
    tall_terms = jnp.concatenate([terms_long, jnp.zeros((lanes - 16, s.long), f32)], axis=0)
    r.terms_t[...] = jnp.transpose(tall_terms).astype(bf16)
    x_wait(4, r.t5)
    group_wait(7, r.tl)
    te = jnp.sum(r.tl[...], axis=0)
    t5 = jnp.sum(r.t5[...], axis=0)
    sums = t5[2:3]
    gain_sums, shift_sums = (sums[:, 0:1], sums[:, 32:33]), (sums[:, 64:65], sums[:, 96:97])
    r.tiny[0:1, :] = jnp.broadcast_to(sums[:, 128:129] / float(nb * s.n_dev), (1, lanes))
    first_lane = iota((1, lanes), 1) == 0
    r.tiny[1:2, :] = jnp.where(first_lane, *gain_sums)
    r.tiny[2:3, :] = jnp.where(first_lane, *shift_sums)
    g2s, s2s = t5[0:1], t5[1:2]
    for k in range(2):
        weight = (hc0, hc1)[k] * (scale_p[nb * k : nb * k + 1] / s.count)
        gain_part = gain_sums[k] * inv_p[nb * k : nb * k + 1]
        mean_k = mean_p[nb * k : nb * k + 1]
        s2s = s2s - weight * (shift_sums[k] * te[0:1] + gain_part * (te[k + 1 : k + 2] - mean_k * te[0:1]))
        g2s = g2s - weight * (shift_sums[k] * te[4:5] + gain_part * (te[k + 5 : k + 6] - mean_k * te[4:5]))
    scales = [scale_p[nb * k : nb * k + 1] / s.count for k in range(2)]
    ones_of = [shift_sums[k] * scales[k] for k in range(2)]
    xhat_of = [gain_sums[k] * scales[k] for k in range(2)]

    row = iota((lanes, ch), 0)
    mix = jnp.where(row == 0, hc0, jnp.where(row == 1, hc1, 0.0))
    mix = jnp.where(row == 2, -(hc0 * ones_of[0] + hc1 * ones_of[1]), mix)
    mix = jnp.where(row == 3, -hc0 * xhat_of[0], jnp.where(row == 4, -hc1 * xhat_of[1], mix))
    r.up[...] = dot(r.terms_t[...], mix.astype(bf16))

    def sums_back(field, xhat, carry):
        f = field.reshape(br // 8, 8, ch)
        g = (field * xhat).reshape(br // 8, 8, ch)
        return carry[0] + jnp.sum(g, axis=0), carry[1] + jnp.sum(f, axis=0)

    def to_field2(i, _):
        at = rows_of(i)
        xhat = (r.h2[at, :] - mean2) * inv2
        dz = r.cot_s[at, :] + r.up[at, :] * r.dz[at, :]
        r.dz[at, :] = dz
        d = (gain2 * inv2) * (dz - (s2s + xhat * g2s) * (1.0 / s.count))
        store3(r.d3, i, jnp.where(inside, d, 0.0))
        return 0

    lax.fori_loop(0, s.side, to_field2, 0)

    def wgrad(planes_t, di):
        start = pl.multiple_of(2 * br - br * di, 16)
        return dot(planes_t[...], r.d3[pl.ds(start, s.rows), :])

    def leave(planes_t, first, b):
        def one(di, _):
            rs_fill(di, wgrad(planes_t, di), b)
            if s.fast:
                rs_cross(b, di)
            return 0

        lax.fori_loop(first, 3, one, 0)
        rs_fill_rest(b)
        if not s.fast:
            rs_cross(b, 0)

    early = 1 if s.fast else 0
    for di in range(early):
        rs_fill(di, wgrad(r.at, di), rs2)
        rs_cross(rs2, di)
    g_forward(2 * n1 + 1)
    conv(r.d3, r.wb2, r.h2)

    def back1(i, carry):
        at = rows_of(i)
        dn = jnp.where(inside, r.h2[at, :] * r.back1[at, :], 0.0)
        r.h2[at, :] = dn
        return sums_back(dn, (r.h1[at, :] - mean1) * inv1, carry)

    g1, s1 = lax.fori_loop(0, s.side, back1, (zero, zero))
    r.st6[0:1, :] = jnp.sum(g1, axis=0, keepdims=True)
    r.st6[1:2, :] = jnp.sum(s1, axis=0, keepdims=True)
    x_send(5, r.st6, r.t6)
    against_out = dot(r.terms[...], r.out_r[...])
    for k in range(2):
        r.sth[k : k + 1, :] = (
            against_out[k : k + 1] - ones_of[k] * against_out[2:3] - xhat_of[k] * against_out[k + 3 : k + 4]
        )
    x_send(6, r.sth, r.th)
    for part in range(early):
        rs_plane(rs2, part)
    leave(r.at, early, rs2)
    for part in range(early, s.nch - 1):
        rs_plane(rs2, part)
    g_cross(2 * n1 + 1)
    x_wait(5, r.t6)
    t6 = jnp.sum(r.t6[...], axis=0)
    g1s, s1s = t6[0:1], t6[1:2]

    def to_field1(i, _):
        at = rows_of(i)
        xhat = (r.h1[at, :] - mean1) * inv1
        d = (gain1 * inv1) * (r.h2[at, :] - (s1s + xhat * g1s) * (1.0 / s.count))
        store3(r.d3, i, jnp.where(inside, d, 0.0))
        return 0

    rs_plane(rs2, s.nch - 1)
    lax.fori_loop(0, s.side, to_field1, 0)
    leave(r.xt, 0, rs1)
    for part in range(s.nch):
        rs_plane(rs1, part)
    conv(r.d3, r.wb1, r.h1)
    for part in range(s.nch):
        rs_line(rs2, part)

    def result(i, _):
        at = rows_of(i)
        r.in_grad_v[i] = to_board(r.dz[at, :] + r.h1[at, :])
        return 0

    lax.fori_loop(0, s.side, result, 0)
    put_in_grad = pltpu.make_async_copy(r.in_grad_v, r.in_grad, r.local_sem.at[len(names) + 1])
    put_in_grad.start()
    x_wait(6, r.th)
    shares = jnp.concatenate([g1s, g2s, s1s, s2s, jnp.sum(r.th[...], axis=0), jnp.zeros((2, ch), f32)], axis=0)
    r.tiny[8:16, :] = pltpu.roll(shares, lax.rem(ch - w * me, ch), 1)[:, 0:lanes]

    for part in range(s.nch):
        rs_line(rs1, part)

    g_done(2 * n1 + 1)
    fd = r.fd[...].astype(f32).reshape(s.n_dev, 16, s.line)
    features = fd[:, 0:8, :].reshape(8 * s.n_dev, s.line).astype(bf16)
    dls = fd[:, 8:16, 0 : s.mp].reshape(8 * s.n_dev, s.mp).astype(bf16)
    t = iota((s.rp, 1), 0)
    source = s.rsh * me + t
    mine = (t < s.rsh) & (source < s.head_in)
    col = iota((s.rp, s.line), 1)
    col8 = iota((s.rp, 8 * s.n_dev), 1) & 7
    own = jnp.where((t < s.rsh) & (source == s.head_in) & (col8 < nb), 1.0, 0.0)
    for k in range(2):
        in_k = mine & (source >= k * s.cells) & (source < (k + 1) * s.cells)
        cell = jnp.where(in_k, source - k * s.cells, 0)
        cell_i = divided(cell, s.side, s.cells)
        place = jnp.where(in_k, cell_i * wide + (cell - cell_i * s.side), -1)
        pick = (col == place).astype(f32).astype(bf16)
        rows_k = dot_nt(pick, features)
        own = own + jnp.where((col8 >= nb) if k else (col8 < nb), rows_k, 0.0)
    grad = dot(own.astype(bf16), dls)
    r.dense_grad[...] = grad

    for part in range(s.nch):
        rs_finish(rs2, part, r.c2_grad)
    for part in range(s.nch):
        rs_finish(rs1, part, r.c1_grad)

    for u in range(len(units)):
        g_drain(u)
    for number, slots in enumerate((r.t1, r.t2, r.t3, None, r.t5, r.t6, r.th)):
        if number != 3:
            x_drain(number, slots)
    group_wait(3, r.te, 0)
    group_wait(7, r.tl, 0)
    rs_drain(rs1)
    rs_drain(rs2)
    put_out.wait()
    put_in_grad.wait()


def place(w, x_ref, in_x_ref, c1, c2, dense, tiny, *refs):
    (out, loss, in_grad, c1_out, c2_out, gains, shifts, hc, hng, dense_out), refs = refs[:10], refs[10:]
    (out_v, in_v, c1_v, c2_v, dense_v, tiny_v), (came, went) = refs[:6], refs[6:]
    sources, held = (tiny, dense, c1, c2, x_ref, in_x_ref), (tiny_v, dense_v, c1_v, c2_v, out_v, in_v)
    fetch = [pltpu.make_async_copy(a, b, came.at[i]) for i, (a, b) in enumerate(zip(sources, held))]
    put = [
        pltpu.make_async_copy(a, b, went.at[i])
        for i, (a, b) in enumerate(((c1_v, c1_out), (c2_v, c2_out), (out_v, out), (in_v, in_grad)))
    ]
    for copy in fetch:
        copy.start()
    for i in range(4):
        fetch[i + 2].wait()
        put[i].start()
    fetch[0].wait()
    fetch[1].wait()
    loss[...] = tiny_v[0:1, 0:1]
    hng[...] = tiny_v[1:3, 0:2]
    gains[...] = tiny_v[8:10, 0:w]
    shifts[...] = tiny_v[10:12, 0:w]
    hc[...] = tiny_v[12:14, 0:w]
    dense_out[...] = dense_v[0 : dense_out.shape[0], 0 : dense_out.shape[1]]
    for copy in put:
        copy.wait()


def body(x, w1, w2, gains, shifts, hc, hng, hns, dense, legal, target, cot):
    x, cot = (jnp.transpose(v, (1, 2, 0, 3)) for v in (x, cot))
    s = sizes_of(lax.axis_size("gx"), lax.axis_size("gy"), x, w1, dense, legal.shape[1])
    vmem, hbm = pltpu.VMEM, pl.ANY
    inputs = dict(
        x=x, w1=w1, w2=w2, gains=gains, shifts=shifts, hc=hc, hng=hng, hns=hns, dense=dense, legal=legal,
        target=target, cot=cot,
    )
    outputs = dict(
        out=(x.shape, bf16), in_grad=(x.shape, bf16), c1_grad=(w1.shape, f32), c2_grad=(w2.shape, f32),
        dense_grad=((s.rp, s.mp), f32), tiny=((16, lanes), f32),
    )
    gxn, qn, n, ch = s.gx_n, s.q_n, s.n_dev, s.ch
    field = pltpu.VMEM((s.long, ch), f32)
    boards = pltpu.VMEM((s.side, s.wide, s.nb, ch), bf16)
    planes = pltpu.VMEM((s.padded, 3 * ch), bf16)
    turned = pltpu.VMEM((ch, s.rows), bf16)
    weight = pltpu.VMEM((3, 3 * ch, ch), bf16)
    two = pltpu.VMEM((2, ch), f32)
    eight = pltpu.VMEM((8, ch), f32)
    dma = pltpu.SemaphoreType.DMA
    scratch = dict(
        local_sem=dma((14,)), g_sem=dma((2 * s.nch + 2, 5 + gxn)), x_sem=dma((8, 2)),
        rs_sem1=dma((s.nch, 6)), rs_sem2=dma((s.nch, 6)),
        x_v=boards, cot_v=boards, out_v=pltpu.VMEM(x.shape, bf16), in_grad_v=pltpu.VMEM(x.shape, bf16),
        stage=pltpu.VMEM((s.blk1, lanes), f32), small=pltpu.VMEM((8, lanes), f32),
        s1=pltpu.VMEM((gxn, qn, 2, s.blk1, lanes), bf16), s2=pltpu.VMEM((gxn, qn, 2, s.blk, lanes), bf16),
        sd=pltpu.VMEM((gxn, qn, 2, s.rp, s.mp), bf16), dense_f=pltpu.VMEM((s.rp, s.mp), f32),
        x3=planes, a3=planes, d3=planes, out_r=pltpu.VMEM((s.long, ch), bf16), terms=pltpu.VMEM((16, s.long), bf16), terms_t=pltpu.VMEM((s.long, lanes), bf16),
        xt=turned, at=turned, wt1=weight, wt2=weight, wb1=weight, wb2=weight,
        pars=pltpu.VMEM((8, ch), f32), h1=field, h2=field, dz=field, back1=field, up=field, cot_s=field,
        st1=two, t1=pltpu.VMEM((n, 2, ch), f32), st2=two, t2=pltpu.VMEM((n, 2, ch), f32),
        st3=pltpu.VMEM((1, lanes), f32), t3=pltpu.VMEM((n, 1, lanes), f32), ste=eight, te=pltpu.VMEM((s.gy_n, 8, ch), f32), stl=eight, tl=pltpu.VMEM((gxn, 8, ch), f32),
        st5=pltpu.VMEM((3, ch), f32), t5=pltpu.VMEM((n, 3, ch), f32), st6=two, t6=pltpu.VMEM((n, 2, ch), f32),
        sth=two, th=pltpu.VMEM((n, 2, ch), f32), vu=pltpu.VMEM((s.long, 2 * ch), bf16),
        fd_own=pltpu.VMEM((16, s.line), f32), fd=pltpu.VMEM((gxn, qn, 2, 16, s.line), bf16),
        dk=pltpu.VMEM((2, s.line, s.mp), bf16), expand=pltpu.VMEM((s.long, s.line), bf16),
        legal_both=pltpu.VMEM((8, s.mp), jnp.int32),
    )
    for name in ("w1", "w2", "gains", "shifts", "hc", "dense", "legal"):
        scratch[name + "_v"] = pltpu.VMEM(inputs[name].shape, inputs[name].dtype)
    for name in ("hng", "hns", "target"):
        scratch[name + "_v"] = pltpu.SMEM(inputs[name].shape, inputs[name].dtype)
    if not s.fast:
        scratch["flat"] = pltpu.VMEM((9, ch, ch), f32)
        scratch["eight"] = pltpu.VMEM((9, 8, ch), f32)
    for number in ("1", "2"):
        scratch["rsb" + number] = pltpu.VMEM((s.nch, 2, gxn, qn, s.crows, lanes), bf16)
        scratch["rc" + number] = pltpu.VMEM((s.nch, gxn, qn, s.crows, lanes), bf16)
        scratch["pb" + number] = pltpu.VMEM((s.nch, qn, gxn, s.crows, lanes), bf16)
        scratch["rp" + number] = pltpu.VMEM((s.nch, qn - 1, gxn, s.crows, lanes), bf16)
        scratch["zb" + number] = pltpu.VMEM((s.nch, gxn, s.crows, lanes), bf16)
        scratch["rd" + number] = pltpu.VMEM((gxn * qn - 1, s.crows, lanes), bf16)
        scratch["rz" + number] = pltpu.VMEM((s.nch, gxn - 1, s.crows, lanes), bf16)
    run = pl.pallas_call(
        functools.partial(kernel, s, tuple(inputs), tuple(outputs), tuple(scratch)),
        out_shape=[jax.ShapeDtypeStruct(shape, kind) for shape, kind in outputs.values()],
        in_specs=[pl.BlockSpec(memory_space=hbm) for _ in inputs],
        out_specs=[pl.BlockSpec(memory_space=hbm if n in ("out", "in_grad") else vmem) for n in outputs],
        scratch_shapes=list(scratch.values()),
        compiler_params=pltpu.CompilerParams(
            collective_id=0, has_side_effects=True, vmem_limit_bytes=60 * 1024 * 1024
        ),
        cost_estimate=pl.CostEstimate(flops=10_500_000_000, bytes_accessed=8_000_000, transcendentals=800_000),
        name="tower",
    )
    results = run(*inputs.values())
    kinds = [jax.ShapeDtypeStruct(v.shape, v.dtype) for v in results]
    out, in_grad, c1_grad, c2_grad, dense_grad, _ = kinds
    small = [jax.ShapeDtypeStruct(v.shape, f32) for v in (gains, shifts, hc)]
    loss, pair = (jax.ShapeDtypeStruct(shape, f32) for shape in ((1, 1), (2, 2)))
    shapes = [out, loss, in_grad, c1_grad, c2_grad, *small, pair, jax.ShapeDtypeStruct(dense.shape, f32)]
    results = pl.pallas_call(
        functools.partial(place, s.w),
        out_shape=shapes,
        in_specs=[pl.BlockSpec(memory_space=hbm) for _ in kinds],
        out_specs=[pl.BlockSpec(memory_space=hbm if n in (0, 2, 3, 4) else vmem) for n in range(len(shapes))],
        scratch_shapes=[pltpu.VMEM(v.shape, v.dtype) for v in kinds] + [dma((len(kinds),))] * 2,
        name="place",
    )(*results)
    out, loss, in_grad, *rest = results
    out, in_grad = (jnp.transpose(v, (2, 0, 1, 3)) for v in (out, in_grad))
    return (out, loss.reshape(()), in_grad, *rest)


def solution(mesh):
    both = ("gx", "gy")
    board = P(both, None, None, None)
    kernels = P(None, both, None)
    pairs = P(None, both)
    return jax.shard_map(
        body,
        mesh=mesh,
        in_specs=(
            board, kernels, kernels, pairs, pairs, pairs, P(), P(), P(both, None), P(both, None), P(both), board,
        ),
        out_specs=(board, P(), board, kernels, kernels, pairs, pairs, pairs, P(), P(both, None)),
        check_vma=False,
    )
```

```python
import functools
import types

import jax
import jax.numpy as jnp
from jax import lax
from jax.experimental import pallas as pl
from jax.experimental.pallas import tpu as pltpu
from jax.sharding import PartitionSpec as P

MESH = pl.DeviceIdType.MESH
f32 = jnp.float32
bf16 = jnp.bfloat16
epsilon = 1e-05
negative_fill = -1e30
root = 0.7978845608028654
cube = 0.044715
lanes = 128


def up_to(value, unit):
    return -(-value // unit) * unit


def divided(values, divisor, limit):
    for shift in range(16, 24):
        factor = -(-(1 << shift) // divisor)
        if all((n * factor) >> shift == n // divisor and n * factor < 2**31 for n in range(limit)):
            return lax.shift_right_logical(values * factor, jnp.int32(shift))
    raise ValueError("no factor")


def iota(shape, axis):
    return lax.broadcasted_iota(jnp.int32, shape, axis)


def gelu_both(v):
    square = v * v
    slope = jnp.tanh(v * (root + (root * cube) * square))
    half = 0.5 + 0.5 * slope
    back = half + (0.5 * v) * (1.0 - slope * slope) * (root + (3.0 * root * cube) * square)
    return v * half, back


def gelu(v):
    half = 0.5 * v
    return half + half * jnp.tanh(v * (root + (root * cube) * (v * v)))


def dot(left, right):
    return jnp.dot(left, right, preferred_element_type=f32)


def dot_nt(left, right):
    return lax.dot_general(left, right, (((1,), (1,)), ((), ())), preferred_element_type=f32)


def sizes_of(gx_n, gy_n, x, w1, dense, moves):
    s = types.SimpleNamespace()
    s.gx_n, s.gy_n, s.q_n, s.n_dev = gx_n, gy_n, gy_n // 2, gx_n * gy_n
    s.side, s.nb, s.ch = x.shape[0], x.shape[2], x.shape[3]
    s.w = w1.shape[1]
    s.wide = s.side + 1
    s.br = s.wide * s.nb
    s.rows = s.side * s.br
    s.line = up_to(s.side * s.wide, lanes)
    s.long = up_to(s.rows, 3 * lanes)
    s.padded = s.long + 2 * s.br
    s.cells = s.side * s.side
    s.moves = moves
    s.mp = up_to(moves, lanes)
    s.rsh = dense.shape[0]
    s.rp = up_to(s.rsh, 16)
    s.head_in = 2 * s.cells
    s.blk = up_to(18 * s.w, 16)
    s.blk1 = up_to(19 * s.w, 16)
    s.fast = s.w == 8
    s.nch = 3 if s.fast else 1
    s.crows = s.blk // s.nch
    s.count = float(s.nb * s.cells * s.n_dev)
    assert s.nb == 4 and s.br % 16 == 0 and 8 % s.w == 0
    assert gx_n & (gx_n - 1) == 0 and gy_n & (gy_n - 1) == 0 and gy_n > 1
    return s


def kernel(s, in_names, out_names, scratch_names, *refs):
    r = types.SimpleNamespace(**dict(zip(in_names + out_names + scratch_names, refs)))
    gx, gy = lax.axis_index("gx"), lax.axis_index("gy")
    q, c = lax.div(gy, 2), lax.rem(gy, 2)
    me = gx * s.gy_n + gy
    other = (gx, gy + 1 - 2 * c)
    gxn, qn, nb, br, wide, ch = s.gx_n, s.q_n, s.nb, s.br, s.wide, s.ch

    def z_peer(k):
        return gx ^ k

    def q_peer(j):
        return q ^ j

    def send(src, dst, out_sem, in_sem, device):
        pltpu.make_async_remote_copy(
            src_ref=src, dst_ref=dst, send_sem=out_sem, recv_sem=in_sem, device_id=device, device_id_type=MESH
        ).start()

    def take(sem, ref):
        pltpu.make_async_copy(ref, ref, sem).wait()

    barrier = pltpu.get_barrier_semaphore()
    partners = [(z_peer(k), gy) for k in range(1, gxn)]
    partners += [(gx, 2 * q_peer(j) + c) for j in range(1, qn)]
    partners += [other]
    for p in partners:
        pl.semaphore_signal(barrier, inc=1, device_id=p, device_id_type=MESH)
    names = ("x", "w1", "w2", "gains", "shifts", "hc", "dense", "cot", "legal", "hng", "hns", "target")
    fetch = {}
    for n, name in enumerate(names):
        held = getattr(r, name + "_v")
        held = held.at[:, pl.ds(0, s.side)] if name in ("x", "cot") else held
        fetch[name] = pltpu.make_async_copy(getattr(r, name), held, r.local_sem.at[n])
        fetch[name].start()
    for fields in (r.x_v, r.cot_v):
        fields[:, s.side] = jnp.zeros((s.side, nb, ch), bf16)

    w = s.w

    def stage(weight):
        r.stage[...] = jnp.zeros_like(r.stage)
        for t in range(9):
            v = weight[t].astype(f32)
            r.stage[2 * w * t : 2 * w * t + w, :] = v[:, :lanes]
            r.stage[2 * w * t + w : 2 * w * t + 2 * w, :] = v[:, lanes:]

    def stage_all():
        for name in names[1:7]:
            fetch[name].wait()
        r.small[...] = jnp.zeros_like(r.small)
        r.small[0:2, 0:w] = r.gains_v[...].astype(f32)
        r.small[2:4, 0:w] = r.shifts_v[...].astype(f32)
        r.small[4:6, 0:w] = r.hc_v[...].astype(f32)
        stage(r.w1_v)
        r.stage[18 * w : 19 * w, 0:8] = jnp.transpose(r.small[...])[0:w, :]
        r.s1[gx, q, c] = r.stage[...].astype(bf16)
        stage(r.w2_v)
        r.s2[gx, q, c] = r.stage[0 : s.blk, :].astype(bf16)
        r.dense_f[...] = jnp.zeros_like(r.dense_f)
        r.dense_f[0 : s.rsh, 0 : s.moves] = r.dense_v[...].astype(f32)
        r.sd[gx, q, c] = r.dense_f[...].astype(bf16)

    for planes in (r.x3, r.a3, r.d3):
        planes[0:br, :] = jnp.zeros((br, 3 * ch), bf16)
        planes[br + s.rows :, :] = jnp.zeros((s.padded - br - s.rows, 3 * ch), bf16)
    inside = iota((br, ch), 0) < nb * s.side

    def store3(planes, i, block):
        at = pl.ds(pl.multiple_of((i + 1) * br, 16), br)
        planes[at, 0:ch] = pltpu.roll(block, nb, 0).astype(bf16)
        planes[at, ch : 2 * ch] = block.astype(bf16)
        planes[at, 2 * ch :] = pltpu.roll(block, br - nb, 0).astype(bf16)

    def rows_of(i):
        return pl.ds(pl.multiple_of(i * br, 16), br)

    def from_board(block):
        return block.astype(f32).reshape(br, ch)

    def to_board(block):
        return block.reshape(wide, nb, ch)[0 : s.side].astype(bf16)

    def x_rows(i, _):
        store3(r.x3, i, from_board(r.x_v[i]))
        return 0

    fetch["x"].wait()
    lax.fori_loop(0, s.side, x_rows, 0)
    stage_all()

    pl.semaphore_wait(barrier, len(partners))

    def span(unit):
        store, part = unit
        if store is r.sd or store is r.fd:
            return pl.ds(0, store.shape[3])
        whole = s.blk1 if store is r.s1 else s.blk
        if s.nch == 1:
            return pl.ds(0, whole)
        start = part * s.crows
        return pl.ds(start, whole - start if part == s.nch - 1 else s.crows)

    units = [(r.s1, p) for p in range(s.nch)] + [(r.s2, p) for p in range(s.nch)] + [(r.sd, 0), (r.fd, 0)]

    turned = {s.nch} if s.nch > 1 else set()

    def g_start(u):
        store, at = units[u][0], span(units[u])
        own = store.at[gx, q, c, at]
        for k in range(1, gxn):
            if u not in turned:
                send(own, own, r.g_sem.at[u, 0], r.g_sem.at[u, 5 + k], (z_peer(k), gy))
        for j in range(qn - 1, 0, -1):
            send(own, own, r.g_sem.at[u, 1], r.g_sem.at[u, 4], (gx, 2 * q_peer(j) + c))

    def g_forward(u):
        store, at = units[u][0], span(units[u])
        if u in turned:
            take(r.g_sem.at[u, 4], store.at[gx, pl.ds(0, qn - 1), 0, at])
            block = store.at[gx, :, c, at]
            for k in range(gxn - 1, 0, -1):
                send(block, block, r.g_sem.at[u, 2], r.g_sem.at[u, 5 + k], (z_peer(k), gy))
            return
        for k in range(1, gxn):
            block = store.at[z_peer(k), q, c, at]
            take(r.g_sem.at[u, 5 + k], block)
            for j in range(qn - 1, 0, -1):
                send(block, block, r.g_sem.at[u, 2], r.g_sem.at[u, 4], (gx, 2 * q_peer(j) + c))

    def g_cross(u):
        store, at = units[u][0], span(units[u])
        if u in turned:
            for k in range(1, gxn):
                take(r.g_sem.at[u, 5 + k], store.at[z_peer(k), :, c, at])
        else:
            take(r.g_sem.at[u, 4], store.at[:, pl.ds(0, qn - 1), 0, at])
        block = store.at[:, :, c, at]
        send(block, block, r.g_sem.at[u, 3], r.g_sem.at[u, 5], other)

    def g_done(u):
        store, at = units[u][0], span(units[u])
        take(r.g_sem.at[u, 5], store.at[:, :, 0, at])

    def g_drain(u):
        store, at = units[u][0], span(units[u])
        take(r.g_sem.at[u, 1], store.at[0, pl.ds(0, qn - 1), 0, at])
        if u in turned:
            take(r.g_sem.at[u, 2], store.at[pl.ds(0, gxn - 1), :, 0, at])
        else:
            take(r.g_sem.at[u, 0], store.at[pl.ds(0, gxn - 1), 0, 0, at])
            take(r.g_sem.at[u, 2], store.at[pl.ds(0, gxn - 1), pl.ds(0, qn - 1), 0, at])
        take(r.g_sem.at[u, 3], store.at[:, :, 0, at])

    def shard_of(store, d):
        return store[lax.div(d, s.gy_n), lax.div(lax.rem(d, s.gy_n), 2), lax.rem(d, 2)]

    def unpack(store, part, weight):
        if s.fast:
            for dj in range(3):
                at = 16 * (3 * part + dj)
                v = store[:, :, :, at : at + 16, :].astype(f32).reshape(s.n_dev, 16, lanes)
                low = v[:, 0:8, :].reshape(ch, lanes)
                high = v[:, 8:16, :].reshape(ch, lanes)
                weight[part, dj * ch : (dj + 1) * ch, :] = jnp.concatenate([low, high], axis=1).astype(bf16)
            return

        def one(g, _):
            for e in range(8 // w):
                r.stage[0 : s.blk, :] = shard_of(store, g * (8 // w) + e)[0 : s.blk].astype(f32)
                for t in range(9):
                    r.eight[t, w * e : w * e + w, 0:lanes] = r.stage[2 * w * t : 2 * w * t + w, :]
                    r.eight[t, w * e : w * e + w, lanes:] = r.stage[2 * w * t + w : 2 * w * t + 2 * w, :]
            for t in range(9):
                r.flat[t, pl.ds(pl.multiple_of(8 * g, 8), 8), :] = r.eight[t]
            return 0

        lax.fori_loop(0, ch // 8, one, 0)
        for t in range(9):
            weight[t // 3, (t % 3) * ch : (t % 3 + 1) * ch, :] = r.flat[t].astype(bf16)

    def unpack_small():
        if s.fast:
            v = r.s1[:, :, :, 18 * w : 18 * w + 16, :].astype(f32).reshape(s.n_dev, 16, lanes)
            rows = v[:, 0:8, :].reshape(ch, lanes)
        else:

            def one(g, _):
                for e in range(8 // w):
                    r.stage[...] = shard_of(r.s1, g * (8 // w) + e).astype(f32)
                    r.eight[0, w * e : w * e + w, 0:lanes] = r.stage[18 * w : 19 * w, :]
                r.flat[0, pl.ds(pl.multiple_of(8 * g, 8), 8), :] = r.eight[0]
                return 0

            lax.fori_loop(0, ch // 8, one, 0)
            rows = r.flat[0, :, 0:lanes]
        r.pars[...] = jnp.transpose(rows)[0:8, :]

    def x_send(number, src, slots):
        def one(k):
            device = (gx ^ lax.div(k, s.gy_n), gy ^ lax.rem(k, s.gy_n))
            send(src, slots.at[me], r.x_sem.at[number, 0], r.x_sem.at[number, 1], device)

        if s.n_dev <= 64:
            hops = {k: k // s.gy_n + bin(k % s.gy_n // 2).count("1") for k in range(1, s.n_dev)}
            for k in sorted(hops, key=lambda k: (-hops[k], k)):
                send(
                    src, slots.at[me], r.x_sem.at[number, 0], r.x_sem.at[number, 1],
                    (gx ^ (k // s.gy_n), gy ^ (k % s.gy_n)),
                )
        else:
            lax.fori_loop(0, s.n_dev - 1, lambda n, _: (one(s.n_dev - 1 - n), 0)[1], 0)
        slots[me] = src[...]

    def x_wait(number, slots):
        take(r.x_sem.at[number, 1], slots.at[pl.ds(0, s.n_dev - 1)])

    def x_drain(number, slots):
        take(r.x_sem.at[number, 0], slots.at[pl.ds(0, s.n_dev - 1)])

    def plane_send(number, src, slots):
        for k in range(s.gy_n - 1, 0, -1):
            send(src, slots.at[gy], r.x_sem.at[number, 0], r.x_sem.at[number, 1], (gx, gy ^ k))
        slots[gy] = src[...]

    def line_send(number, src, slots):
        for k in range(gxn - 1, 0, -1):
            send(src, slots.at[gx], r.x_sem.at[number, 0], r.x_sem.at[number, 1], (gx ^ k, gy))
        slots[gx] = src[...]

    def group_wait(number, slots, way=1):
        take(r.x_sem.at[number, way], slots.at[pl.ds(0, slots.shape[0] - 1)])

    def rs_fill(part, grad, b):
        if s.fast:
            for dj in range(3):
                g = grad[:, (2 - dj) * ch : (3 - dj) * ch]
                low = g[:, :lanes].reshape(s.n_dev, 8, lanes)
                high = g[:, lanes:].reshape(s.n_dev, 8, lanes)
                v = jnp.concatenate([low, high], axis=1).astype(bf16).reshape(gxn, qn, 2, 16, lanes)
                for core in range(2):
                    b.rsb[part, core, :, :, 16 * dj : 16 * dj + 16, :] = v[:, :, core]
        else:
            for dj in range(3):
                r.flat[3 * part + dj] = grad[:, (2 - dj) * ch : (3 - dj) * ch]

    def rs_fill_rest(b):
        if s.fast:
            return
        r.stage[...] = jnp.zeros_like(r.stage)

        def one(g, _):
            for t in range(9):
                r.eight[t] = r.flat[t, pl.ds(pl.multiple_of(8 * g, 8), 8), :]
            for e in range(8 // w):
                d = g * (8 // w) + e
                for t in range(9):
                    v = r.eight[t, w * e : w * e + w, :]
                    r.stage[2 * w * t : 2 * w * t + w, :] = v[:, :lanes]
                    r.stage[2 * w * t + w : 2 * w * t + 2 * w, :] = v[:, lanes:]
                at = (0, lax.rem(d, 2), lax.div(d, s.gy_n), lax.div(lax.rem(d, s.gy_n), 2))
                b.rsb[at] = r.stage[0 : s.blk, :].astype(bf16)
            return 0

        lax.fori_loop(0, ch // 8, one, 0)

    def rs_cross(b, part):
        send(b.rsb.at[part, 1 - c], b.rc.at[part], b.sem.at[part, 0], b.sem.at[part, 1], other)

    def rs_plane(b, part):
        take(b.sem.at[part, 1], b.rc.at[part])
        for p in range(qn):
            total = b.rsb[part, c, :, p].astype(f32) + b.rc[part, :, p].astype(f32)
            b.pb[part, p] = total.astype(bf16)
        if s.nch > 1 and part == s.nch - 1:
            for k in range(gxn - 1, -1, -1):
                for j in range(qn - 1, -1, -1):
                    if k + j:
                        block = b.pb.at[part, q_peer(j), z_peer(k)]
                        device = (z_peer(k), 2 * q_peer(j) + c)
                        send(block, b.rd.at[k * qn + j - 1], b.sem.at[part, 2], b.sem.at[part, 3], device)
            return
        for j in range(1, qn):
            to = q_peer(j)
            send(b.pb.at[part, to], b.rp.at[part, j - 1], b.sem.at[part, 2], b.sem.at[part, 3], (gx, 2 * to + c))

    def rs_line(b, part):
        if s.nch > 1 and part == s.nch - 1:
            return
        take(b.sem.at[part, 3], b.rp.at[part])
        total = b.pb[part, q].astype(f32)
        for j in range(qn - 1):
            total = total + b.rp[part, j].astype(f32)
        b.zb[part] = total.astype(bf16)
        for k in range(1, gxn):
            to = z_peer(k)
            send(b.zb.at[part, to], b.rz.at[part, k - 1], b.sem.at[part, 4], b.sem.at[part, 5], (to, gy))

    def rs_finish(b, part, out):
        if s.nch > 1 and part == s.nch - 1:
            take(b.sem.at[part, 3], b.rd)
            total = b.pb[part, q, gx].astype(f32) + jnp.sum(b.rd[...].astype(f32), axis=0)
        else:
            take(b.sem.at[part, 5], b.rz.at[part])
            total = b.zb[part, gx].astype(f32)
            for k in range(gxn - 1):
                total = total + b.rz[part, k].astype(f32)
        taps = 9 // s.nch
        for t in range(taps):
            at = 2 * w * t
            out[part * taps + t] = jnp.concatenate([total[at : at + w], total[at + w : at + 2 * w]], axis=1)

    def rs_drain(b):
        for part in range(s.nch):
            take(b.sem.at[part, 0], b.rc.at[part])
            if s.nch > 1 and part == s.nch - 1:
                take(b.sem.at[part, 2], b.rd)
                continue
            take(b.sem.at[part, 2], b.rp.at[part])
            take(b.sem.at[part, 4], b.rz.at[part])

    def rs_buffers(number):
        names = ("rsb", "rc", "pb", "rp", "zb", "rz", "rd")
        b = types.SimpleNamespace(**{n: getattr(r, n + number) for n in names})
        b.sem = getattr(r, "rs_sem" + number)
        return b

    rs1, rs2 = rs_buffers("1"), rs_buffers("2")

    def local_stats(field, out):
        pivot = field[0:1, :]

        def one(i, carry):
            d = jnp.where(inside, field[rows_of(i), :] - pivot, 0.0).reshape(br // 8, 8, ch)
            return carry[0] + jnp.sum(d, axis=0), carry[1] + jnp.sum(d * d, axis=0)

        zero = jnp.zeros((8, ch), f32)
        first, second = lax.fori_loop(0, s.side, one, (zero, zero))
        n = float(nb * s.cells)
        first = jnp.sum(first, axis=0, keepdims=True) / n
        second = jnp.sum(second, axis=0, keepdims=True) - n * first * first
        out[0:1, :] = pivot + first
        out[1:2, :] = second

    def global_stats(slots):
        v = slots[...]
        n = float(nb * s.cells)
        mean = jnp.sum(v[:, 0:1, :], axis=0) / s.n_dev
        d = v[:, 0:1, :] - mean
        spread_sum = jnp.sum(v[:, 1:2, :] + n * d * d, axis=0)
        return mean, lax.rsqrt(spread_sum / s.count + epsilon)

    n1 = s.nch
    for u in range(n1):
        g_start(u)
    for u in turned:
        g_start(u)
    for u in range(n1, 2 * n1):
        if u not in turned:
            g_start(u)
    for u in range(2 * n1):
        g_forward(u)
    g_start(2 * n1)
    row, col = iota((s.long, s.line), 0), iota((s.long, s.line), 1)
    r.expand[...] = (col == lax.shift_right_logical(row, 2)).astype(f32).astype(bf16)
    r.out_r[s.rows :, :] = jnp.zeros((s.long - s.rows, ch), bf16)
    r.vu[s.rows :, :] = jnp.zeros((s.long - s.rows, 2 * ch), bf16)
    r.xt[...] = jnp.transpose(r.x3[br : br + s.rows, ch : 2 * ch])
    for u in range(n1):
        g_cross(u)

    def conv_part(planes, weight, di, out):
        v = dot(planes[br * di : br * di + s.rows, :], weight[di])
        out[0 : s.rows, :] = v if di == 0 else out[0 : s.rows, :] + v

    chunk = s.long // 3

    def conv(planes, weight, out):
        def one(k, _):
            at = pl.multiple_of(k * chunk, 16)
            v = dot(planes[pl.ds(at, chunk), :], weight[0])
            v = v + dot(planes[pl.ds(at + br, chunk), :], weight[1])
            out[pl.ds(at, chunk), :] = v + dot(planes[pl.ds(at + 2 * br, chunk), :], weight[2])
            return 0

        lax.fori_loop(0, 3, one, 0)

    for part in range(n1):
        g_done(part)
        unpack(r.s1, part, r.wt1)
        if s.fast:
            conv_part(r.x3, r.wt1, part, r.h1)
    if not s.fast:
        conv(r.x3, r.wt1, r.h1)
    local_stats(r.h1, r.st1)
    x_send(0, r.st1, r.t1)

    g_forward(2 * n1)
    unpack_small()
    fetch["cot"].wait()

    def flip(weight, back):
        def one(n, _):
            di, dj = lax.div(n, 3), lax.rem(n, 3)
            tap = weight[2 - di, pl.ds(pl.multiple_of((2 - dj) * ch, ch), ch), :]
            back[di, pl.ds(pl.multiple_of(dj * ch, ch), ch), :] = jnp.transpose(tap)
            return 0

        lax.fori_loop(0, 9, one, 0)

    for u in range(n1, 2 * n1):
        g_cross(u)
    flip(r.wt1, r.wb1)

    gain1, gain2 = r.pars[0:1, :], r.pars[1:2, :]
    shift1, shift2 = r.pars[2:3, :], r.pars[3:4, :]
    hc0, hc1 = r.pars[4:5, :], r.pars[5:6, :]

    x_wait(0, r.t1)
    mean1, inv1 = global_stats(r.t1)

    def act1(i, _):
        n = (r.h1[rows_of(i), :] - mean1) * (inv1 * gain1) + shift1
        a = gelu(n)
        store3(r.a3, i, jnp.where(inside, a, 0.0))
        return 0

    lax.fori_loop(0, s.side, act1, 0)
    for u in range(n1, 2 * n1):
        g_done(u)
        unpack(r.s2, u - n1, r.wt2)
    conv(r.a3, r.wt2, r.h2)
    local_stats(r.h2, r.st2)
    x_send(1, r.st2, r.t2)

    r.at[...] = jnp.transpose(r.a3[br : br + s.rows, ch : 2 * ch])

    def slope1(i, _):
        n = (r.h1[rows_of(i), :] - mean1) * (inv1 * gain1) + shift1
        r.back1[rows_of(i), :] = gelu_both(n)[1]
        return 0

    lax.fori_loop(0, s.side, slope1, 0)
    g_cross(2 * n1)
    g_done(2 * n1)
    at = iota((s.line, 1), 0)
    i_of = divided(at, wide, s.line)
    j_of = at - i_of * wide
    used = (i_of < s.side) & (j_of < s.side)
    wide_slots = s.n_dev * s.rp
    shard_rows = iota((s.line, wide_slots), 1)
    dense_all = r.sd[...].reshape(wide_slots, s.mp)
    for k in range(2):
        source = k * s.cells + i_of * s.side + j_of
        if k == 0:
            source = jnp.where(at == s.side, s.head_in, source)
            wanted = used | (at == s.side)
        else:
            wanted = used
        source = jnp.where(wanted, source, 0)
        shard = divided(source, s.rsh, 1024)
        place = jnp.where(wanted, shard * s.rp + (source - shard * s.rsh), -1)
        pick = (shard_rows == place).astype(f32).astype(bf16)
        r.dk[k] = dot(pick, dense_all).astype(bf16)
    row = iota((16, ch), 0)
    hc_rows = jnp.where(row == 0, hc0, jnp.where(row == 1, hc1, 0.0)).astype(bf16)

    x_wait(1, r.t2)
    mean2, inv2 = global_stats(r.t2)

    def act2(i, _):
        at = rows_of(i)
        xin = r.x3[pl.ds(pl.multiple_of((i + 1) * br, 16), br), ch : 2 * ch].astype(f32)
        z = xin + ((r.h2[at, :] - mean2) * (inv2 * gain2) + shift2)
        r.dz[at, :] = z
        a = jnp.where(inside, gelu(z), 0.0)
        r.out_r[at, :] = a.astype(bf16)
        return 0

    lax.fori_loop(0, s.side, act2, 0)
    p_long = dot_nt(hc_rows, r.out_r[...])[0:8]
    lane = iota((8, s.long), 1)
    lane_j = lane - divided(lane, br, s.long) * br
    valid_long = (lane_j < nb * s.side) & (lane < s.rows)
    row1, lane1 = iota((8, lanes), 0), iota((8, lanes), 1)

    def by_head(v):
        a = v[0:1] + v[1:2] + v[2:3] + v[3:4]
        b = v[4:5] + v[5:6] + v[6:7] + v[7:8]
        return jnp.where(iota(v.shape, 0) < nb, a, b)

    n_local = float(nb * s.cells)
    mean_row = jnp.sum(jnp.where(valid_long, p_long, 0.0), axis=1, keepdims=True) / n_local
    dev = jnp.where(valid_long, p_long - mean_row, 0.0)
    square_row = jnp.sum(dev * dev, axis=1, keepdims=True)
    lane3 = iota((1, lanes), 1)
    means = jnp.where(lane3 < 32, mean_row[0:1], mean_row[1:2])
    r.st3[...] = jnp.where(lane3 < 64, means, jnp.where(lane3 < 96, square_row[0:1], square_row[1:2]))
    x_send(2, r.st3, r.t3)

    for name in names[8:]:
        fetch[name].wait()
    r.legal_both[...] = jnp.zeros_like(r.legal_both)
    r.legal_both[0:nb, 0 : s.moves] = r.legal_v[...]
    r.legal_both[nb : 2 * nb, 0 : s.moves] = r.legal_v[...]

    def slope2(i, carry):
        at = rows_of(i)
        slope = jnp.where(inside, gelu_both(r.dz[at, :])[1], 0.0)
        r.dz[at, :] = slope
        scaled = slope * ((r.h2[at, :] - mean2) * inv2)
        r.vu[at, 0:ch] = slope.astype(bf16)
        r.vu[at, ch:] = scaled.astype(bf16)
        r.out_v[i] = to_board(r.out_r[at, :].astype(f32))
        cot = from_board(r.cot_v[i])
        r.cot_s[at, :] = cot * slope
        a = (cot * scaled).reshape(br // 8, 8, ch)
        b = (cot * slope).reshape(br // 8, 8, ch)
        return carry[0] + jnp.sum(a, axis=0), carry[1] + jnp.sum(b, axis=0)

    zero = jnp.zeros((8, ch), f32)
    cot_g, cot_s = lax.fori_loop(0, s.side, slope2, (zero, zero))
    put_out = pltpu.make_async_copy(r.out_v, r.out, r.local_sem.at[len(names)])
    put_out.start()
    cot_g, cot_s = jnp.sum(cot_g, axis=0, keepdims=True), jnp.sum(cot_s, axis=0, keepdims=True)
    row = iota((16, s.long), 0)
    centred = jnp.where(valid_long[0:1], p_long[0:2] - mean_row[0:2], 0.0)
    against = jnp.where(
        row == 0, jnp.where(valid_long[0:1], 1.0, 0.0), jnp.where(row == 1, centred[0:1], jnp.where(row == 2, centred[1:2], 0.0))
    ).astype(bf16)
    early = dot(against, r.vu[...])
    for half in range(2):
        part = early[:, half * ch : (half + 1) * ch]
        ones = part[0:1]
        r.ste[4 * half : 4 * half + 1, :] = ones
        r.ste[4 * half + 1 : 4 * half + 2, :] = part[1:2] + mean_row[0:1] * ones
        r.ste[4 * half + 2 : 4 * half + 3, :] = part[2:3] + mean_row[1:2] * ones
        r.ste[4 * half + 3 : 4 * half + 4, :] = jnp.zeros((1, ch), f32)
    plane_send(3, r.ste, r.te)
    row = iota((8, s.long), 0)
    wanted = (lane & (nb - 1)) == (row & (nb - 1))
    rest = jnp.where(wanted, jnp.where(row < nb, p_long[0:1], p_long[1:2]), 0.0)
    parts = []
    for _ in range(3):
        part = rest.astype(bf16).astype(f32)
        parts.append(part)
        rest = rest - part
    parts = jnp.concatenate(parts + [jnp.zeros_like(rest)], axis=0).astype(bf16)
    p8 = dot(parts, r.expand[...])
    p8 = p8[0:8] + p8[8:16] + p8[16:24]
    row = iota((8, s.line), 0)
    lane = iota((8, s.line), 1)
    lane_i = divided(lane, wide, s.line)
    valid = (lane_i < s.side) & (lane - lane_i * wide < s.side)
    first_head = row < nb

    x_wait(2, r.t3)
    v = r.t3[...]
    mean_k = jnp.sum(v, axis=0) / float(s.n_dev)
    dev = v - mean_k
    squares = jnp.sum(jnp.where(lane3 < 64, n_local * dev * dev, v), axis=0)

    def of_head(v, at):
        return jnp.where(iota((8, 1), 0) < nb, v[:, at : at + 1], v[:, at + 32 : at + 33])

    mean_long = jnp.concatenate([mean_k[:, 0:1], mean_k[:, 32:33]], axis=0)
    mean_p = of_head(mean_k, 0)
    squares = of_head(squares, 0) + of_head(squares, 64)
    inv_p = lax.rsqrt(squares / s.count + epsilon)
    inv_long = jnp.concatenate([inv_p[0:1], inv_p[nb : nb + 1]], axis=0)
    gain_p = jnp.where(iota((8, 1), 0) < nb, r.hng_v[0], r.hng_v[1])
    shift_p = jnp.where(iota((8, 1), 0) < nb, r.hns_v[0], r.hns_v[1])
    xhat_p = (p8 - mean_p) * inv_p
    feature, back_p = gelu_both(xhat_p * gain_p + shift_p)
    flat = jnp.where(valid, feature, 0.0).astype(bf16)
    one_lane = first_head & (lane == s.side)
    flat_f = flat.astype(f32)
    lhs0 = jnp.where(one_lane, 1.0, jnp.where(first_head, flat_f, 0.0))
    lhs1 = jnp.where(first_head, 0.0, flat_f)
    pad8 = jnp.zeros((8, s.line), f32)

    def tall(v):
        return jnp.concatenate([v, pad8[:, : v.shape[1]]], axis=0).astype(bf16)

    half = (dot(tall(lhs0), r.dk[0]) + dot(tall(lhs1), r.dk[1]))[0:8]
    logits = half + pltpu.roll(half, nb, 0)
    move = iota((8, s.mp), 1)
    masked = jnp.where(r.legal_both[...] == 1, logits, negative_fill)
    top = jnp.max(masked, axis=1, keepdims=True)
    terms = jnp.exp(masked - top)
    total = jnp.sum(terms, axis=1, keepdims=True)
    row_b = iota((8, 1), 0) & (nb - 1)
    target = jnp.where(
        row_b < 2,
        jnp.where(row_b == 0, r.target_v[0], r.target_v[1]),
        jnp.where(row_b == 2, r.target_v[2], r.target_v[3]),
    )
    chosen = move == target
    picked = jnp.sum(jnp.where(chosen, logits, 0.0), axis=1, keepdims=True)
    ce = top + jnp.log(total) - picked
    dl = (terms / total - chosen.astype(f32)).astype(bf16).astype(f32)
    first_move = iota((8, s.mp), 0) < nb
    dq = dot_nt(tall(jnp.where(first_move, dl, 0.0)), r.dk[0]) + dot_nt(
        tall(jnp.where(first_move, 0.0, dl)), r.dk[1]
    )
    dnh = jnp.where(valid, dq[0:8] * back_p, 0.0)
    gain_row = jnp.sum(dnh * xhat_p, axis=1, keepdims=True)
    shift_row = jnp.sum(dnh, axis=1, keepdims=True)
    scale_p = gain_p * inv_p
    long_row, long_lane = iota((8, s.long), 0), iota((8, s.long), 1)
    dnh_long = dot_nt(tall(dnh), r.expand[...])[0:8]
    dnh_long = jnp.where((long_lane & (nb - 1)) == (long_row & (nb - 1)), dnh_long, 0.0)
    late = dot(jnp.concatenate([dnh_long, jnp.zeros_like(dnh_long)], axis=0).astype(bf16), r.vu[...])[0:8]
    head_rows = jnp.where(iota((8, ch), 0) < nb, hc0, hc1) * scale_p
    late_s = jnp.sum(late[:, 0:ch] * head_rows, axis=0, keepdims=True)
    late_g = jnp.sum(late[:, ch:] * head_rows, axis=0, keepdims=True)
    r.st5[0:1, :] = cot_g + late_g
    r.st5[1:2, :] = cot_s + late_s

    def heads(v):
        return v[0:1] + v[1:2] + v[2:3] + v[3:4], v[4:5] + v[5:6] + v[6:7] + v[7:8]

    gain_heads, shift_heads, ce_sum = heads(gain_row), heads(shift_row), heads(ce)[0]
    lane5 = iota((1, ch), 1)
    low = jnp.where(lane5 < 32, gain_heads[0], gain_heads[1])
    high = jnp.where(lane5 < 96, shift_heads[0], shift_heads[1])
    r.st5[2:3, :] = jnp.where(lane5 < 64, low, jnp.where(lane5 < 128, high, ce_sum))
    x_send(4, r.st5, r.t5)
    group_wait(3, r.te)
    r.stl[...] = jnp.sum(r.te[...], axis=0)
    line_send(7, r.stl, r.tl)
    r.fd_own[...] = jnp.zeros_like(r.fd_own)
    r.fd_own[0:8, :] = flat_f
    r.fd_own[8:16, 0 : s.mp] = dl
    r.fd[gx, q, c] = r.fd_own[...].astype(bf16)
    g_start(2 * n1 + 1)
    flip(r.wt2, r.wb2)
    scaled_long = dnh_long * scale_p
    dnh_heads = [jnp.sum(scaled_long[nb * k : nb * k + nb], axis=0, keepdims=True) for k in range(2)]
    xhat_long = (p_long[0:2] - mean_long) * inv_long
    xhat_long = jnp.where(valid_long[0:1], xhat_long, 0.0)
    row = iota((16, s.long), 0)
    terms_long = jnp.where(valid_long[0:1], 1.0, 0.0)
    for n, value in ((0, dnh_heads[0]), (1, dnh_heads[1]), (3, xhat_long[0:1]), (4, xhat_long[1:2])):
        terms_long = jnp.where(row == n, value, terms_long)
    terms_long = jnp.where(row < 5, terms_long, 0.0)
    r.terms[...] = terms_long.astype(bf16)
    tall_terms = jnp.concatenate([terms_long, jnp.zeros((lanes - 16, s.long), f32)], axis=0)
    r.terms_t[...] = jnp.transpose(tall_terms).astype(bf16)
    x_wait(4, r.t5)
    group_wait(7, r.tl)
    te = jnp.sum(r.tl[...], axis=0)
    t5 = jnp.sum(r.t5[...], axis=0)
    sums = t5[2:3]
    gain_sums, shift_sums = (sums[:, 0:1], sums[:, 32:33]), (sums[:, 64:65], sums[:, 96:97])
    r.tiny[0:1, :] = jnp.broadcast_to(sums[:, 128:129] / float(nb * s.n_dev), (1, lanes))
    first_lane = iota((1, lanes), 1) == 0
    r.tiny[1:2, :] = jnp.where(first_lane, *gain_sums)
    r.tiny[2:3, :] = jnp.where(first_lane, *shift_sums)
    g2s, s2s = t5[0:1], t5[1:2]
    for k in range(2):
        weight = (hc0, hc1)[k] * (scale_p[nb * k : nb * k + 1] / s.count)
        gain_part = gain_sums[k] * inv_p[nb * k : nb * k + 1]
        mean_k = mean_p[nb * k : nb * k + 1]
        s2s = s2s - weight * (shift_sums[k] * te[0:1] + gain_part * (te[k + 1 : k + 2] - mean_k * te[0:1]))
        g2s = g2s - weight * (shift_sums[k] * te[4:5] + gain_part * (te[k + 5 : k + 6] - mean_k * te[4:5]))
    scales = [scale_p[nb * k : nb * k + 1] / s.count for k in range(2)]
    ones_of = [shift_sums[k] * scales[k] for k in range(2)]
    xhat_of = [gain_sums[k] * scales[k] for k in range(2)]

    row = iota((lanes, ch), 0)
    mix = jnp.where(row == 0, hc0, jnp.where(row == 1, hc1, 0.0))
    mix = jnp.where(row == 2, -(hc0 * ones_of[0] + hc1 * ones_of[1]), mix)
    mix = jnp.where(row == 3, -hc0 * xhat_of[0], jnp.where(row == 4, -hc1 * xhat_of[1], mix))
    r.up[...] = dot(r.terms_t[...], mix.astype(bf16))

    def sums_back(field, xhat, carry):
        f = field.reshape(br // 8, 8, ch)
        g = (field * xhat).reshape(br // 8, 8, ch)
        return carry[0] + jnp.sum(g, axis=0), carry[1] + jnp.sum(f, axis=0)

    def to_field2(i, _):
        at = rows_of(i)
        xhat = (r.h2[at, :] - mean2) * inv2
        dz = r.cot_s[at, :] + r.up[at, :] * r.dz[at, :]
        r.dz[at, :] = dz
        d = (gain2 * inv2) * (dz - (s2s + xhat * g2s) * (1.0 / s.count))
        store3(r.d3, i, jnp.where(inside, d, 0.0))
        return 0

    lax.fori_loop(0, s.side, to_field2, 0)

    def wgrad(planes_t, di):
        start = pl.multiple_of(2 * br - br * di, 16)
        return dot(planes_t[...], r.d3[pl.ds(start, s.rows), :])

    def leave(planes_t, first, b):
        def one(di, _):
            rs_fill(di, wgrad(planes_t, di), b)
            if s.fast:
                rs_cross(b, di)
            return 0

        lax.fori_loop(first, 3, one, 0)
        rs_fill_rest(b)
        if not s.fast:
            rs_cross(b, 0)

    early = 1 if s.fast else 0
    for di in range(early):
        rs_fill(di, wgrad(r.at, di), rs2)
        rs_cross(rs2, di)
    g_forward(2 * n1 + 1)
    conv(r.d3, r.wb2, r.h2)

    def back1(i, carry):
        at = rows_of(i)
        dn = jnp.where(inside, r.h2[at, :] * r.back1[at, :], 0.0)
        r.h2[at, :] = dn
        return sums_back(dn, (r.h1[at, :] - mean1) * inv1, carry)

    g1, s1 = lax.fori_loop(0, s.side, back1, (zero, zero))
    r.st6[0:1, :] = jnp.sum(g1, axis=0, keepdims=True)
    r.st6[1:2, :] = jnp.sum(s1, axis=0, keepdims=True)
    x_send(5, r.st6, r.t6)
    for part in range(early):
        rs_plane(rs2, part)
    leave(r.at, early, rs2)
    for part in range(early, s.nch - 1):
        rs_plane(rs2, part)
    g_cross(2 * n1 + 1)
    rs_plane(rs2, s.nch - 1)
    against_out = dot(r.terms[...], r.out_r[...])
    for k in range(2):
        r.sth[k : k + 1, :] = (
            against_out[k : k + 1] - ones_of[k] * against_out[2:3] - xhat_of[k] * against_out[k + 3 : k + 4]
        )
    x_send(6, r.sth, r.th)
    x_wait(5, r.t6)
    t6 = jnp.sum(r.t6[...], axis=0)
    g1s, s1s = t6[0:1], t6[1:2]

    def to_field1(i, _):
        at = rows_of(i)
        xhat = (r.h1[at, :] - mean1) * inv1
        d = (gain1 * inv1) * (r.h2[at, :] - (s1s + xhat * g1s) * (1.0 / s.count))
        store3(r.d3, i, jnp.where(inside, d, 0.0))
        return 0

    lax.fori_loop(0, s.side, to_field1, 0)
    leave(r.xt, 0, rs1)
    for part in range(s.nch):
        rs_plane(rs1, part)
    conv(r.d3, r.wb1, r.h1)
    for part in range(s.nch):
        rs_line(rs2, part)

    def result(i, _):
        at = rows_of(i)
        r.in_grad_v[i] = to_board(r.dz[at, :] + r.h1[at, :])
        return 0

    lax.fori_loop(0, s.side, result, 0)
    put_in_grad = pltpu.make_async_copy(r.in_grad_v, r.in_grad, r.local_sem.at[len(names) + 1])
    put_in_grad.start()
    x_wait(6, r.th)
    shares = jnp.concatenate([g1s, g2s, s1s, s2s, jnp.sum(r.th[...], axis=0), jnp.zeros((2, ch), f32)], axis=0)
    r.tiny[8:16, :] = pltpu.roll(shares, lax.rem(ch - w * me, ch), 1)[:, 0:lanes]

    for part in range(s.nch):
        rs_line(rs1, part)

    g_done(2 * n1 + 1)
    fd = r.fd[...].astype(f32).reshape(s.n_dev, 16, s.line)
    features = fd[:, 0:8, :].reshape(8 * s.n_dev, s.line).astype(bf16)
    dls = fd[:, 8:16, 0 : s.mp].reshape(8 * s.n_dev, s.mp).astype(bf16)
    t = iota((s.rp, 1), 0)
    source = s.rsh * me + t
    mine = (t < s.rsh) & (source < s.head_in)
    col = iota((s.rp, s.line), 1)
    col8 = iota((s.rp, 8 * s.n_dev), 1) & 7
    own = jnp.where((t < s.rsh) & (source == s.head_in) & (col8 < nb), 1.0, 0.0)
    for k in range(2):
        in_k = mine & (source >= k * s.cells) & (source < (k + 1) * s.cells)
        cell = jnp.where(in_k, source - k * s.cells, 0)
        cell_i = divided(cell, s.side, s.cells)
        place = jnp.where(in_k, cell_i * wide + (cell - cell_i * s.side), -1)
        pick = (col == place).astype(f32).astype(bf16)
        rows_k = dot_nt(pick, features)
        own = own + jnp.where((col8 >= nb) if k else (col8 < nb), rows_k, 0.0)
    grad = dot(own.astype(bf16), dls)
    r.dense_grad[...] = grad

    for part in range(s.nch):
        rs_finish(rs2, part, r.c2_grad)
    for part in range(s.nch):
        rs_finish(rs1, part, r.c1_grad)

    for u in range(len(units)):
        g_drain(u)
    for number, slots in enumerate((r.t1, r.t2, r.t3, None, r.t5, r.t6, r.th)):
        if number != 3:
            x_drain(number, slots)
    group_wait(3, r.te, 0)
    group_wait(7, r.tl, 0)
    rs_drain(rs1)
    rs_drain(rs2)
    put_out.wait()
    put_in_grad.wait()


def place(w, x_ref, in_x_ref, c1, c2, dense, tiny, *refs):
    (out, loss, in_grad, c1_out, c2_out, gains, shifts, hc, hng, dense_out), refs = refs[:10], refs[10:]
    (out_v, in_v, c1_v, c2_v, dense_v, tiny_v), (came, went) = refs[:6], refs[6:]
    side = out.shape[0]
    cuts = [(n * side // 2, (n + 1) * side // 2) for n in range(2)]
    moves = [(x_ref, out_v, out), (in_x_ref, in_v, in_grad)]
    moves = [tuple(v.at[pl.ds(a, b - a)] for v in move) for move in moves for a, b in cuts]
    moves += [(c1, c1_v, c1_out), (c2, c2_v, c2_out)]
    fetch = [pltpu.make_async_copy(a, b, came.at[n]) for n, (a, b, _) in enumerate(moves)]
    put = [pltpu.make_async_copy(b, d, went.at[n]) for n, (_, b, d) in enumerate(moves)]
    fetch += [
        pltpu.make_async_copy(a, b, came.at[len(moves) + n])
        for n, (a, b) in enumerate(((tiny, tiny_v), (dense, dense_v)))
    ]
    for copy in fetch:
        copy.start()
    for n in range(len(moves)):
        fetch[n].wait()
        put[n].start()
    fetch[-2].wait()
    fetch[-1].wait()
    loss[...] = tiny_v[0:1, 0:1]
    hng[...] = tiny_v[1:3, 0:2]
    gains[...] = tiny_v[8:10, 0:w]
    shifts[...] = tiny_v[10:12, 0:w]
    hc[...] = tiny_v[12:14, 0:w]
    dense_out[...] = dense_v[0 : dense_out.shape[0], 0 : dense_out.shape[1]]
    for copy in put:
        copy.wait()


def body(x, w1, w2, gains, shifts, hc, hng, hns, dense, legal, target, cot):
    x, cot = (jnp.transpose(v, (1, 2, 0, 3)) for v in (x, cot))
    s = sizes_of(lax.axis_size("gx"), lax.axis_size("gy"), x, w1, dense, legal.shape[1])
    vmem, hbm = pltpu.VMEM, pl.ANY
    inputs = dict(
        x=x, w1=w1, w2=w2, gains=gains, shifts=shifts, hc=hc, hng=hng, hns=hns, dense=dense, legal=legal,
        target=target, cot=cot,
    )
    outputs = dict(
        out=(x.shape, bf16), in_grad=(x.shape, bf16), c1_grad=(w1.shape, f32), c2_grad=(w2.shape, f32),
        dense_grad=((s.rp, s.mp), f32), tiny=((16, lanes), f32),
    )
    gxn, qn, n, ch = s.gx_n, s.q_n, s.n_dev, s.ch
    field = pltpu.VMEM((s.long, ch), f32)
    boards = pltpu.VMEM((s.side, s.wide, s.nb, ch), bf16)
    planes = pltpu.VMEM((s.padded, 3 * ch), bf16)
    turned = pltpu.VMEM((ch, s.rows), bf16)
    weight = pltpu.VMEM((3, 3 * ch, ch), bf16)
    two = pltpu.VMEM((2, ch), f32)
    eight = pltpu.VMEM((8, ch), f32)
    dma = pltpu.SemaphoreType.DMA
    scratch = dict(
        local_sem=dma((14,)), g_sem=dma((2 * s.nch + 2, 5 + gxn)), x_sem=dma((8, 2)),
        rs_sem1=dma((s.nch, 6)), rs_sem2=dma((s.nch, 6)),
        x_v=boards, cot_v=boards, out_v=pltpu.VMEM(x.shape, bf16), in_grad_v=pltpu.VMEM(x.shape, bf16),
        stage=pltpu.VMEM((s.blk1, lanes), f32), small=pltpu.VMEM((8, lanes), f32),
        s1=pltpu.VMEM((gxn, qn, 2, s.blk1, lanes), bf16), s2=pltpu.VMEM((gxn, qn, 2, s.blk, lanes), bf16),
        sd=pltpu.VMEM((gxn, qn, 2, s.rp, s.mp), bf16), dense_f=pltpu.VMEM((s.rp, s.mp), f32),
        x3=planes, a3=planes, d3=planes, out_r=pltpu.VMEM((s.long, ch), bf16), terms=pltpu.VMEM((16, s.long), bf16), terms_t=pltpu.VMEM((s.long, lanes), bf16),
        xt=turned, at=turned, wt1=weight, wt2=weight, wb1=weight, wb2=weight,
        pars=pltpu.VMEM((8, ch), f32), h1=field, h2=field, dz=field, back1=field, up=field, cot_s=field,
        st1=two, t1=pltpu.VMEM((n, 2, ch), f32), st2=two, t2=pltpu.VMEM((n, 2, ch), f32),
        st3=pltpu.VMEM((1, lanes), f32), t3=pltpu.VMEM((n, 1, lanes), f32), ste=eight, te=pltpu.VMEM((s.gy_n, 8, ch), f32), stl=eight, tl=pltpu.VMEM((gxn, 8, ch), f32),
        st5=pltpu.VMEM((3, ch), f32), t5=pltpu.VMEM((n, 3, ch), f32), st6=two, t6=pltpu.VMEM((n, 2, ch), f32),
        sth=two, th=pltpu.VMEM((n, 2, ch), f32), vu=pltpu.VMEM((s.long, 2 * ch), bf16),
        fd_own=pltpu.VMEM((16, s.line), f32), fd=pltpu.VMEM((gxn, qn, 2, 16, s.line), bf16),
        dk=pltpu.VMEM((2, s.line, s.mp), bf16), expand=pltpu.VMEM((s.long, s.line), bf16),
        legal_both=pltpu.VMEM((8, s.mp), jnp.int32),
    )
    for name in ("w1", "w2", "gains", "shifts", "hc", "dense", "legal"):
        scratch[name + "_v"] = pltpu.VMEM(inputs[name].shape, inputs[name].dtype)
    for name in ("hng", "hns", "target"):
        scratch[name + "_v"] = pltpu.SMEM(inputs[name].shape, inputs[name].dtype)
    if not s.fast:
        scratch["flat"] = pltpu.VMEM((9, ch, ch), f32)
        scratch["eight"] = pltpu.VMEM((9, 8, ch), f32)
    for number in ("1", "2"):
        scratch["rsb" + number] = pltpu.VMEM((s.nch, 2, gxn, qn, s.crows, lanes), bf16)
        scratch["rc" + number] = pltpu.VMEM((s.nch, gxn, qn, s.crows, lanes), bf16)
        scratch["pb" + number] = pltpu.VMEM((s.nch, qn, gxn, s.crows, lanes), bf16)
        scratch["rp" + number] = pltpu.VMEM((s.nch, qn - 1, gxn, s.crows, lanes), bf16)
        scratch["zb" + number] = pltpu.VMEM((s.nch, gxn, s.crows, lanes), bf16)
        scratch["rd" + number] = pltpu.VMEM((gxn * qn - 1, s.crows, lanes), bf16)
        scratch["rz" + number] = pltpu.VMEM((s.nch, gxn - 1, s.crows, lanes), bf16)
    run = pl.pallas_call(
        functools.partial(kernel, s, tuple(inputs), tuple(outputs), tuple(scratch)),
        out_shape=[jax.ShapeDtypeStruct(shape, kind) for shape, kind in outputs.values()],
        in_specs=[pl.BlockSpec(memory_space=hbm) for _ in inputs],
        out_specs=[pl.BlockSpec(memory_space=hbm if n in ("out", "in_grad") else vmem) for n in outputs],
        scratch_shapes=list(scratch.values()),
        compiler_params=pltpu.CompilerParams(
            collective_id=0, has_side_effects=True, vmem_limit_bytes=60 * 1024 * 1024
        ),
        cost_estimate=pl.CostEstimate(flops=10_500_000_000, bytes_accessed=8_000_000, transcendentals=800_000),
        name="tower",
    )
    results = run(*inputs.values())
    kinds = [jax.ShapeDtypeStruct(v.shape, v.dtype) for v in results]
    out, in_grad, c1_grad, c2_grad, dense_grad, _ = kinds
    small = [jax.ShapeDtypeStruct(v.shape, f32) for v in (gains, shifts, hc)]
    loss, pair = (jax.ShapeDtypeStruct(shape, f32) for shape in ((1, 1), (2, 2)))
    shapes = [out, loss, in_grad, c1_grad, c2_grad, *small, pair, jax.ShapeDtypeStruct(dense.shape, f32)]
    results = pl.pallas_call(
        functools.partial(place, s.w),
        out_shape=shapes,
        in_specs=[pl.BlockSpec(memory_space=hbm) for _ in kinds],
        out_specs=[pl.BlockSpec(memory_space=hbm if n in (0, 2, 3, 4) else vmem) for n in range(len(shapes))],
        scratch_shapes=[pltpu.VMEM(v.shape, v.dtype) for v in kinds] + [dma((16,))] * 2,
        name="place",
    )(*results)
    out, loss, in_grad, *rest = results
    out, in_grad = (jnp.transpose(v, (2, 0, 1, 3)) for v in (out, in_grad))
    return (out, loss.reshape(()), in_grad, *rest)


def solution(mesh):
    both = ("gx", "gy")
    board = P(both, None, None, None)
    kernels = P(None, both, None)
    pairs = P(None, both)
    return jax.shard_map(
        body,
        mesh=mesh,
        in_specs=(
            board, kernels, kernels, pairs, pairs, pairs, P(), P(), P(both, None), P(both, None), P(both), board,
        ),
        out_specs=(board, P(), board, kernels, kernels, pairs, pairs, pairs, P(), P(both, None)),
        check_vma=False,
    )
```

```python
import functools
import types

import jax
import jax.numpy as jnp
from jax import lax
from jax.experimental import pallas as pl
from jax.experimental.pallas import tpu as pltpu
from jax.sharding import PartitionSpec as P

MESH = pl.DeviceIdType.MESH
f32 = jnp.float32
bf16 = jnp.bfloat16
epsilon = 1e-05
negative_fill = -1e30
root = 0.7978845608028654
cube = 0.044715
lanes = 128


def up_to(value, unit):
    return -(-value // unit) * unit


def divided(values, divisor, limit):
    for shift in range(16, 24):
        factor = -(-(1 << shift) // divisor)
        if all((n * factor) >> shift == n // divisor and n * factor < 2**31 for n in range(limit)):
            return lax.shift_right_logical(values * factor, jnp.int32(shift))
    raise ValueError("no factor")


def iota(shape, axis):
    return lax.broadcasted_iota(jnp.int32, shape, axis)


def gelu_both(v):
    square = v * v
    slope = jnp.tanh(v * (root + (root * cube) * square))
    half = 0.5 + 0.5 * slope
    back = half + (0.5 * v) * (1.0 - slope * slope) * (root + (3.0 * root * cube) * square)
    return v * half, back


def gelu(v):
    half = 0.5 * v
    return half + half * jnp.tanh(v * (root + (root * cube) * (v * v)))


def dot(left, right):
    return jnp.dot(left, right, preferred_element_type=f32)


def dot_nt(left, right):
    return lax.dot_general(left, right, (((1,), (1,)), ((), ())), preferred_element_type=f32)


def sizes_of(gx_n, gy_n, x, w1, dense, moves):
    s = types.SimpleNamespace()
    s.gx_n, s.gy_n, s.q_n, s.n_dev = gx_n, gy_n, gy_n // 2, gx_n * gy_n
    s.side, s.nb, s.ch = x.shape[0], x.shape[2], x.shape[3]
    s.w = w1.shape[1]
    s.wide = s.side + 1
    s.br = s.wide * s.nb
    s.rows = s.side * s.br
    s.line = up_to(s.side * s.wide, lanes)
    s.long = up_to(s.rows, 3 * lanes)
    s.padded = s.long + 2 * s.br
    s.cells = s.side * s.side
    s.moves = moves
    s.mp = up_to(moves, lanes)
    s.rsh = dense.shape[0]
    s.rp = up_to(s.rsh, 16)
    s.head_in = 2 * s.cells
    s.blk = up_to(18 * s.w, 16)
    s.blk1 = up_to(19 * s.w, 16)
    s.fast = s.w == 8
    s.nch = 3 if s.fast else 1
    s.crows = s.blk // s.nch
    s.count = float(s.nb * s.cells * s.n_dev)
    assert s.nb == 4 and s.br % 16 == 0 and 8 % s.w == 0
    assert gx_n & (gx_n - 1) == 0 and gy_n & (gy_n - 1) == 0 and gy_n > 1
    return s


def kernel(s, in_names, out_names, scratch_names, *refs):
    r = types.SimpleNamespace(**dict(zip(in_names + out_names + scratch_names, refs)))
    gx, gy = lax.axis_index("gx"), lax.axis_index("gy")
    q, c = lax.div(gy, 2), lax.rem(gy, 2)
    me = gx * s.gy_n + gy
    other = (gx, gy + 1 - 2 * c)
    gxn, qn, nb, br, wide, ch = s.gx_n, s.q_n, s.nb, s.br, s.wide, s.ch

    def z_peer(k):
        return gx ^ k

    def q_peer(j):
        return q ^ j

    def send(src, dst, out_sem, in_sem, device):
        pltpu.make_async_remote_copy(
            src_ref=src, dst_ref=dst, send_sem=out_sem, recv_sem=in_sem, device_id=device, device_id_type=MESH
        ).start()

    def take(sem, ref):
        pltpu.make_async_copy(ref, ref, sem).wait()

    barrier = pltpu.get_barrier_semaphore()
    partners = [(z_peer(k), gy) for k in range(1, gxn)]
    partners += [(gx, 2 * q_peer(j) + c) for j in range(1, qn)]
    partners += [other]
    for p in partners:
        pl.semaphore_signal(barrier, inc=1, device_id=p, device_id_type=MESH)
    names = ("x", "w1", "w2", "gains", "shifts", "hc", "dense", "cot", "legal", "hng", "hns", "target")
    fetch = {}
    for n, name in enumerate(names):
        held = getattr(r, name + "_v")
        held = held.at[:, pl.ds(0, s.side)] if name in ("x", "cot") else held
        fetch[name] = pltpu.make_async_copy(getattr(r, name), held, r.local_sem.at[n])
        fetch[name].start()
    for fields in (r.x_v, r.cot_v):
        fields[:, s.side] = jnp.zeros((s.side, nb, ch), bf16)

    w = s.w

    def stage(weight):
        r.stage[...] = jnp.zeros_like(r.stage)
        for t in range(9):
            v = weight[t].astype(f32)
            r.stage[2 * w * t : 2 * w * t + w, :] = v[:, :lanes]
            r.stage[2 * w * t + w : 2 * w * t + 2 * w, :] = v[:, lanes:]

    def stage_all():
        for name in names[1:7]:
            fetch[name].wait()
        r.small[...] = jnp.zeros_like(r.small)
        r.small[0:2, 0:w] = r.gains_v[...].astype(f32)
        r.small[2:4, 0:w] = r.shifts_v[...].astype(f32)
        r.small[4:6, 0:w] = r.hc_v[...].astype(f32)
        stage(r.w1_v)
        r.stage[18 * w : 19 * w, 0:8] = jnp.transpose(r.small[...])[0:w, :]
        r.s1[gx, q, c] = r.stage[...].astype(bf16)
        stage(r.w2_v)
        r.s2[gx, q, c] = r.stage[0 : s.blk, :].astype(bf16)
        r.dense_f[...] = jnp.zeros_like(r.dense_f)
        r.dense_f[0 : s.rsh, 0 : s.moves] = r.dense_v[...].astype(f32)
        r.sd[gx, q, c] = r.dense_f[...].astype(bf16)

    for planes in (r.x3, r.a3, r.d3):
        planes[0:br, :] = jnp.zeros((br, 3 * ch), bf16)
        planes[br + s.rows :, :] = jnp.zeros((s.padded - br - s.rows, 3 * ch), bf16)
    inside = iota((br, ch), 0) < nb * s.side

    def store3(planes, i, block):
        at = pl.ds(pl.multiple_of((i + 1) * br, 16), br)
        planes[at, 0:ch] = pltpu.roll(block, nb, 0).astype(bf16)
        planes[at, ch : 2 * ch] = block.astype(bf16)
        planes[at, 2 * ch :] = pltpu.roll(block, br - nb, 0).astype(bf16)

    def rows_of(i):
        return pl.ds(pl.multiple_of(i * br, 16), br)

    def from_board(block):
        return block.astype(f32).reshape(br, ch)

    def to_board(block):
        return block.reshape(wide, nb, ch)[0 : s.side].astype(bf16)

    def x_rows(i, _):
        store3(r.x3, i, from_board(r.x_v[i]))
        return 0

    fetch["x"].wait()
    lax.fori_loop(0, s.side, x_rows, 0)
    stage_all()

    pl.semaphore_wait(barrier, len(partners))

    def span(unit):
        store, part = unit
        if store is r.sd or store is r.fd:
            return pl.ds(0, store.shape[3])
        whole = s.blk1 if store is r.s1 else s.blk
        if s.nch == 1:
            return pl.ds(0, whole)
        start = part * s.crows
        return pl.ds(start, whole - start if part == s.nch - 1 else s.crows)

    units = [(r.s1, p) for p in range(s.nch)] + [(r.s2, p) for p in range(s.nch)] + [(r.sd, 0), (r.fd, 0)]

    turned = {s.nch} if s.nch > 1 else set()

    def g_start(u):
        store, at = units[u][0], span(units[u])
        own = store.at[gx, q, c, at]
        for k in range(1, gxn):
            if u not in turned:
                send(own, own, r.g_sem.at[u, 0], r.g_sem.at[u, 5 + k], (z_peer(k), gy))
        for j in range(qn - 1, 0, -1):
            send(own, own, r.g_sem.at[u, 1], r.g_sem.at[u, 4], (gx, 2 * q_peer(j) + c))

    def g_forward(u):
        store, at = units[u][0], span(units[u])
        if u in turned:
            take(r.g_sem.at[u, 4], store.at[gx, pl.ds(0, qn - 1), 0, at])
            block = store.at[gx, :, c, at]
            for k in range(gxn - 1, 0, -1):
                send(block, block, r.g_sem.at[u, 2], r.g_sem.at[u, 5 + k], (z_peer(k), gy))
            return
        for k in range(1, gxn):
            block = store.at[z_peer(k), q, c, at]
            take(r.g_sem.at[u, 5 + k], block)
            for j in range(qn - 1, 0, -1):
                send(block, block, r.g_sem.at[u, 2], r.g_sem.at[u, 4], (gx, 2 * q_peer(j) + c))

    def g_cross(u):
        store, at = units[u][0], span(units[u])
        if u in turned:
            for k in range(1, gxn):
                take(r.g_sem.at[u, 5 + k], store.at[z_peer(k), :, c, at])
        else:
            take(r.g_sem.at[u, 4], store.at[:, pl.ds(0, qn - 1), 0, at])
        block = store.at[:, :, c, at]
        send(block, block, r.g_sem.at[u, 3], r.g_sem.at[u, 5], other)

    def g_done(u):
        store, at = units[u][0], span(units[u])
        take(r.g_sem.at[u, 5], store.at[:, :, 0, at])

    def g_drain(u):
        store, at = units[u][0], span(units[u])
        take(r.g_sem.at[u, 1], store.at[0, pl.ds(0, qn - 1), 0, at])
        if u in turned:
            take(r.g_sem.at[u, 2], store.at[pl.ds(0, gxn - 1), :, 0, at])
        else:
            take(r.g_sem.at[u, 0], store.at[pl.ds(0, gxn - 1), 0, 0, at])
            take(r.g_sem.at[u, 2], store.at[pl.ds(0, gxn - 1), pl.ds(0, qn - 1), 0, at])
        take(r.g_sem.at[u, 3], store.at[:, :, 0, at])

    def shard_of(store, d):
        return store[lax.div(d, s.gy_n), lax.div(lax.rem(d, s.gy_n), 2), lax.rem(d, 2)]

    def unpack(store, part, weight):
        if s.fast:
            for dj in range(3):
                at = 16 * (3 * part + dj)
                v = store[:, :, :, at : at + 16, :].astype(f32).reshape(s.n_dev, 16, lanes)
                low = v[:, 0:8, :].reshape(ch, lanes)
                high = v[:, 8:16, :].reshape(ch, lanes)
                weight[part, dj * ch : (dj + 1) * ch, :] = jnp.concatenate([low, high], axis=1).astype(bf16)
            return

        def one(g, _):
            for e in range(8 // w):
                r.stage[0 : s.blk, :] = shard_of(store, g * (8 // w) + e)[0 : s.blk].astype(f32)
                for t in range(9):
                    r.eight[t, w * e : w * e + w, 0:lanes] = r.stage[2 * w * t : 2 * w * t + w, :]
                    r.eight[t, w * e : w * e + w, lanes:] = r.stage[2 * w * t + w : 2 * w * t + 2 * w, :]
            for t in range(9):
                r.flat[t, pl.ds(pl.multiple_of(8 * g, 8), 8), :] = r.eight[t]
            return 0

        lax.fori_loop(0, ch // 8, one, 0)
        for t in range(9):
            weight[t // 3, (t % 3) * ch : (t % 3 + 1) * ch, :] = r.flat[t].astype(bf16)

    def unpack_small():
        if s.fast:
            v = r.s1[:, :, :, 18 * w : 18 * w + 16, :].astype(f32).reshape(s.n_dev, 16, lanes)
            rows = v[:, 0:8, :].reshape(ch, lanes)
        else:

            def one(g, _):
                for e in range(8 // w):
                    r.stage[...] = shard_of(r.s1, g * (8 // w) + e).astype(f32)
                    r.eight[0, w * e : w * e + w, 0:lanes] = r.stage[18 * w : 19 * w, :]
                r.flat[0, pl.ds(pl.multiple_of(8 * g, 8), 8), :] = r.eight[0]
                return 0

            lax.fori_loop(0, ch // 8, one, 0)
            rows = r.flat[0, :, 0:lanes]
        r.pars[...] = jnp.transpose(rows)[0:8, :]

    def x_send(number, src, slots):
        def one(k):
            device = (gx ^ lax.div(k, s.gy_n), gy ^ lax.rem(k, s.gy_n))
            send(src, slots.at[me], r.x_sem.at[number, 0], r.x_sem.at[number, 1], device)

        if s.n_dev <= 64:
            hops = {k: k // s.gy_n + bin(k % s.gy_n // 2).count("1") for k in range(1, s.n_dev)}
            for k in sorted(hops, key=lambda k: (-hops[k], k)):
                send(
                    src, slots.at[me], r.x_sem.at[number, 0], r.x_sem.at[number, 1],
                    (gx ^ (k // s.gy_n), gy ^ (k % s.gy_n)),
                )
        else:
            lax.fori_loop(0, s.n_dev - 1, lambda n, _: (one(s.n_dev - 1 - n), 0)[1], 0)
        slots[me] = src[...]

    def x_wait(number, slots):
        take(r.x_sem.at[number, 1], slots.at[pl.ds(0, s.n_dev - 1)])

    def x_drain(number, slots):
        take(r.x_sem.at[number, 0], slots.at[pl.ds(0, s.n_dev - 1)])

    def plane_send(number, src, slots):
        for k in range(s.gy_n - 1, 0, -1):
            send(src, slots.at[gy], r.x_sem.at[number, 0], r.x_sem.at[number, 1], (gx, gy ^ k))
        slots[gy] = src[...]

    def line_send(number, src, slots):
        for k in range(gxn - 1, 0, -1):
            send(src, slots.at[gx], r.x_sem.at[number, 0], r.x_sem.at[number, 1], (gx ^ k, gy))
        slots[gx] = src[...]

    def group_wait(number, slots, way=1):
        take(r.x_sem.at[number, way], slots.at[pl.ds(0, slots.shape[0] - 1)])

    def rs_fill(part, grad, b):
        if s.fast:
            for dj in range(3):
                g = grad[:, (2 - dj) * ch : (3 - dj) * ch]
                low = g[:, :lanes].reshape(s.n_dev, 8, lanes)
                high = g[:, lanes:].reshape(s.n_dev, 8, lanes)
                v = jnp.concatenate([low, high], axis=1).astype(bf16).reshape(gxn, qn, 2, 16, lanes)
                for core in range(2):
                    b.rsb[part, core, :, :, 16 * dj : 16 * dj + 16, :] = v[:, :, core]
        else:
            for dj in range(3):
                r.flat[3 * part + dj] = grad[:, (2 - dj) * ch : (3 - dj) * ch]

    def rs_fill_rest(b):
        if s.fast:
            return
        r.stage[...] = jnp.zeros_like(r.stage)

        def one(g, _):
            for t in range(9):
                r.eight[t] = r.flat[t, pl.ds(pl.multiple_of(8 * g, 8), 8), :]
            for e in range(8 // w):
                d = g * (8 // w) + e
                for t in range(9):
                    v = r.eight[t, w * e : w * e + w, :]
                    r.stage[2 * w * t : 2 * w * t + w, :] = v[:, :lanes]
                    r.stage[2 * w * t + w : 2 * w * t + 2 * w, :] = v[:, lanes:]
                at = (0, lax.rem(d, 2), lax.div(d, s.gy_n), lax.div(lax.rem(d, s.gy_n), 2))
                b.rsb[at] = r.stage[0 : s.blk, :].astype(bf16)
            return 0

        lax.fori_loop(0, ch // 8, one, 0)

    def rs_cross(b, part):
        send(b.rsb.at[part, 1 - c], b.rc.at[part], b.sem.at[part, 0], b.sem.at[part, 1], other)

    def rs_plane(b, part):
        take(b.sem.at[part, 1], b.rc.at[part])
        for p in range(qn):
            total = b.rsb[part, c, :, p].astype(f32) + b.rc[part, :, p].astype(f32)
            b.pb[part, p] = total.astype(bf16)
        if s.nch > 1 and part == s.nch - 1:
            for k in range(gxn - 1, -1, -1):
                for j in range(qn - 1, -1, -1):
                    if k + j:
                        block = b.pb.at[part, q_peer(j), z_peer(k)]
                        device = (z_peer(k), 2 * q_peer(j) + c)
                        send(block, b.rd.at[k * qn + j - 1], b.sem.at[part, 2], b.sem.at[part, 3], device)
            return
        for j in range(1, qn):
            to = q_peer(j)
            send(b.pb.at[part, to], b.rp.at[part, j - 1], b.sem.at[part, 2], b.sem.at[part, 3], (gx, 2 * to + c))

    def rs_line(b, part):
        if s.nch > 1 and part == s.nch - 1:
            return
        take(b.sem.at[part, 3], b.rp.at[part])
        total = b.pb[part, q].astype(f32)
        for j in range(qn - 1):
            total = total + b.rp[part, j].astype(f32)
        b.zb[part] = total.astype(bf16)
        for k in range(1, gxn):
            to = z_peer(k)
            send(b.zb.at[part, to], b.rz.at[part, k - 1], b.sem.at[part, 4], b.sem.at[part, 5], (to, gy))

    def rs_finish(b, part, out):
        if s.nch > 1 and part == s.nch - 1:
            take(b.sem.at[part, 3], b.rd)
            total = b.pb[part, q, gx].astype(f32) + jnp.sum(b.rd[...].astype(f32), axis=0)
        else:
            take(b.sem.at[part, 5], b.rz.at[part])
            total = b.zb[part, gx].astype(f32)
            for k in range(gxn - 1):
                total = total + b.rz[part, k].astype(f32)
        taps = 9 // s.nch
        for t in range(taps):
            at = 2 * w * t
            out[part * taps + t] = jnp.concatenate([total[at : at + w], total[at + w : at + 2 * w]], axis=1)

    def rs_drain(b):
        for part in range(s.nch):
            take(b.sem.at[part, 0], b.rc.at[part])
            if s.nch > 1 and part == s.nch - 1:
                take(b.sem.at[part, 2], b.rd)
                continue
            take(b.sem.at[part, 2], b.rp.at[part])
            take(b.sem.at[part, 4], b.rz.at[part])

    def rs_buffers(number):
        names = ("rsb", "rc", "pb", "rp", "zb", "rz", "rd")
        b = types.SimpleNamespace(**{n: getattr(r, n + number) for n in names})
        b.sem = getattr(r, "rs_sem" + number)
        return b

    rs1, rs2 = rs_buffers("1"), rs_buffers("2")

    def local_stats(field, out):
        pivot = field[0:1, :]

        def one(i, carry):
            d = jnp.where(inside, field[rows_of(i), :] - pivot, 0.0).reshape(br // 8, 8, ch)
            return carry[0] + jnp.sum(d, axis=0), carry[1] + jnp.sum(d * d, axis=0)

        zero = jnp.zeros((8, ch), f32)
        first, second = lax.fori_loop(0, s.side, one, (zero, zero))
        n = float(nb * s.cells)
        first = jnp.sum(first, axis=0, keepdims=True) / n
        second = jnp.sum(second, axis=0, keepdims=True) - n * first * first
        out[0:1, :] = pivot + first
        out[1:2, :] = second

    def global_stats(slots):
        v = slots[...]
        n = float(nb * s.cells)
        mean = jnp.sum(v[:, 0:1, :], axis=0) / s.n_dev
        d = v[:, 0:1, :] - mean
        spread_sum = jnp.sum(v[:, 1:2, :] + n * d * d, axis=0)
        return mean, lax.rsqrt(spread_sum / s.count + epsilon)

    n1 = s.nch
    for u in range(n1):
        g_start(u)
    for u in turned:
        g_start(u)
    for u in range(n1, 2 * n1):
        if u not in turned:
            g_start(u)
    for u in range(2 * n1):
        g_forward(u)
    g_start(2 * n1)
    row, col = iota((s.long, s.line), 0), iota((s.long, s.line), 1)
    r.expand[...] = (col == lax.shift_right_logical(row, 2)).astype(f32).astype(bf16)
    r.out_r[s.rows :, :] = jnp.zeros((s.long - s.rows, ch), bf16)
    r.vu[s.rows :, :] = jnp.zeros((s.long - s.rows, 2 * ch), bf16)
    r.xt[...] = jnp.transpose(r.x3[br : br + s.rows, ch : 2 * ch])
    for u in range(n1):
        g_cross(u)

    def conv_part(planes, weight, di, out):
        v = dot(planes[br * di : br * di + s.rows, :], weight[di])
        out[0 : s.rows, :] = v if di == 0 else out[0 : s.rows, :] + v

    chunk = s.long // 2

    def conv(planes, weight, out):
        def one(k, _):
            at = pl.multiple_of(k * chunk, 16)
            v = dot(planes[pl.ds(at, chunk), :], weight[0])
            v = v + dot(planes[pl.ds(at + br, chunk), :], weight[1])
            out[pl.ds(at, chunk), :] = v + dot(planes[pl.ds(at + 2 * br, chunk), :], weight[2])
            return 0

        lax.fori_loop(0, 2, one, 0)

    for part in range(n1):
        g_done(part)
        unpack(r.s1, part, r.wt1)
        if s.fast:
            conv_part(r.x3, r.wt1, part, r.h1)
    if not s.fast:
        conv(r.x3, r.wt1, r.h1)
    local_stats(r.h1, r.st1)
    x_send(0, r.st1, r.t1)

    g_forward(2 * n1)
    unpack_small()
    fetch["cot"].wait()

    def flip(weight, back):
        def one(n, _):
            di, dj = lax.div(n, 3), lax.rem(n, 3)
            tap = weight[2 - di, pl.ds(pl.multiple_of((2 - dj) * ch, ch), ch), :]
            back[di, pl.ds(pl.multiple_of(dj * ch, ch), ch), :] = jnp.transpose(tap)
            return 0

        lax.fori_loop(0, 9, one, 0)

    for u in range(n1, 2 * n1):
        g_cross(u)
    flip(r.wt1, r.wb1)

    gain1, gain2 = r.pars[0:1, :], r.pars[1:2, :]
    shift1, shift2 = r.pars[2:3, :], r.pars[3:4, :]
    hc0, hc1 = r.pars[4:5, :], r.pars[5:6, :]

    x_wait(0, r.t1)
    mean1, inv1 = global_stats(r.t1)

    def act1(i, _):
        n = (r.h1[rows_of(i), :] - mean1) * (inv1 * gain1) + shift1
        a = gelu(n)
        store3(r.a3, i, jnp.where(inside, a, 0.0))
        return 0

    lax.fori_loop(0, s.side, act1, 0)
    for u in range(n1, 2 * n1):
        g_done(u)
        unpack(r.s2, u - n1, r.wt2)
    conv(r.a3, r.wt2, r.h2)
    local_stats(r.h2, r.st2)
    x_send(1, r.st2, r.t2)

    r.at[...] = jnp.transpose(r.a3[br : br + s.rows, ch : 2 * ch])

    def slope1(i, _):
        n = (r.h1[rows_of(i), :] - mean1) * (inv1 * gain1) + shift1
        r.back1[rows_of(i), :] = gelu_both(n)[1]
        return 0

    lax.fori_loop(0, s.side, slope1, 0)
    g_cross(2 * n1)
    g_done(2 * n1)
    at = iota((s.line, 1), 0)
    i_of = divided(at, wide, s.line)
    j_of = at - i_of * wide
    used = (i_of < s.side) & (j_of < s.side)
    wide_slots = s.n_dev * s.rp
    shard_rows = iota((s.line, wide_slots), 1)
    dense_all = r.sd[...].reshape(wide_slots, s.mp)
    for k in range(2):
        source = k * s.cells + i_of * s.side + j_of
        if k == 0:
            source = jnp.where(at == s.side, s.head_in, source)
            wanted = used | (at == s.side)
        else:
            wanted = used
        source = jnp.where(wanted, source, 0)
        shard = divided(source, s.rsh, 1024)
        place = jnp.where(wanted, shard * s.rp + (source - shard * s.rsh), -1)
        pick = (shard_rows == place).astype(f32).astype(bf16)
        r.dk[k] = dot(pick, dense_all).astype(bf16)
    row = iota((16, ch), 0)
    hc_rows = jnp.where(row == 0, hc0, jnp.where(row == 1, hc1, 0.0)).astype(bf16)

    x_wait(1, r.t2)
    mean2, inv2 = global_stats(r.t2)

    def act2(i, _):
        at = rows_of(i)
        xin = r.x3[pl.ds(pl.multiple_of((i + 1) * br, 16), br), ch : 2 * ch].astype(f32)
        z = xin + ((r.h2[at, :] - mean2) * (inv2 * gain2) + shift2)
        r.dz[at, :] = z
        a = jnp.where(inside, gelu(z), 0.0)
        r.out_r[at, :] = a.astype(bf16)
        return 0

    lax.fori_loop(0, s.side, act2, 0)
    p_long = dot_nt(hc_rows, r.out_r[...])[0:8]
    lane = iota((8, s.long), 1)
    lane_j = lane - divided(lane, br, s.long) * br
    valid_long = (lane_j < nb * s.side) & (lane < s.rows)
    row1, lane1 = iota((8, lanes), 0), iota((8, lanes), 1)

    def by_head(v):
        a = v[0:1] + v[1:2] + v[2:3] + v[3:4]
        b = v[4:5] + v[5:6] + v[6:7] + v[7:8]
        return jnp.where(iota(v.shape, 0) < nb, a, b)

    n_local = float(nb * s.cells)
    mean_row = jnp.sum(jnp.where(valid_long, p_long, 0.0), axis=1, keepdims=True) / n_local
    dev = jnp.where(valid_long, p_long - mean_row, 0.0)
    square_row = jnp.sum(dev * dev, axis=1, keepdims=True)
    lane3 = iota((1, lanes), 1)
    means = jnp.where(lane3 < 32, mean_row[0:1], mean_row[1:2])
    r.st3[...] = jnp.where(lane3 < 64, means, jnp.where(lane3 < 96, square_row[0:1], square_row[1:2]))
    x_send(2, r.st3, r.t3)

    for name in names[8:]:
        fetch[name].wait()
    r.legal_both[...] = jnp.zeros_like(r.legal_both)
    r.legal_both[0:nb, 0 : s.moves] = r.legal_v[...]
    r.legal_both[nb : 2 * nb, 0 : s.moves] = r.legal_v[...]

    def slope2(i, carry):
        at = rows_of(i)
        slope = jnp.where(inside, gelu_both(r.dz[at, :])[1], 0.0)
        r.dz[at, :] = slope
        scaled = slope * ((r.h2[at, :] - mean2) * inv2)
        r.vu[at, 0:ch] = slope.astype(bf16)
        r.vu[at, ch:] = scaled.astype(bf16)
        r.out_v[i] = to_board(r.out_r[at, :].astype(f32))
        cot = from_board(r.cot_v[i])
        r.cot_s[at, :] = cot * slope
        a = (cot * scaled).reshape(br // 8, 8, ch)
        b = (cot * slope).reshape(br // 8, 8, ch)
        return carry[0] + jnp.sum(a, axis=0), carry[1] + jnp.sum(b, axis=0)

    zero = jnp.zeros((8, ch), f32)
    cot_g, cot_s = lax.fori_loop(0, s.side, slope2, (zero, zero))
    put_out = pltpu.make_async_copy(r.out_v, r.out, r.local_sem.at[len(names)])
    put_out.start()
    cot_g, cot_s = jnp.sum(cot_g, axis=0, keepdims=True), jnp.sum(cot_s, axis=0, keepdims=True)
    row = iota((16, s.long), 0)
    centred = jnp.where(valid_long[0:1], p_long[0:2] - mean_row[0:2], 0.0)
    against = jnp.where(
        row == 0, jnp.where(valid_long[0:1], 1.0, 0.0), jnp.where(row == 1, centred[0:1], jnp.where(row == 2, centred[1:2], 0.0))
    ).astype(bf16)
    early = dot(against, r.vu[...])
    for half in range(2):
        part = early[:, half * ch : (half + 1) * ch]
        ones = part[0:1]
        r.ste[4 * half : 4 * half + 1, :] = ones
        r.ste[4 * half + 1 : 4 * half + 2, :] = part[1:2] + mean_row[0:1] * ones
        r.ste[4 * half + 2 : 4 * half + 3, :] = part[2:3] + mean_row[1:2] * ones
        r.ste[4 * half + 3 : 4 * half + 4, :] = jnp.zeros((1, ch), f32)
    plane_send(3, r.ste, r.te)
    row = iota((8, s.long), 0)
    wanted = (lane & (nb - 1)) == (row & (nb - 1))
    rest = jnp.where(wanted, jnp.where(row < nb, p_long[0:1], p_long[1:2]), 0.0)
    parts = []
    for _ in range(3):
        part = rest.astype(bf16).astype(f32)
        parts.append(part)
        rest = rest - part
    parts = jnp.concatenate(parts + [jnp.zeros_like(rest)], axis=0).astype(bf16)
    p8 = dot(parts, r.expand[...])
    p8 = p8[0:8] + p8[8:16] + p8[16:24]
    row = iota((8, s.line), 0)
    lane = iota((8, s.line), 1)
    lane_i = divided(lane, wide, s.line)
    valid = (lane_i < s.side) & (lane - lane_i * wide < s.side)
    first_head = row < nb

    x_wait(2, r.t3)
    v = r.t3[...]
    mean_k = jnp.sum(v, axis=0) / float(s.n_dev)
    dev = v - mean_k
    squares = jnp.sum(jnp.where(lane3 < 64, n_local * dev * dev, v), axis=0)

    def of_head(v, at):
        return jnp.where(iota((8, 1), 0) < nb, v[:, at : at + 1], v[:, at + 32 : at + 33])

    mean_long = jnp.concatenate([mean_k[:, 0:1], mean_k[:, 32:33]], axis=0)
    mean_p = of_head(mean_k, 0)
    squares = of_head(squares, 0) + of_head(squares, 64)
    inv_p = lax.rsqrt(squares / s.count + epsilon)
    inv_long = jnp.concatenate([inv_p[0:1], inv_p[nb : nb + 1]], axis=0)
    gain_p = jnp.where(iota((8, 1), 0) < nb, r.hng_v[0], r.hng_v[1])
    shift_p = jnp.where(iota((8, 1), 0) < nb, r.hns_v[0], r.hns_v[1])
    xhat_p = (p8 - mean_p) * inv_p
    feature, back_p = gelu_both(xhat_p * gain_p + shift_p)
    flat = jnp.where(valid, feature, 0.0).astype(bf16)
    one_lane = first_head & (lane == s.side)
    flat_f = flat.astype(f32)
    lhs0 = jnp.where(one_lane, 1.0, jnp.where(first_head, flat_f, 0.0))
    lhs1 = jnp.where(first_head, 0.0, flat_f)
    pad8 = jnp.zeros((8, s.line), f32)

    def tall(v):
        return jnp.concatenate([v, pad8[:, : v.shape[1]]], axis=0).astype(bf16)

    half = (dot(tall(lhs0), r.dk[0]) + dot(tall(lhs1), r.dk[1]))[0:8]
    logits = half + pltpu.roll(half, nb, 0)
    move = iota((8, s.mp), 1)
    masked = jnp.where(r.legal_both[...] == 1, logits, negative_fill)
    top = jnp.max(masked, axis=1, keepdims=True)
    terms = jnp.exp(masked - top)
    total = jnp.sum(terms, axis=1, keepdims=True)
    row_b = iota((8, 1), 0) & (nb - 1)
    target = jnp.where(
        row_b < 2,
        jnp.where(row_b == 0, r.target_v[0], r.target_v[1]),
        jnp.where(row_b == 2, r.target_v[2], r.target_v[3]),
    )
    chosen = move == target
    picked = jnp.sum(jnp.where(chosen, logits, 0.0), axis=1, keepdims=True)
    ce = top + jnp.log(total) - picked
    dl = (terms / total - chosen.astype(f32)).astype(bf16).astype(f32)
    first_move = iota((8, s.mp), 0) < nb
    dq = dot_nt(tall(jnp.where(first_move, dl, 0.0)), r.dk[0]) + dot_nt(
        tall(jnp.where(first_move, 0.0, dl)), r.dk[1]
    )
    dnh = jnp.where(valid, dq[0:8] * back_p, 0.0)
    gain_row = jnp.sum(dnh * xhat_p, axis=1, keepdims=True)
    shift_row = jnp.sum(dnh, axis=1, keepdims=True)
    scale_p = gain_p * inv_p
    long_row, long_lane = iota((8, s.long), 0), iota((8, s.long), 1)
    dnh_long = dot_nt(tall(dnh), r.expand[...])[0:8]
    dnh_long = jnp.where((long_lane & (nb - 1)) == (long_row & (nb - 1)), dnh_long, 0.0)
    late = dot(jnp.concatenate([dnh_long, jnp.zeros_like(dnh_long)], axis=0).astype(bf16), r.vu[...])[0:8]
    head_rows = jnp.where(iota((8, ch), 0) < nb, hc0, hc1) * scale_p
    late_s = jnp.sum(late[:, 0:ch] * head_rows, axis=0, keepdims=True)
    late_g = jnp.sum(late[:, ch:] * head_rows, axis=0, keepdims=True)
    r.st5[0:1, :] = cot_g + late_g
    r.st5[1:2, :] = cot_s + late_s

    def heads(v):
        return v[0:1] + v[1:2] + v[2:3] + v[3:4], v[4:5] + v[5:6] + v[6:7] + v[7:8]

    gain_heads, shift_heads, ce_sum = heads(gain_row), heads(shift_row), heads(ce)[0]
    lane5 = iota((1, ch), 1)
    low = jnp.where(lane5 < 32, gain_heads[0], gain_heads[1])
    high = jnp.where(lane5 < 96, shift_heads[0], shift_heads[1])
    r.st5[2:3, :] = jnp.where(lane5 < 64, low, jnp.where(lane5 < 128, high, ce_sum))
    x_send(4, r.st5, r.t5)
    group_wait(3, r.te)
    r.stl[...] = jnp.sum(r.te[...], axis=0)
    line_send(7, r.stl, r.tl)
    r.fd_own[...] = jnp.zeros_like(r.fd_own)
    r.fd_own[0:8, :] = flat_f
    r.fd_own[8:16, 0 : s.mp] = dl
    r.fd[gx, q, c] = r.fd_own[...].astype(bf16)
    g_start(2 * n1 + 1)
    flip(r.wt2, r.wb2)
    scaled_long = dnh_long * scale_p
    dnh_heads = [jnp.sum(scaled_long[nb * k : nb * k + nb], axis=0, keepdims=True) for k in range(2)]
    xhat_long = (p_long[0:2] - mean_long) * inv_long
    xhat_long = jnp.where(valid_long[0:1], xhat_long, 0.0)
    row = iota((16, s.long), 0)
    terms_long = jnp.where(valid_long[0:1], 1.0, 0.0)
    for n, value in ((0, dnh_heads[0]), (1, dnh_heads[1]), (3, xhat_long[0:1]), (4, xhat_long[1:2])):
        terms_long = jnp.where(row == n, value, terms_long)
    terms_long = jnp.where(row < 5, terms_long, 0.0)
    r.terms[...] = terms_long.astype(bf16)
    tall_terms = jnp.concatenate([terms_long, jnp.zeros((lanes - 16, s.long), f32)], axis=0)
    r.terms_t[...] = jnp.transpose(tall_terms).astype(bf16)
    x_wait(4, r.t5)
    group_wait(7, r.tl)
    te = jnp.sum(r.tl[...], axis=0)
    t5 = jnp.sum(r.t5[...], axis=0)
    sums = t5[2:3]
    gain_sums, shift_sums = (sums[:, 0:1], sums[:, 32:33]), (sums[:, 64:65], sums[:, 96:97])
    r.tiny[0:1, :] = jnp.broadcast_to(sums[:, 128:129] / float(nb * s.n_dev), (1, lanes))
    first_lane = iota((1, lanes), 1) == 0
    r.tiny[1:2, :] = jnp.where(first_lane, *gain_sums)
    r.tiny[2:3, :] = jnp.where(first_lane, *shift_sums)
    g2s, s2s = t5[0:1], t5[1:2]
    for k in range(2):
        weight = (hc0, hc1)[k] * (scale_p[nb * k : nb * k + 1] / s.count)
        gain_part = gain_sums[k] * inv_p[nb * k : nb * k + 1]
        mean_k = mean_p[nb * k : nb * k + 1]
        s2s = s2s - weight * (shift_sums[k] * te[0:1] + gain_part * (te[k + 1 : k + 2] - mean_k * te[0:1]))
        g2s = g2s - weight * (shift_sums[k] * te[4:5] + gain_part * (te[k + 5 : k + 6] - mean_k * te[4:5]))
    scales = [scale_p[nb * k : nb * k + 1] / s.count for k in range(2)]
    ones_of = [shift_sums[k] * scales[k] for k in range(2)]
    xhat_of = [gain_sums[k] * scales[k] for k in range(2)]

    row = iota((lanes, ch), 0)
    mix = jnp.where(row == 0, hc0, jnp.where(row == 1, hc1, 0.0))
    mix = jnp.where(row == 2, -(hc0 * ones_of[0] + hc1 * ones_of[1]), mix)
    mix = jnp.where(row == 3, -hc0 * xhat_of[0], jnp.where(row == 4, -hc1 * xhat_of[1], mix))
    r.up[...] = dot(r.terms_t[...], mix.astype(bf16))

    def sums_back(field, xhat, carry):
        f = field.reshape(br // 8, 8, ch)
        g = (field * xhat).reshape(br // 8, 8, ch)
        return carry[0] + jnp.sum(g, axis=0), carry[1] + jnp.sum(f, axis=0)

    def to_field2(i, _):
        at = rows_of(i)
        xhat = (r.h2[at, :] - mean2) * inv2
        dz = r.cot_s[at, :] + r.up[at, :] * r.dz[at, :]
        r.dz[at, :] = dz
        d = (gain2 * inv2) * (dz - (s2s + xhat * g2s) * (1.0 / s.count))
        store3(r.d3, i, jnp.where(inside, d, 0.0))
        return 0

    lax.fori_loop(0, s.side, to_field2, 0)

    def wgrad(planes_t, di):
        start = pl.multiple_of(2 * br - br * di, 16)
        return dot(planes_t[...], r.d3[pl.ds(start, s.rows), :])

    def leave(planes_t, first, b):
        def one(di, _):
            rs_fill(di, wgrad(planes_t, di), b)
            if s.fast:
                rs_cross(b, di)
            return 0

        lax.fori_loop(first, 3, one, 0)
        rs_fill_rest(b)
        if not s.fast:
            rs_cross(b, 0)

    early = 1 if s.fast else 0
    for di in range(early):
        rs_fill(di, wgrad(r.at, di), rs2)
        rs_cross(rs2, di)
    g_forward(2 * n1 + 1)
    conv(r.d3, r.wb2, r.h2)

    def back1(i, carry):
        at = rows_of(i)
        dn = jnp.where(inside, r.h2[at, :] * r.back1[at, :], 0.0)
        r.h2[at, :] = dn
        return sums_back(dn, (r.h1[at, :] - mean1) * inv1, carry)

    g1, s1 = lax.fori_loop(0, s.side, back1, (zero, zero))
    r.st6[0:1, :] = jnp.sum(g1, axis=0, keepdims=True)
    r.st6[1:2, :] = jnp.sum(s1, axis=0, keepdims=True)
    x_send(5, r.st6, r.t6)
    for part in range(early):
        rs_plane(rs2, part)
    leave(r.at, early, rs2)
    for part in range(early, s.nch - 1):
        rs_plane(rs2, part)
    g_cross(2 * n1 + 1)
    rs_plane(rs2, s.nch - 1)
    against_out = dot(r.terms[...], r.out_r[...])
    for k in range(2):
        r.sth[k : k + 1, :] = (
            against_out[k : k + 1] - ones_of[k] * against_out[2:3] - xhat_of[k] * against_out[k + 3 : k + 4]
        )
    x_send(6, r.sth, r.th)
    x_wait(5, r.t6)
    t6 = jnp.sum(r.t6[...], axis=0)
    g1s, s1s = t6[0:1], t6[1:2]

    def to_field1(i, _):
        at = rows_of(i)
        xhat = (r.h1[at, :] - mean1) * inv1
        d = (gain1 * inv1) * (r.h2[at, :] - (s1s + xhat * g1s) * (1.0 / s.count))
        store3(r.d3, i, jnp.where(inside, d, 0.0))
        return 0

    lax.fori_loop(0, s.side, to_field1, 0)
    leave(r.xt, 0, rs1)
    for part in range(s.nch):
        rs_plane(rs1, part)
    conv(r.d3, r.wb1, r.h1)
    for part in range(s.nch):
        rs_line(rs2, part)

    def result(i, _):
        at = rows_of(i)
        r.in_grad_v[i] = to_board(r.dz[at, :] + r.h1[at, :])
        return 0

    lax.fori_loop(0, s.side, result, 0)
    put_in_grad = pltpu.make_async_copy(r.in_grad_v, r.in_grad, r.local_sem.at[len(names) + 1])
    put_in_grad.start()
    x_wait(6, r.th)
    shares = jnp.concatenate([g1s, g2s, s1s, s2s, jnp.sum(r.th[...], axis=0), jnp.zeros((2, ch), f32)], axis=0)
    r.tiny[8:16, :] = pltpu.roll(shares, lax.rem(ch - w * me, ch), 1)[:, 0:lanes]

    for part in range(s.nch):
        rs_line(rs1, part)

    g_done(2 * n1 + 1)
    fd = r.fd[...].astype(f32).reshape(s.n_dev, 16, s.line)
    features = fd[:, 0:8, :].reshape(8 * s.n_dev, s.line).astype(bf16)
    dls = fd[:, 8:16, 0 : s.mp].reshape(8 * s.n_dev, s.mp).astype(bf16)
    t = iota((s.rp, 1), 0)
    source = s.rsh * me + t
    mine = (t < s.rsh) & (source < s.head_in)
    col = iota((s.rp, s.line), 1)
    col8 = iota((s.rp, 8 * s.n_dev), 1) & 7
    own = jnp.where((t < s.rsh) & (source == s.head_in) & (col8 < nb), 1.0, 0.0)
    for k in range(2):
        in_k = mine & (source >= k * s.cells) & (source < (k + 1) * s.cells)
        cell = jnp.where(in_k, source - k * s.cells, 0)
        cell_i = divided(cell, s.side, s.cells)
        place = jnp.where(in_k, cell_i * wide + (cell - cell_i * s.side), -1)
        pick = (col == place).astype(f32).astype(bf16)
        rows_k = dot_nt(pick, features)
        own = own + jnp.where((col8 >= nb) if k else (col8 < nb), rows_k, 0.0)
    grad = dot(own.astype(bf16), dls)
    r.dense_grad[...] = grad

    for part in range(s.nch):
        rs_finish(rs2, part, r.c2_grad)
    for part in range(s.nch):
        rs_finish(rs1, part, r.c1_grad)

    for u in range(len(units)):
        g_drain(u)
    for number, slots in enumerate((r.t1, r.t2, r.t3, None, r.t5, r.t6, r.th)):
        if number != 3:
            x_drain(number, slots)
    group_wait(3, r.te, 0)
    group_wait(7, r.tl, 0)
    rs_drain(rs1)
    rs_drain(rs2)
    put_out.wait()
    put_in_grad.wait()


def place(w, x_ref, in_x_ref, c1, c2, dense, tiny, *refs):
    (out, loss, in_grad, c1_out, c2_out, gains, shifts, hc, hng, dense_out), refs = refs[:10], refs[10:]
    (out_v, in_v, c1_v, c2_v, dense_v, tiny_v), (came, went) = refs[:6], refs[6:]
    side = out.shape[0]
    cuts = [(n * side // 2, (n + 1) * side // 2) for n in range(2)]
    moves = [(x_ref, out_v, out), (in_x_ref, in_v, in_grad)]
    moves = [tuple(v.at[pl.ds(a, b - a)] for v in move) for move in moves for a, b in cuts]
    moves += [(c1, c1_v, c1_out), (c2, c2_v, c2_out)]
    fetch = [pltpu.make_async_copy(a, b, came.at[n]) for n, (a, b, _) in enumerate(moves)]
    put = [pltpu.make_async_copy(b, d, went.at[n]) for n, (_, b, d) in enumerate(moves)]
    fetch += [
        pltpu.make_async_copy(a, b, came.at[len(moves) + n])
        for n, (a, b) in enumerate(((tiny, tiny_v), (dense, dense_v)))
    ]
    for copy in fetch:
        copy.start()
    for n in range(len(moves)):
        fetch[n].wait()
        put[n].start()
    fetch[-2].wait()
    fetch[-1].wait()
    loss[...] = tiny_v[0:1, 0:1]
    hng[...] = tiny_v[1:3, 0:2]
    gains[...] = tiny_v[8:10, 0:w]
    shifts[...] = tiny_v[10:12, 0:w]
    hc[...] = tiny_v[12:14, 0:w]
    dense_out[...] = dense_v[0 : dense_out.shape[0], 0 : dense_out.shape[1]]
    for copy in put:
        copy.wait()


def body(x, w1, w2, gains, shifts, hc, hng, hns, dense, legal, target, cot):
    x, cot = (jnp.transpose(v, (1, 2, 0, 3)) for v in (x, cot))
    s = sizes_of(lax.axis_size("gx"), lax.axis_size("gy"), x, w1, dense, legal.shape[1])
    vmem, hbm = pltpu.VMEM, pl.ANY
    inputs = dict(
        x=x, w1=w1, w2=w2, gains=gains, shifts=shifts, hc=hc, hng=hng, hns=hns, dense=dense, legal=legal,
        target=target, cot=cot,
    )
    outputs = dict(
        out=(x.shape, bf16), in_grad=(x.shape, bf16), c1_grad=(w1.shape, f32), c2_grad=(w2.shape, f32),
        dense_grad=((s.rp, s.mp), f32), tiny=((16, lanes), f32),
    )
    gxn, qn, n, ch = s.gx_n, s.q_n, s.n_dev, s.ch
    field = pltpu.VMEM((s.long, ch), f32)
    boards = pltpu.VMEM((s.side, s.wide, s.nb, ch), bf16)
    planes = pltpu.VMEM((s.padded, 3 * ch), bf16)
    turned = pltpu.VMEM((ch, s.rows), bf16)
    weight = pltpu.VMEM((3, 3 * ch, ch), bf16)
    two = pltpu.VMEM((2, ch), f32)
    eight = pltpu.VMEM((8, ch), f32)
    dma = pltpu.SemaphoreType.DMA
    scratch = dict(
        local_sem=dma((14,)), g_sem=dma((2 * s.nch + 2, 5 + gxn)), x_sem=dma((8, 2)),
        rs_sem1=dma((s.nch, 6)), rs_sem2=dma((s.nch, 6)),
        x_v=boards, cot_v=boards, out_v=pltpu.VMEM(x.shape, bf16), in_grad_v=pltpu.VMEM(x.shape, bf16),
        stage=pltpu.VMEM((s.blk1, lanes), f32), small=pltpu.VMEM((8, lanes), f32),
        s1=pltpu.VMEM((gxn, qn, 2, s.blk1, lanes), bf16), s2=pltpu.VMEM((gxn, qn, 2, s.blk, lanes), bf16),
        sd=pltpu.VMEM((gxn, qn, 2, s.rp, s.mp), bf16), dense_f=pltpu.VMEM((s.rp, s.mp), f32),
        x3=planes, a3=planes, d3=planes, out_r=pltpu.VMEM((s.long, ch), bf16), terms=pltpu.VMEM((16, s.long), bf16), terms_t=pltpu.VMEM((s.long, lanes), bf16),
        xt=turned, at=turned, wt1=weight, wt2=weight, wb1=weight, wb2=weight,
        pars=pltpu.VMEM((8, ch), f32), h1=field, h2=field, dz=field, back1=field, up=field, cot_s=field,
        st1=two, t1=pltpu.VMEM((n, 2, ch), f32), st2=two, t2=pltpu.VMEM((n, 2, ch), f32),
        st3=pltpu.VMEM((1, lanes), f32), t3=pltpu.VMEM((n, 1, lanes), f32), ste=eight, te=pltpu.VMEM((s.gy_n, 8, ch), f32), stl=eight, tl=pltpu.VMEM((gxn, 8, ch), f32),
        st5=pltpu.VMEM((3, ch), f32), t5=pltpu.VMEM((n, 3, ch), f32), st6=two, t6=pltpu.VMEM((n, 2, ch), f32),
        sth=two, th=pltpu.VMEM((n, 2, ch), f32), vu=pltpu.VMEM((s.long, 2 * ch), bf16),
        fd_own=pltpu.VMEM((16, s.line), f32), fd=pltpu.VMEM((gxn, qn, 2, 16, s.line), bf16),
        dk=pltpu.VMEM((2, s.line, s.mp), bf16), expand=pltpu.VMEM((s.long, s.line), bf16),
        legal_both=pltpu.VMEM((8, s.mp), jnp.int32),
    )
    for name in ("w1", "w2", "gains", "shifts", "hc", "dense", "legal"):
        scratch[name + "_v"] = pltpu.VMEM(inputs[name].shape, inputs[name].dtype)
    for name in ("hng", "hns", "target"):
        scratch[name + "_v"] = pltpu.SMEM(inputs[name].shape, inputs[name].dtype)
    if not s.fast:
        scratch["flat"] = pltpu.VMEM((9, ch, ch), f32)
        scratch["eight"] = pltpu.VMEM((9, 8, ch), f32)
    for number in ("1", "2"):
        scratch["rsb" + number] = pltpu.VMEM((s.nch, 2, gxn, qn, s.crows, lanes), bf16)
        scratch["rc" + number] = pltpu.VMEM((s.nch, gxn, qn, s.crows, lanes), bf16)
        scratch["pb" + number] = pltpu.VMEM((s.nch, qn, gxn, s.crows, lanes), bf16)
        scratch["rp" + number] = pltpu.VMEM((s.nch, qn - 1, gxn, s.crows, lanes), bf16)
        scratch["zb" + number] = pltpu.VMEM((s.nch, gxn, s.crows, lanes), bf16)
        scratch["rd" + number] = pltpu.VMEM((gxn * qn - 1, s.crows, lanes), bf16)
        scratch["rz" + number] = pltpu.VMEM((s.nch, gxn - 1, s.crows, lanes), bf16)
    run = pl.pallas_call(
        functools.partial(kernel, s, tuple(inputs), tuple(outputs), tuple(scratch)),
        out_shape=[jax.ShapeDtypeStruct(shape, kind) for shape, kind in outputs.values()],
        in_specs=[pl.BlockSpec(memory_space=hbm) for _ in inputs],
        out_specs=[pl.BlockSpec(memory_space=hbm if n in ("out", "in_grad") else vmem) for n in outputs],
        scratch_shapes=list(scratch.values()),
        compiler_params=pltpu.CompilerParams(
            collective_id=0, has_side_effects=True, vmem_limit_bytes=60 * 1024 * 1024
        ),
        cost_estimate=pl.CostEstimate(flops=10_500_000_000, bytes_accessed=8_000_000, transcendentals=800_000),
        name="tower",
    )
    results = run(*inputs.values())
    kinds = [jax.ShapeDtypeStruct(v.shape, v.dtype) for v in results]
    out, in_grad, c1_grad, c2_grad, dense_grad, _ = kinds
    small = [jax.ShapeDtypeStruct(v.shape, f32) for v in (gains, shifts, hc)]
    loss, pair = (jax.ShapeDtypeStruct(shape, f32) for shape in ((1, 1), (2, 2)))
    shapes = [out, loss, in_grad, c1_grad, c2_grad, *small, pair, jax.ShapeDtypeStruct(dense.shape, f32)]
    results = pl.pallas_call(
        functools.partial(place, s.w),
        out_shape=shapes,
        in_specs=[pl.BlockSpec(memory_space=hbm) for _ in kinds],
        out_specs=[pl.BlockSpec(memory_space=hbm if n in (0, 2, 3, 4) else vmem) for n in range(len(shapes))],
        scratch_shapes=[pltpu.VMEM(v.shape, v.dtype) for v in kinds] + [dma((16,))] * 2,
        name="place",
    )(*results)
    out, loss, in_grad, *rest = results
    out, in_grad = (jnp.transpose(v, (2, 0, 1, 3)) for v in (out, in_grad))
    return (out, loss.reshape(()), in_grad, *rest)


def solution(mesh):
    both = ("gx", "gy")
    board = P(both, None, None, None)
    kernels = P(None, both, None)
    pairs = P(None, both)
    return jax.shard_map(
        body,
        mesh=mesh,
        in_specs=(
            board, kernels, kernels, pairs, pairs, pairs, P(), P(), P(both, None), P(both, None), P(both), board,
        ),
        out_specs=(board, P(), board, kernels, kernels, pairs, pairs, pairs, P(), P(both, None)),
        check_vma=False,
    )
```
